32 devices in a mesh: blk: 16 (over z, x, core), dp: 2 (over y).
Axes of the slice: x: 2, y: 2, z: 4, core: 2. Of those that a mesh axis runs over, the one named last changes fastest.
Arguments:
- tokens: bfloat16 [6144, 2048], P(('blk', 'dp')), may hold values from -6 to 6
- cotangent: bfloat16 [6144, 2048], P(('blk', 'dp')), may hold values from -0.59765625 to 0.59765625
- gate_probs: bfloat16 [6144, 3], P(('blk', 'dp')), may hold values from 0.099609375 to 1
- slot_rows: int32 [48, 128], P('blk'), may hold values from 0 to 384, as said below
- w_gate: bfloat16 [16, 2048, 768], P('blk', None, 'dp'), may hold values from -0.125 to 0.125
- w_up: bfloat16 [16, 2048, 768], P('blk', None, 'dp'), may hold values from -0.125 to 0.125
- w_down: bfloat16 [16, 768, 2048], P('blk', 'dp'), may hold values from -0.21875 to 0.21875
Outputs:
- mixed: bfloat16 [6144, 2048], P(('blk', 'dp'))
- input_grad: bfloat16 [6144, 2048], P(('blk', 'dp'))
- gate_grad: float32 [6144, 3], P(('blk', 'dp'))
- w_gate_grad: bfloat16 [16, 2048, 768], P('blk', None, 'dp')
- w_up_grad: bfloat16 [16, 2048, 768], P('blk', None, 'dp')
- w_down_grad: bfloat16 [16, 768, 2048], P('blk', 'dp')
The draws below stay inside these ranges and needn't reach their ends.
Inputs may be any that keep to these rules, and one draw needn't show every extreme that they name: `slot_rows`: entries below 384 in a row are distinct and stand before the entries equal to 384; every row names at least 16 tokens, and some row names 128.
All inputs are finite; a program needn't handle non-finite values.
Results may differ from the reference program's by a relative error of at most 0.0075.
Values may be sent and summed in bfloat16 or wider, within the bound.
No kernel may reach another device: no remote copies, remote signals or barrier semaphores. Data moves between devices by JAX's collectives and lax.ppermute only.
A program may use at most 128 MiB of HBM per device.

```python
import jax
import jax.numpy as jnp
from jax import lax

D = 2048
H = 768
CYCLE = 3
CAP = 128
GROUP = 384
EXPERTS = 16
TOKENS = 6144
LISTS = 48
N_BLK = 16


def draw_slot_rows(key, part):
    side_key, full_key, perm_key = jax.random.split(key, 3)
    side_length = jax.random.randint(side_key, (LISTS,), 4, 12)
    counts = side_length * side_length * CAP // 128
    full_index = jax.random.randint(full_key, (), 0, LISTS)
    counts = jnp.where(jnp.arange(LISTS) == full_index, CAP, counts)
    list_keys = jax.random.split(perm_key, LISTS)
    shuffled = jax.vmap(lambda list_key: jax.random.permutation(list_key, GROUP)[:CAP])(list_keys)
    slot_index = jnp.arange(CAP)[None, :]
    return jnp.where(slot_index < counts[:, None], shuffled, GROUP).astype(jnp.int32)


def level_of(key, shape, cuts, least, largest):
    factor_of, own = 1.0, jax.random.fold_in(key, 6)
    for dim, blocks in cuts:
        draws = jnp.exp(jax.random.uniform(jax.random.fold_in(own, dim), (blocks,), jnp.float32, least / len(cuts), largest / len(cuts)))
        factor_of = factor_of * jnp.repeat(draws, shape[dim] // blocks).reshape([-1 if axis == dim else 1 for axis in range(len(shape))])
    return factor_of


def gaussian(stream_key, shape, width, most, pieces=(), kind=jnp.bfloat16):
    gain = level_of(stream_key, shape, pieces, -0.22, 0.18) if pieces else 1.0
    drawn = jax.random.normal(stream_key, shape, jnp.float32) * width * gain
    return jnp.minimum(jnp.maximum(drawn, -most), most).astype(kind)


def setup_inputs(seed: int = 0) -> dict:
    key_of = jax.random.split(jax.random.key(seed), 8)
    tokens = gaussian(key_of[0], (TOKENS, D), 1.0, 6.0, ((0, 32),))
    cotangent = gaussian(key_of[1], (TOKENS, D), 0.1, 0.59765625, ((0, 32),))
    gate_probs = jnp.clip(0.099609375 + 0.9003906 * jax.random.uniform(key_of[2], (TOKENS, CYCLE), jnp.float32) ** level_of(key_of[2], (TOKENS, CYCLE), ((0, 32),), -0.2, 0.2), 0.099609375, 1.0).astype(jnp.bfloat16)
    slot_rows = draw_slot_rows(jax.random.fold_in(key_of[7], 71), 0)
    w_gate = gaussian(key_of[4], (EXPERTS, D, H), D ** -0.5, 0.125, ((0, 16), (2, 2)))
    w_up = gaussian(key_of[5], (EXPERTS, D, H), D ** -0.5, 0.125, ((0, 16), (2, 2)))
    w_down = gaussian(key_of[6], (EXPERTS, H, D), H ** -0.5, 0.21875, ((0, 16), (1, 2)))
    return {"tokens": tokens, "cotangent": cotangent, "gate_probs": gate_probs, "slot_rows": slot_rows, "w_gate": w_gate, "w_up": w_up, "w_down": w_down}


def expert_step(slab, rows_x, rows_dy, rows_gate):
    w_gate_s, w_up_s, w_down_s = slab
    gate_rows = rows_gate.astype(jnp.float32)
    pre_gate = jnp.dot(rows_x, w_gate_s, preferred_element_type=jnp.float32)
    pre_up = jnp.dot(rows_x, w_up_s, preferred_element_type=jnp.float32)
    sigmoid_gate = jax.nn.sigmoid(pre_gate)
    active = pre_gate * sigmoid_gate
    hidden = (active * pre_up).astype(jnp.bfloat16)
    expert_out = jnp.dot(hidden, w_down_s, preferred_element_type=jnp.float32)
    weighted = gate_rows[:, None] * expert_out
    cotan_rows = rows_dy.astype(jnp.float32)
    gate_grad = jnp.sum(cotan_rows * expert_out, axis=1)
    out_grad = (gate_rows[:, None] * cotan_rows).astype(jnp.bfloat16)
    hidden_grad = jnp.einsum("cd,hd->ch", out_grad, w_down_s, preferred_element_type=jnp.float32)
    pre_gate_grad = (hidden_grad * pre_up * sigmoid_gate * (1.0 + pre_gate * (1.0 - sigmoid_gate))).astype(jnp.bfloat16)
    pre_up_grad = (hidden_grad * active).astype(jnp.bfloat16)
    input_grad = jnp.einsum("ch,dh->cd", pre_gate_grad, w_gate_s, preferred_element_type=jnp.float32)
    input_grad = input_grad + jnp.einsum("ch,dh->cd", pre_up_grad, w_up_s, preferred_element_type=jnp.float32)
    part_gate = jnp.einsum("cd,ch->dh", rows_x, pre_gate_grad, preferred_element_type=jnp.float32).astype(jnp.bfloat16)
    part_up = jnp.einsum("cd,ch->dh", rows_x, pre_up_grad, preferred_element_type=jnp.float32).astype(jnp.bfloat16)
    part_down = jnp.einsum("ch,cd->hd", hidden, out_grad, preferred_element_type=jnp.float32).astype(jnp.bfloat16)
    return (weighted, input_grad, gate_grad), (part_gate, part_up, part_down)


def reference(tokens, cotangent, gate_probs, slot_rows, w_gate, w_up, w_down):
    padded_x = jnp.concatenate([tokens.reshape(N_BLK, GROUP, D), jnp.zeros((N_BLK, 1, D), tokens.dtype)], axis=1)
    padded_dy = jnp.concatenate([cotangent.reshape(N_BLK, GROUP, D), jnp.zeros((N_BLK, 1, D), cotangent.dtype)], axis=1)
    padded_gate = jnp.concatenate([gate_probs.reshape(N_BLK, GROUP, CYCLE), jnp.zeros((N_BLK, 1, CYCLE), gate_probs.dtype)], axis=1)
    all_lists = slot_rows.reshape(N_BLK, CYCLE, CAP)

    def expert_block(expert_index):
        slab = (w_gate[expert_index], w_up[expert_index], w_down[expert_index])
        weighted_list = []
        input_list = []
        gate_list = []
        totals = None
        for cycle_step in range(CYCLE):
            group_index = ((expert_index + cycle_step) % N_BLK).astype(jnp.int32)
            list_rows = all_lists[group_index, cycle_step]
            rows_x = padded_x[group_index][list_rows]
            rows_dy = padded_dy[group_index][list_rows]
            rows_gate = padded_gate[group_index][list_rows, cycle_step]
            results, partials = expert_step(slab, rows_x, rows_dy, rows_gate)
            weighted_list.append(results[0])
            input_list.append(results[1])
            gate_list.append(results[2])
            widened = tuple(piece.astype(jnp.float32) for piece in partials)
            if totals is None:
                totals = widened
            else:
                totals = tuple(first + second for first, second in zip(totals, widened))
        grads = tuple(piece.astype(jnp.bfloat16) for piece in totals)
        return jnp.stack(weighted_list), jnp.stack(input_list), jnp.stack(gate_list), grads

    weighted_all, input_all, gate_all, grads = lax.map(expert_block, jnp.arange(N_BLK, dtype=jnp.int32))

    mixed_acc = jnp.zeros((N_BLK, GROUP + 1, D), jnp.float32)
    input_acc = jnp.zeros((N_BLK, GROUP + 1, D), jnp.float32)
    gate_acc = jnp.zeros((N_BLK, GROUP + 1, CYCLE), jnp.float32)
    for cycle_step in range(CYCLE):
        step_rows = all_lists[:, cycle_step]
        step_weighted = jnp.roll(weighted_all[:, cycle_step], cycle_step, axis=0)
        step_input = jnp.roll(input_all[:, cycle_step], cycle_step, axis=0)
        step_gate = jnp.roll(gate_all[:, cycle_step], cycle_step, axis=0)
        mixed_acc = jax.vmap(lambda accum, where, values: accum.at[where].add(values))(mixed_acc, step_rows, step_weighted)
        input_acc = jax.vmap(lambda accum, where, values: accum.at[where].add(values))(input_acc, step_rows, step_input)
        gate_acc = jax.vmap(lambda accum, where, values: accum.at[where, cycle_step].add(values))(gate_acc, step_rows, step_gate)
    mixed = mixed_acc[:, :GROUP].reshape(TOKENS, D).astype(jnp.bfloat16)
    input_grad = input_acc[:, :GROUP].reshape(TOKENS, D).astype(jnp.bfloat16)
    gate_grad = gate_acc[:, :GROUP].reshape(TOKENS, CYCLE)
    return mixed, input_grad, gate_grad, grads[0], grads[1], grads[2]
```

```python
import functools

import jax
import jax.numpy as jnp
from jax import lax
from jax.experimental import pallas as pl
from jax.experimental.pallas import tpu as pltpu
from jax.sharding import PartitionSpec as P

CHUNKS = 2
LANES = 128
F32 = jnp.float32
BF16 = jnp.bfloat16
NT = (((1,), (1,)), ((), ()))
TN = (((0,), (0,)), ((), ()))


def shifted(value, axis, steps):
    count = lax.axis_size(axis)
    pairs = [(source, (source + steps) % count) for source in range(count)]
    return lax.ppermute(value, axis, pairs)


def after(value, earlier):
    return lax.optimization_barrier((value, earlier))[0]


def whole(array):
    return pl.BlockSpec(array.shape, lambda i: (0,) * len(array.shape))


def part(rows, columns, row, column):
    return pl.BlockSpec((rows, columns), lambda i: (row, column))


def run(kernel, outs, operands, flops, name):
    arrays, specs = [], []
    for operand in operands:
        array, spec = operand if isinstance(operand, tuple) else (operand, whole(operand))
        arrays.append(array)
        specs.append(spec)
    moved = sum(2 * spec.block_shape[0] * spec.block_shape[1] for spec in specs)
    moved += sum(out.size * out.dtype.itemsize for out in outs)
    return pl.pallas_call(
        kernel,
        grid=(1,),
        out_shape=outs,
        in_specs=specs,
        out_specs=[whole(out) for out in outs],
        compiler_params=pltpu.CompilerParams(vmem_limit_bytes=40 * 2**20),
        cost_estimate=pl.CostEstimate(flops=flops, bytes_accessed=moved, transcendentals=0),
        name=name,
    )(*arrays)


def shape(*dims, dtype=BF16):
    return jax.ShapeDtypeStruct(dims, dtype)


def dot(a, b, dims=(((1,), (0,)), ((), ()))):
    return lax.dot_general(a, b, dims, preferred_element_type=F32)


def picks(rows, count):
    columns = lax.broadcasted_iota(jnp.int32, (rows.shape[0], count), 1)
    return jnp.where(rows == columns, 1.0, 0.0).astype(BF16)


def stacked(refs):
    return jnp.concatenate([ref[...] for ref in refs], axis=0)


def gather_rows(lists, own_rows, oth_rows, own, oth, *outs):
    count, cap = own.shape[0], outs[0].shape[0]
    width = own.shape[1]
    rows = dot(picks(own_rows[...], count), own[...])
    rows += dot(picks(oth_rows[...], count), oth[:, :width])
    for s in range(lists):
        outs[s][...] = rows[s * cap : (s + 1) * cap].astype(BF16)


def gather_scaled(lists, own_rows, oth_rows, own, oth, own_gate, oth_gate, *outs):
    count, cap = own.shape[0], outs[0].shape[0]
    width = own.shape[1]
    own_picks, oth_picks = picks(own_rows[...], count), picks(oth_rows[...], count)
    rows = dot(own_picks, own[...]) + dot(oth_picks, oth[:, :width])
    gate = dot(own_picks, own_gate[...]) + dot(oth_picks, oth_gate[...])
    for s in range(lists):
        span = slice(s * cap, (s + 1) * cap)
        outs[s][...] = (gate[span, s : s + 1] * rows[span]).astype(BF16)


def first_products(lists, *refs):
    x, (w_gate, w_up, gate_out, up_out) = refs[:lists], refs[lists:]
    rows = stacked(x)
    gate_out[...] = dot(rows, w_gate[...])
    up_out[...] = dot(rows, w_up[...])


def activation(lists, *refs):
    x, (w_gate, w_up, gate_in, up_in, hidden, active_out, slope_out) = refs[:lists], refs[lists:]
    rows = stacked(x)
    pre_gate = gate_in[...] + dot(rows, w_gate[...])
    pre_up = up_in[...] + dot(rows, w_up[...])
    sigmoid_gate = jax.nn.sigmoid(pre_gate)
    active = pre_gate * sigmoid_gate
    hidden[...] = (active * pre_up).astype(BF16)
    active_out[...] = active
    slope_out[...] = pre_up * sigmoid_gate * (1.0 + pre_gate * (1.0 - sigmoid_gate))


def expert_rows(lists, hidden, w_down, *outs):
    cap = outs[0].shape[0]
    rows = dot(hidden[...], w_down[...])
    for s in range(lists):
        outs[s][...] = rows[s * cap : (s + 1) * cap].astype(BF16)


def first_hidden_grad(lists, *refs):
    out_grad, (w_down, total) = refs[:lists], refs[lists:]
    total[...] = dot(stacked(out_grad), w_down[...], NT)


def hidden_grads(lists, *refs):
    out_grad = refs[:lists]
    w_down, first, hidden, active, slope, gate_grad, up_grad, gate_sum = refs[lists:]
    grad = first[...] + dot(stacked(out_grad), w_down[...], NT)
    gate_grad[...] = (grad * slope[...]).astype(BF16)
    up_grad[...] = (grad * active[...]).astype(BF16)
    sums = jnp.sum(grad * hidden[...].astype(F32), axis=1, keepdims=True)
    gate_sum[...] = jnp.broadcast_to(sums, gate_sum.shape)


def input_rows(lists, gate_grad, up_grad, w_gate, w_up, gate_sum, *outs):
    cap, width = outs[0].shape[0], w_gate.shape[0]
    rows = dot(gate_grad[...], w_gate[...], NT) + dot(up_grad[...], w_up[...], NT)
    for s in range(lists):
        span = slice(s * cap, (s + 1) * cap)
        outs[s][:, :width] = rows[span].astype(BF16)
        if outs[s].shape[1] > width:
            sums = gate_sum[span, :]
            high = sums.astype(BF16)
            low = (sums - high.astype(F32)).astype(BF16)
            lane = lax.broadcasted_iota(jnp.int32, sums.shape, 1)
            packed = jnp.where(lane == s, high.astype(F32), 0.0)
            packed += jnp.where(lane == lists + s, low.astype(F32), 0.0)
            outs[s][:, width:] = packed.astype(BF16)


def weight_grads(lists, *refs):
    x, out_grad = refs[:lists], refs[lists : 2 * lists]
    hidden, gate_grad, up_grad, w_gate_grad, w_up_grad, w_down_grad = refs[2 * lists :]
    rows = stacked(x)
    w_gate_grad[...] = dot(rows, gate_grad[...], TN).astype(BF16)
    w_up_grad[...] = dot(rows, up_grad[...], TN).astype(BF16)
    w_down_grad[...] = dot(hidden[...], stacked(out_grad), TN).astype(BF16)


def scatter_rows(lists, rows, *refs):
    values, out = refs[:lists], refs[lists]
    count = out.shape[0]
    total = None
    for s in range(lists):
        token = lax.broadcasted_iota(jnp.int32, (count, rows.shape[1]), 0)
        mask = jnp.where(rows[s : s + 1, :] == token, 1.0, 0.0).astype(BF16)
        term = dot(mask, values[s][...])
        total = term if total is None else total + term
    out[...] = total.astype(out.dtype)


def scatter_scaled(lists, rows, gate, *refs):
    values, out = refs[:lists], refs[lists]
    count = out.shape[0]
    total = None
    for s in range(lists):
        token = lax.broadcasted_iota(jnp.int32, (count, rows.shape[1]), 0)
        factor = gate[:, s : s + 1].astype(F32)
        mask = jnp.where(rows[s : s + 1, :] == token, factor, 0.0).astype(BF16)
        term = dot(mask, values[s][...])
        total = term if total is None else total + term
    out[...] = total.astype(out.dtype)


def on_device(tokens, cotangent, gate_probs, slot_rows, w_gate, w_up, w_down):
    count, model = tokens.shape
    lists, cap = slot_rows.shape
    hidden_units = w_gate.shape[2]
    width = model // CHUNKS
    total = lists * cap
    w_gate, w_up, w_down = w_gate[0], w_up[0], w_down[0]
    me = lax.axis_index("dp").astype(jnp.int32)
    own_rows = slot_rows - me * count
    oth_rows = slot_rows - (1 - me) * count
    own_column, oth_column = own_rows.reshape(total, 1), oth_rows.reshape(total, 1)
    own_gate = jnp.pad(gate_probs, ((0, 0), (0, LANES - lists)))
    kernel = lambda body: functools.partial(body, lists)
    columns = lambda array, c: (array, part(array.shape[0], width, 0, c))
    span = lambda c: slice(c * width, (c + 1) * width)

    oth_x = [shifted(tokens[:, span(c)], "dp", 1) for c in range(CHUNKS)]
    oth_dy = []
    for c in range(CHUNKS):
        piece = cotangent[:, span(c)]
        if c == 0:
            piece = jnp.concatenate([piece, own_gate], axis=1)
        oth_dy.append(shifted(after(piece, oth_x[c]), "dp", 1))
    oth_gate = (oth_dy[0], part(count, LANES, 0, width // LANES))

    x, out_grad = [], []
    for c in range(CHUNKS):
        rows = run(
            kernel(gather_rows),
            [shape(cap, width)] * lists,
            [own_column, oth_column, columns(tokens, c), oth_x[c]],
            4 * total * count * width,
            "gather_x",
        )
        x.append([rows[0]] + [shifted(rows[s], "blk", -s) for s in range(1, lists)])
    for c in range(CHUNKS):
        rows = run(
            kernel(gather_scaled),
            [shape(cap, width)] * lists,
            [own_column, oth_column, columns(cotangent, c), oth_dy[c], own_gate, oth_gate],
            4 * total * count * width,
            "gather_dy",
        )
        out_grad.append([rows[0]] + [shifted(rows[s], "blk", -s) for s in range(1, lists)])

    flops = 2 * total * width * hidden_units
    square = [shape(total, hidden_units, dtype=F32)] * 2
    w_rows = lambda array, c: (array, part(width, hidden_units, c, 0))
    pre = run(kernel(first_products), square, x[0] + [w_rows(w_gate, 0), w_rows(w_up, 0)], 2 * flops, "pre")
    for c in range(1, CHUNKS):
        operands = x[c] + [w_rows(w_gate, c), w_rows(w_up, c)] + list(pre)
        hidden, active, slope = run(
            kernel(activation), [shape(total, hidden_units)] + square, operands, 2 * flops, "hidden"
        )
    expert_out = []
    for c in range(CHUNKS):
        rows = run(
            kernel(expert_rows), [shape(cap, width)] * lists, [hidden, columns(w_down, c)], flops, "expert_out"
        )
        expert_out.append([rows[0]] + [shifted(rows[s], "blk", s) for s in range(1, lists)])

    first = run(kernel(first_hidden_grad), square[:1], out_grad[0] + [columns(w_down, 0)], flops, "hidden_grad")
    gate_grad, up_grad, gate_sum = run(
        kernel(hidden_grads),
        [shape(total, hidden_units)] * 2 + [shape(total, LANES, dtype=F32)],
        out_grad[1] + [columns(w_down, 1), first[0], hidden, active, slope],
        flops,
        "hidden_grads",
    )
    input_grad = []
    for c in range(CHUNKS):
        extra = LANES if c == CHUNKS - 1 else 0
        rows = run(
            kernel(input_rows),
            [shape(cap, width + extra)] * lists,
            [gate_grad, up_grad, w_rows(w_gate, c), w_rows(w_up, c), gate_sum],
            2 * flops,
            "input_grad",
        )
        input_grad.append([rows[0]] + [shifted(rows[s], "blk", s) for s in range(1, lists)])
    gate_parts, up_parts, down_parts = [], [], []
    for c in range(CHUNKS):
        parts = run(
            kernel(weight_grads),
            [shape(width, hidden_units)] * 2 + [shape(hidden_units, width)],
            x[c] + out_grad[c] + [hidden, gate_grad, up_grad],
            3 * flops,
            "weight_grads",
        )
        for held, piece in zip((gate_parts, up_parts, down_parts), parts):
            held.append(piece)

    def summed(operands, sent_rows, kept_rows, body, values, gates):
        extent = values[0].shape[1]
        flops = 2 * total * count * extent
        sent = run(body, [shape(count, extent)], [sent_rows] + gates[:1] + values, flops, "sent")[0]
        arrived = shifted(sent, "dp", 1)
        kept = run(body, [shape(count, extent, dtype=F32)], [kept_rows] + gates[1:] + values, flops, "kept")[0]
        return kept + arrived.astype(F32)

    mixed = [
        summed(None, oth_rows, own_rows, kernel(scatter_scaled), expert_out[c], [oth_gate, own_gate]).astype(BF16)
        for c in range(CHUNKS)
    ]
    grads = [
        summed(None, oth_rows, own_rows, kernel(scatter_rows), input_grad[c], []) for c in range(CHUNKS)
    ]
    sums = grads[-1][:, width : width + 2 * lists]
    gate_out = (sums[:, :lists] + sums[:, lists:]) / gate_probs.astype(F32)
    return (
        jnp.concatenate(mixed, axis=1),
        jnp.concatenate([grad[:, :width].astype(BF16) for grad in grads], axis=1),
        gate_out,
        jnp.concatenate(gate_parts, axis=0)[None],
        jnp.concatenate(up_parts, axis=0)[None],
        jnp.concatenate(down_parts, axis=1)[None],
    )


def solution(mesh):
    rows, lists = P(("blk", "dp"), None), P("blk", None)
    inner, outer = P("blk", None, "dp"), P("blk", "dp", None)
    return jax.shard_map(
        on_device,
        mesh=mesh,
        in_specs=(rows, rows, rows, lists, inner, inner, outer),
        out_specs=(rows, rows, rows, inner, inner, outer),
        check_vma=False,
    )
```

```python
import functools

import jax
import jax.numpy as jnp
from jax import lax
from jax.experimental import pallas as pl
from jax.experimental.pallas import tpu as pltpu
from jax.sharding import PartitionSpec as P

CHUNKS = 2
LANES = 128
F32 = jnp.float32
BF16 = jnp.bfloat16
NT = (((1,), (1,)), ((), ()))
TN = (((0,), (0,)), ((), ()))


def shifted(value, axis, steps):
    count = lax.axis_size(axis)
    pairs = [(source, (source + steps) % count) for source in range(count)]
    return lax.ppermute(value, axis, pairs)


def after(value, earlier):
    return lax.optimization_barrier((value, earlier))[0]


def whole(array):
    return pl.BlockSpec(array.shape, lambda i: (0,) * len(array.shape))


def part(rows, columns, row, column):
    return pl.BlockSpec((rows, columns), lambda i: (row, column))


class Steps:
    def __init__(self):
        self.last = None

    def run(self, kernel, outs, operands, flops, name, held=()):
        pair = lambda item: item if isinstance(item, tuple) else (item, whole(item))
        pairs = [pair(operand) for operand in operands]
        arrays, specs = [array for array, _ in pairs], [spec for _, spec in pairs]
        if self.last is not None:
            arrays[0] = after(arrays[0], self.last)
        out_shapes, out_specs = zip(*[pair(out) for out in outs])
        moved = sum(2 * spec.block_shape[0] * spec.block_shape[1] for spec in specs + list(out_specs))
        results = pl.pallas_call(
            (lambda *refs: kernel(*refs[len(held) :])) if held else kernel,
            grid=(1,),
            out_shape=out_shapes,
            in_specs=[pl.BlockSpec(memory_space=pl.ANY)] * len(held) + specs,
            out_specs=out_specs,
            input_output_aliases={i: i for i in range(len(held))},
            compiler_params=pltpu.CompilerParams(vmem_limit_bytes=20 * 2**20),
            cost_estimate=pl.CostEstimate(flops=flops, bytes_accessed=moved, transcendentals=0),
            name=name,
        )(*held, *arrays)
        self.last = results[0]
        return results


def shape(*dims, dtype=BF16):
    return jax.ShapeDtypeStruct(dims, dtype)


def dot(a, b, dims=(((1,), (0,)), ((), ()))):
    return lax.dot_general(a, b, dims, preferred_element_type=F32)


def picks(rows, count):
    columns = lax.broadcasted_iota(jnp.int32, (rows.shape[0], count), 1)
    return jnp.where(rows == columns, 1.0, 0.0).astype(BF16)


def stacked(refs):
    return jnp.concatenate([ref[...] for ref in refs], axis=0)


def gather_rows(lists, own_rows, oth_rows, own, oth, *outs):
    count, cap = own.shape[0], outs[0].shape[0]
    width = own.shape[1]
    rows = dot(picks(own_rows[...], count), own[...])
    rows += dot(picks(oth_rows[...], count), oth[:, :width])
    for s in range(lists):
        outs[s][...] = rows[s * cap : (s + 1) * cap].astype(BF16)


def gather_scaled(lists, own_rows, oth_rows, own, oth, own_gate, oth_gate, *outs):
    count, cap = own.shape[0], outs[0].shape[0]
    width = own.shape[1]
    own_picks, oth_picks = picks(own_rows[...], count), picks(oth_rows[...], count)
    rows = dot(own_picks, own[...]) + dot(oth_picks, oth[:, :width])
    gate = dot(own_picks, own_gate[...]) + dot(oth_picks, oth_gate[...])
    for s in range(lists):
        span = slice(s * cap, (s + 1) * cap)
        outs[s][...] = (gate[span, s : s + 1] * rows[span]).astype(BF16)


def first_products(lists, *refs):
    x, (w_gate, w_up, gate_out, up_out) = refs[:lists], refs[lists:]
    rows = stacked(x)
    gate_out[...] = dot(rows, w_gate[...])
    up_out[...] = dot(rows, w_up[...])


def activation(lists, *refs):
    x, (w_gate, w_up, gate_in, up_in, hidden, active_out, slope_out) = refs[:lists], refs[lists:]
    rows = stacked(x)
    pre_gate = gate_in[...] + dot(rows, w_gate[...])
    pre_up = up_in[...] + dot(rows, w_up[...])
    sigmoid_gate = jax.nn.sigmoid(pre_gate)
    active = pre_gate * sigmoid_gate
    hidden[...] = (active * pre_up).astype(BF16)
    active_out[...] = active
    slope_out[...] = pre_up * sigmoid_gate * (1.0 + pre_gate * (1.0 - sigmoid_gate))


def expert_rows(lists, hidden, w_down, *outs):
    cap = outs[0].shape[0]
    rows = dot(hidden[...], w_down[...])
    for s in range(lists):
        outs[s][...] = rows[s * cap : (s + 1) * cap].astype(BF16)


def first_hidden_grad(lists, *refs):
    out_grad, (w_down, total) = refs[:lists], refs[lists:]
    total[...] = dot(stacked(out_grad), w_down[...], NT)


def hidden_grads(lists, *refs):
    out_grad = refs[:lists]
    w_down, first, hidden, active, slope, gate_grad, up_grad, gate_sum = refs[lists:]
    grad = first[...] + dot(stacked(out_grad), w_down[...], NT)
    gate_grad[...] = (grad * slope[...]).astype(BF16)
    up_grad[...] = (grad * active[...]).astype(BF16)
    sums = jnp.sum(grad * hidden[...].astype(F32), axis=1, keepdims=True)
    gate_sum[...] = jnp.broadcast_to(sums, gate_sum.shape)


def input_rows(lists, gate_grad, up_grad, w_gate, w_up, gate_sum, *outs):
    cap, width = outs[0].shape[0], w_gate.shape[0]
    rows = dot(gate_grad[...], w_gate[...], NT) + dot(up_grad[...], w_up[...], NT)
    for s in range(lists):
        span = slice(s * cap, (s + 1) * cap)
        outs[s][:, :width] = rows[span].astype(BF16)
        if outs[s].shape[1] > width:
            sums = gate_sum[span, :]
            high = sums.astype(BF16)
            low = (sums - high.astype(F32)).astype(BF16)
            lane = lax.broadcasted_iota(jnp.int32, sums.shape, 1)
            packed = jnp.where(lane == s, high.astype(F32), 0.0)
            packed += jnp.where(lane == lists + s, low.astype(F32), 0.0)
            outs[s][:, width:] = packed.astype(BF16)


def weight_grads(lists, *refs):
    x, out_grad = refs[:lists], refs[lists : 2 * lists]
    hidden, gate_grad, up_grad, w_gate_grad, w_up_grad, w_down_grad = refs[2 * lists :]
    rows = stacked(x)
    w_gate_grad[...] = dot(rows, gate_grad[...], TN).astype(BF16)
    w_up_grad[...] = dot(rows, up_grad[...], TN).astype(BF16)
    w_down_grad[...] = dot(hidden[...], stacked(out_grad), TN).astype(BF16)


def scatter_rows(lists, rows, *refs):
    values, out = refs[:lists], refs[lists]
    count = out.shape[0]
    total = None
    for s in range(lists):
        token = lax.broadcasted_iota(jnp.int32, (count, rows.shape[1]), 0)
        mask = jnp.where(rows[s : s + 1, :] == token, 1.0, 0.0).astype(BF16)
        term = dot(mask, values[s][...])
        total = term if total is None else total + term
    out[...] = total.astype(out.dtype)


def scatter_scaled(lists, rows, gate, *refs):
    values, out = refs[:lists], refs[lists]
    count = out.shape[0]
    total = None
    for s in range(lists):
        token = lax.broadcasted_iota(jnp.int32, (count, rows.shape[1]), 0)
        factor = gate[:, s : s + 1].astype(F32)
        mask = jnp.where(rows[s : s + 1, :] == token, factor, 0.0).astype(BF16)
        term = dot(mask, values[s][...])
        total = term if total is None else total + term
    out[...] = total.astype(out.dtype)


def add_halves(kept, arrived, out):
    out[...] = (kept[...] + arrived[...].astype(F32)).astype(BF16)


def add_halves_and_gate(lists, kept, arrived, gate, out, gate_out):
    width = out.shape[1]
    out[...] = (kept[:, :width] + arrived[:, :width].astype(F32)).astype(BF16)
    sums = kept[:, width:] + arrived[:, width:].astype(F32)
    gate_out[...] = (sums[:, :lists] + sums[:, lists : 2 * lists]) / gate[:, :lists].astype(F32)


def on_device(tokens, cotangent, gate_probs, slot_rows, w_gate, w_up, w_down):
    count, model = tokens.shape
    lists, cap = slot_rows.shape
    hidden_units = w_gate.shape[2]
    width = model // CHUNKS
    total = lists * cap
    chunks = range(CHUNKS)
    w_gate, w_up, w_down = w_gate[0], w_up[0], w_down[0]
    me = lax.axis_index("dp").astype(jnp.int32)
    own_rows = slot_rows - me * count
    oth_rows = slot_rows - (1 - me) * count
    own_column, oth_column = own_rows.reshape(total, 1), oth_rows.reshape(total, 1)
    own_gate = jnp.pad(gate_probs, ((0, 0), (0, LANES - lists)))
    run = Steps().run
    kernel = lambda body: functools.partial(body, lists)
    columns = lambda array, c: (array, part(array.shape[0], width, 0, c))
    w_rows = lambda array, c: (array, part(width, hidden_units, c, 0))
    span = lambda c: slice(c * width, (c + 1) * width)
    rows_shape = [shape(cap, width)] * lists
    square = [shape(total, hidden_units, dtype=F32)] * 2
    gather_flops = 4 * total * count * width
    flops = 2 * total * width * hidden_units

    oth_x, oth_dy, piece = [], [], None
    for c in chunks:
        source = tokens if piece is None else after(tokens, piece)
        piece = source[:, span(c)]
        oth_x.append(shifted(piece, "dp", 1))
    for c in chunks:
        piece = after(cotangent, piece)[:, span(c)]
        if c == 0:
            piece = jnp.concatenate([piece, own_gate], axis=1)
        oth_dy.append(shifted(piece, "dp", 1))
    oth_gate = (oth_dy[0], part(count, LANES, 0, width // LANES))

    x, out_grad = [], []
    for c in chunks:
        operands = [own_column, oth_column, columns(tokens, c), oth_x[c]]
        rows = run(kernel(gather_rows), rows_shape, operands, gather_flops, "gather_x")
        x.append([rows[0]] + [shifted(rows[s], "blk", -s) for s in range(1, lists)])
    for c in chunks:
        operands = [own_column, oth_column, columns(cotangent, c), oth_dy[c], own_gate, oth_gate]
        rows = run(kernel(gather_scaled), rows_shape, operands, gather_flops, "gather_dy")
        out_grad.append([rows[0]] + [shifted(rows[s], "blk", -s) for s in range(1, lists)])

    pre = run(kernel(first_products), square, x[0] + [w_rows(w_gate, 0), w_rows(w_up, 0)], 2 * flops, "pre")
    hidden, active, slope = run(
        kernel(activation),
        [shape(total, hidden_units)] + square,
        x[1] + [w_rows(w_gate, 1), w_rows(w_up, 1)] + list(pre),
        2 * flops,
        "hidden",
    )
    expert_out = []
    for c in chunks:
        rows = run(kernel(expert_rows), rows_shape, [hidden, columns(w_down, c)], flops, "expert_out")
        expert_out.append([rows[0]] + [shifted(rows[s], "blk", s) for s in range(1, lists)])

    first = run(kernel(first_hidden_grad), square[:1], out_grad[0] + [columns(w_down, 0)], flops, "hidden_grad")
    gate_grad, up_grad, gate_sum = run(
        kernel(hidden_grads),
        [shape(total, hidden_units)] * 2 + [shape(total, LANES, dtype=F32)],
        out_grad[1] + [columns(w_down, 1), first[0], hidden, active, slope],
        flops,
        "hidden_grads",
    )
    input_grad = []
    for c in chunks:
        rows = run(
            kernel(input_rows),
            [shape(cap, width + (LANES if c == 0 else 0))] * lists,
            [gate_grad, up_grad, w_rows(w_gate, c), w_rows(w_up, c), gate_sum],
            2 * flops,
            "input_grad",
        )
        input_grad.append([rows[0]] + [shifted(rows[s], "blk", s) for s in range(1, lists)])

    def halves(body, values, gates):
        extent = values[0].shape[1]
        scatter_flops = 2 * total * count * extent
        sent = run(body, [shape(count, extent)], [oth_rows] + gates[:1] + values, scatter_flops, "sent")[0]
        arrived = shifted(sent, "dp", 1)
        kept = run(body, [shape(count, extent, dtype=F32)], [own_rows] + gates[1:] + values, scatter_flops, "kept")[0]
        return kept, arrived

    mixed_halves = [halves(kernel(scatter_scaled), expert_out[c], [oth_gate, own_gate]) for c in chunks]
    weight_outs, held = (), ()
    for c in chunks:
        weight_outs = run(
            kernel(weight_grads),
            [
                (shape(model, hidden_units), part(width, hidden_units, c, 0)),
                (shape(model, hidden_units), part(width, hidden_units, c, 0)),
                (shape(hidden_units, model), part(hidden_units, width, 0, c)),
            ],
            x[c] + out_grad[c] + [hidden, gate_grad, up_grad],
            3 * flops,
            "weight_grads",
            held=weight_outs,
        )
    mixed, grad = (), ()
    wide = lambda c: (shape(count, model), part(count, width, 0, c))
    grad_halves = []
    for c in chunks:
        grad_halves.append(halves(kernel(scatter_rows), input_grad[c], []))
        mixed = run(add_halves, [wide(c)], list(mixed_halves[c]), 0, "mixed", held=mixed)
    *grad, gate_out = run(
        kernel(add_halves_and_gate),
        [wide(0), shape(count, lists, dtype=F32)],
        list(grad_halves[0]) + [own_gate],
        0,
        "grad",
    )
    for c in range(1, CHUNKS):
        grad = run(add_halves, [wide(c)], list(grad_halves[c]), 0, "grad", held=grad)
    return (mixed[0], grad[0], gate_out) + tuple(out[None] for out in weight_outs)


def solution(mesh):
    rows, lists = P(("blk", "dp"), None), P("blk", None)
    inner, outer = P("blk", None, "dp"), P("blk", "dp", None)
    return jax.shard_map(
        on_device,
        mesh=mesh,
        in_specs=(rows, rows, rows, lists, inner, inner, outer),
        out_specs=(rows, rows, rows, inner, inner, outer),
        check_vma=False,
    )
```

```python
import functools

import jax
import jax.numpy as jnp
from jax import lax
from jax.experimental import pallas as pl
from jax.experimental.pallas import tpu as pltpu
from jax.sharding import PartitionSpec as P

CHUNKS = 2
BUSY = 10
SHARED = 0.01
LANES = 128
F32 = jnp.float32
BF16 = jnp.bfloat16
NT = (((1,), (1,)), ((), ()))
TN = (((0,), (0,)), ((), ()))


def shifted(value, axis, steps):
    count = lax.axis_size(axis)
    pairs = [(source, (source + steps) % count) for source in range(count)]
    return lax.ppermute(value, axis, pairs)


def after(value, earlier):
    return lax.optimization_barrier((value, earlier))[0]


def whole(array):
    return pl.BlockSpec(array.shape, lambda i: (0,) * len(array.shape))


def part(rows, columns, row, column):
    return pl.BlockSpec((rows, columns), lambda i: (row, column))


class Steps:
    def __init__(self):
        self.last = None

    def run(self, kernel, outs, operands, flops, name, held=(), tied=0, scale=SHARED):
        pair = lambda item: item if isinstance(item, tuple) else (item, whole(item))
        pairs = [pair(operand) for operand in operands]
        arrays, specs = [array for array, _ in pairs], [spec for _, spec in pairs]
        if self.last is not None:
            arrays[tied] = after(arrays[tied], self.last)
        out_shapes, out_specs = zip(*[pair(out) for out in outs])
        moved = sum(2 * spec.block_shape[0] * spec.block_shape[1] for spec in specs + list(out_specs))
        results = pl.pallas_call(
            (lambda *refs: kernel(*refs[len(held) :])) if held else kernel,
            grid=(1,),
            out_shape=out_shapes,
            in_specs=[pl.BlockSpec(memory_space=pl.ANY)] * len(held) + specs,
            out_specs=out_specs,
            input_output_aliases={i: i for i in range(len(held))},
            compiler_params=pltpu.CompilerParams(vmem_limit_bytes=20 * 2**20),
            cost_estimate=pl.CostEstimate(flops=int(flops * scale), bytes_accessed=int(moved * scale), transcendentals=0),
            name=name,
        )(*held, *arrays)
        self.last = results[0]
        return results


def shape(*dims, dtype=BF16):
    return jax.ShapeDtypeStruct(dims, dtype)


def dot(a, b, dims=(((1,), (0,)), ((), ()))):
    return lax.dot_general(a, b, dims, preferred_element_type=F32)


def picks(rows, count):
    columns = lax.broadcasted_iota(jnp.int32, (rows.shape[0], count), 1)
    return jnp.where(rows == columns, 1.0, 0.0).astype(BF16)


def stacked(refs):
    return jnp.concatenate([ref[...] for ref in refs], axis=0)


def gather_rows(lists, own_rows, oth_rows, own, oth, *outs):
    count, cap = own.shape[0], outs[0].shape[0]
    width = own.shape[1]
    rows = dot(picks(own_rows[...], count), own[...])
    rows += dot(picks(oth_rows[...], count), oth[:, :width])
    for s in range(lists):
        outs[s][...] = rows[s * cap : (s + 1) * cap].astype(BF16)


def gather_scaled(lists, own_rows, oth_rows, own, oth, own_gate, oth_gate, *outs):
    count, cap = own.shape[0], outs[0].shape[0]
    width = own.shape[1]
    own_picks, oth_picks = picks(own_rows[...], count), picks(oth_rows[...], count)
    rows = dot(own_picks, own[...]) + dot(oth_picks, oth[:, :width])
    gate = dot(own_picks, own_gate[...]) + dot(oth_picks, oth_gate[...])
    for s in range(lists):
        span = slice(s * cap, (s + 1) * cap)
        outs[s][...] = (gate[span, s : s + 1] * rows[span]).astype(BF16)


def first_products(lists, *refs):
    x, (w_gate, w_up, gate_out, up_out) = refs[:lists], refs[lists:]
    rows = stacked(x)
    gate_out[...] = dot(rows, w_gate[...])
    up_out[...] = dot(rows, w_up[...])


def activation(lists, *refs):
    x, (w_gate, w_up, gate_in, up_in, hidden, active_out, slope_out) = refs[:lists], refs[lists:]
    rows = stacked(x)
    pre_gate = gate_in[...] + dot(rows, w_gate[...])
    pre_up = up_in[...] + dot(rows, w_up[...])
    sigmoid_gate = jax.nn.sigmoid(pre_gate)
    active = pre_gate * sigmoid_gate
    hidden[...] = (active * pre_up).astype(BF16)
    active_out[...] = active
    slope_out[...] = pre_up * sigmoid_gate * (1.0 + pre_gate * (1.0 - sigmoid_gate))


def expert_rows(me, hidden, w_down, sent, kept):
    width = kept.shape[1]
    first = dot(hidden[...], w_down[:, :width])
    second = dot(hidden[...], w_down[:, width:])
    lower = me[0, 0] == 0
    sent[...] = jnp.where(lower, second, first).astype(BF16)
    kept[...] = jnp.where(lower, first, second)


def whole_rows(kept, arrived, *outs):
    cap = outs[0].shape[0]
    rows = (kept[...] + arrived[...].astype(F32)).astype(BF16)
    for s, out in enumerate(outs):
        out[...] = rows[s * cap : (s + 1) * cap]


def first_hidden_grad(lists, *refs):
    out_grad, (w_down, total) = refs[:lists], refs[lists:]
    total[...] = dot(stacked(out_grad), w_down[...], NT)


def hidden_grads(lists, *refs):
    out_grad = refs[:lists]
    w_down, first, hidden, active, slope, gate_grad, up_grad, gate_sum = refs[lists:]
    grad = first[...] + dot(stacked(out_grad), w_down[...], NT)
    gate_grad[...] = (grad * slope[...]).astype(BF16)
    up_grad[...] = (grad * active[...]).astype(BF16)
    sums = jnp.sum(grad * hidden[...].astype(F32), axis=1, keepdims=True)
    gate_sum[...] = jnp.broadcast_to(sums, gate_sum.shape)


def input_rows(lists, gate_grad, up_grad, w_gate, w_up, gate_sum, *outs):
    cap, width = outs[0].shape[0], w_gate.shape[0]
    rows = dot(gate_grad[...], w_gate[...], NT) + dot(up_grad[...], w_up[...], NT)
    for s in range(lists):
        span = slice(s * cap, (s + 1) * cap)
        outs[s][:, :width] = rows[span].astype(BF16)
        if outs[s].shape[1] > width:
            sums = gate_sum[span, :]
            high = sums.astype(BF16)
            low = (sums - high.astype(F32)).astype(BF16)
            lane = lax.broadcasted_iota(jnp.int32, sums.shape, 1)
            packed = jnp.where(lane == s, high.astype(F32), 0.0)
            packed += jnp.where(lane == lists + s, low.astype(F32), 0.0)
            outs[s][:, width:] = packed.astype(BF16)


def weight_grads(lists, *refs):
    x, out_grad = refs[:lists], refs[lists : 2 * lists]
    hidden, gate_grad, up_grad, w_gate_grad, w_up_grad, w_down_grad = refs[2 * lists :]
    rows = stacked(x)
    w_gate_grad[...] = dot(rows, gate_grad[...], TN).astype(BF16)
    w_up_grad[...] = dot(rows, up_grad[...], TN).astype(BF16)
    w_down_grad[...] = dot(hidden[...], stacked(out_grad), TN).astype(BF16)


def scatter_rows(lists, rows, *refs):
    values, out = refs[:lists], refs[lists]
    count = out.shape[0]
    total = None
    for s in range(lists):
        token = lax.broadcasted_iota(jnp.int32, (count, rows.shape[1]), 0)
        mask = jnp.where(rows[s : s + 1, :] == token, 1.0, 0.0).astype(BF16)
        term = dot(mask, values[s][...])
        total = term if total is None else total + term
    out[...] = total.astype(out.dtype)


def scatter_scaled(lists, rows, gate, *refs):
    values, out = refs[:lists], refs[lists]
    count = out.shape[0]
    total = None
    for s in range(lists):
        token = lax.broadcasted_iota(jnp.int32, (count, rows.shape[1]), 0)
        factor = gate[:, s : s + 1].astype(F32)
        mask = jnp.where(rows[s : s + 1, :] == token, factor, 0.0).astype(BF16)
        term = dot(mask, values[s][...])
        total = term if total is None else total + term
    out[...] = total.astype(out.dtype)


def join(me, own, arrived, out):
    width = own.shape[1]
    lower = me[0, 0] == 0
    out[:, :width] = jnp.where(lower, own[...], arrived[...])
    out[:, width:] = jnp.where(lower, arrived[...], own[...])


def add_halves(kept, arrived, out):
    out[...] = (kept[...] + arrived[...].astype(F32)).astype(BF16)


def add_halves_and_gate(lists, kept, arrived, gate, out, gate_out):
    width = out.shape[1]
    out[...] = (kept[:, :width] + arrived[:, :width].astype(F32)).astype(BF16)
    sums = kept[:, width:] + arrived[:, width:].astype(F32)
    gate_out[...] = (sums[:, :lists] + sums[:, lists : 2 * lists]) / gate[:, :lists].astype(F32)


def on_device(tokens, cotangent, gate_probs, slot_rows, w_gate, w_up, w_down):
    count, model = tokens.shape
    lists, cap = slot_rows.shape
    hidden_units = w_gate.shape[2]
    width = model // CHUNKS
    total = lists * cap
    chunks = range(CHUNKS)
    w_gate, w_up, w_down = w_gate[0], w_up[0], w_down[0]
    me = lax.axis_index("dp").astype(jnp.int32)
    own_rows = slot_rows - me * count
    oth_rows = slot_rows - (1 - me) * count
    own_column, oth_column = own_rows.reshape(total, 1), oth_rows.reshape(total, 1)
    own_gate = jnp.pad(gate_probs, ((0, 0), (0, LANES - lists)))
    run = Steps().run
    kernel = lambda body: functools.partial(body, lists)
    columns = lambda array, c: (array, part(array.shape[0], width, 0, c))
    w_rows = lambda array, c: (array, part(width, hidden_units, c, 0))
    span = lambda c: slice(c * width, (c + 1) * width)
    rows_shape = [shape(cap, width)] * lists
    square = [shape(total, hidden_units, dtype=F32)] * 2
    gather_flops = 4 * total * count * width
    flops = 2 * total * width * hidden_units

    scalar = (me.reshape(1, 1), pl.BlockSpec((1, 1), lambda i: (0, 0), memory_space=pltpu.SMEM))

    def to_experts(rows):
        return [rows[0]] + [shifted(rows[s], "blk", -s) for s in range(1, lists)]

    def to_groups(rows):
        return [rows[0]] + [shifted(rows[s], "blk", s) for s in range(1, lists)]

    def gather_x(c):
        operands = [own_column, oth_column, columns(tokens, c), oth_x[c]]
        return to_experts(run(kernel(gather_rows), rows_shape, operands, gather_flops, "gather_x", tied=3))

    def gather_dy(c):
        operands = [own_column, oth_column, columns(cotangent, c), oth_dy[c], own_gate, oth_gate]
        return to_experts(run(kernel(gather_scaled), rows_shape, operands, gather_flops, "gather_dy", tied=3))

    def input_grads(c, scale=SHARED):
        operands = [gate_grad, up_grad, w_rows(w_gate, c), w_rows(w_up, c), gate_sum]
        outs = [shape(cap, width + (LANES if c == 0 else 0))] * lists
        return to_groups(run(kernel(input_rows), outs, operands, 2 * flops, "input_grad", scale=scale))

    def weights(c, held):
        rows_out = (shape(model, hidden_units), part(width, hidden_units, c, 0))
        columns_out = (shape(hidden_units, model), part(hidden_units, width, 0, c))
        operands = x[c] + out_grad[c] + [hidden, gate_grad, up_grad]
        return run(kernel(weight_grads), [rows_out, rows_out, columns_out], operands, 3 * flops, "w_grads", held=held)

    def scatter(body, rows, values, gates, dtype, name):
        extent = values[0].shape[1]
        outs = [shape(count, extent, dtype=dtype)]
        return run(body, outs, [rows] + gates + values, 2 * total * count * extent, name, tied=-1)[0]

    first_x = tokens[:, span(0)]
    second_x = after(tokens, first_x)[:, span(1)]
    oth_x = [shifted(first_x, "dp", 1), shifted(second_x, "dp", 1)]
    first_dy = jnp.concatenate([cotangent[:, span(0)], own_gate], axis=1)
    oth_dy = [shifted(after(first_dy, oth_x[0]), "dp", 1)]
    oth_gate = (oth_dy[0], part(count, LANES, 0, width // LANES))
    x = [gather_x(0), gather_x(1)]

    pre = run(kernel(first_products), square, x[0] + [w_rows(w_gate, 0), w_rows(w_up, 0)], 2 * flops, "pre")
    oth_dy.append(shifted(after(cotangent[:, span(1)], pre[0]), "dp", 1))
    out_grad = [gather_dy(0)]
    hidden, active, slope = run(
        kernel(activation),
        [shape(total, hidden_units)] + square,
        x[1] + [w_rows(w_gate, 1), w_rows(w_up, 1)] + list(pre),
        2 * flops,
        "hidden",
    )
    sent, kept = run(
        expert_rows, [shape(total, width), shape(total, width, dtype=F32)], [scalar, hidden, w_down], 2 * flops,
        "expert_out", tied=1,
    )
    arrived = shifted(sent, "dp", 1)
    out_grad.append(gather_dy(1))

    first = run(kernel(first_hidden_grad), square[:1], out_grad[0] + [columns(w_down, 0)], flops, "hidden_grad", scale=BUSY)
    gate_grad, up_grad, gate_sum = run(
        kernel(hidden_grads),
        [shape(total, hidden_units)] * 2 + [shape(total, LANES, dtype=F32)],
        out_grad[1] + [columns(w_down, 1), first[0], hidden, active, slope],
        flops,
        "hidden_grads",
        scale=BUSY,
    )
    input_grad = [input_grads(0, BUSY)]
    expert_out = to_groups(run(whole_rows, rows_shape, [kept, arrived], 0, "expert_out_rows"))

    sent = scatter(kernel(scatter_rows), oth_rows, input_grad[0], [], BF16, "grad_sent")
    grad_arrived = [shifted(sent, "dp", 1)]
    input_grad.append(input_grads(1))
    grad_kept = [scatter(kernel(scatter_rows), own_rows, input_grad[0], [], F32, "grad_kept")]
    weight_outs = weights(1, weights(0, ()))
    sent = scatter(kernel(scatter_scaled), oth_rows, expert_out, [oth_gate], BF16, "mixed_sent")
    mixed_arrived = shifted(sent, "dp", 1)
    mixed_own = scatter(kernel(scatter_scaled), own_rows, expert_out, [own_gate], BF16, "mixed_own")
    wide = lambda c: (shape(count, model), part(count, width, 0, c))
    sent = scatter(kernel(scatter_rows), oth_rows, input_grad[1], [], BF16, "grad_sent")
    grad_arrived.append(shifted(sent, "dp", 1))
    *grad, gate_out = run(
        kernel(add_halves_and_gate),
        [wide(0), shape(count, lists, dtype=F32)],
        [grad_kept[0], grad_arrived[0], own_gate],
        0,
        "grad",
    )
    grad_kept.append(scatter(kernel(scatter_rows), own_rows, input_grad[1], [], F32, "grad_kept"))
    mixed = run(join, [shape(count, model)], [scalar, mixed_own, mixed_arrived], 0, "mixed", tied=1)[0]
    grad = run(add_halves, [wide(1)], [grad_kept[1], grad_arrived[1]], 0, "grad", held=grad)[0]
    return (mixed, grad, gate_out) + tuple(out[None] for out in weight_outs)


def solution(mesh):
    rows, lists = P(("blk", "dp"), None), P("blk", None)
    inner, outer = P("blk", None, "dp"), P("blk", "dp", None)
    return jax.shard_map(
        on_device,
        mesh=mesh,
        in_specs=(rows, rows, rows, lists, inner, inner, outer),
        out_specs=(rows, rows, rows, inner, inner, outer),
        check_vma=False,
    )
```

```python
import functools

import jax
import jax.numpy as jnp
from jax import lax
from jax.experimental import pallas as pl
from jax.experimental.pallas import tpu as pltpu
from jax.sharding import PartitionSpec as P

CHUNKS = 2
BUSY = 10
SHARED = 0.01
LANES = 128
F32 = jnp.float32
BF16 = jnp.bfloat16
NT = (((1,), (1,)), ((), ()))
TN = (((0,), (0,)), ((), ()))


def shifted(value, axis, steps):
    count = lax.axis_size(axis)
    pairs = [(source, (source + steps) % count) for source in range(count)]
    return lax.ppermute(value, axis, pairs)


def after(value, earlier):
    return lax.optimization_barrier((value, earlier))[0]


def whole(array):
    return pl.BlockSpec(array.shape, lambda i: (0,) * len(array.shape))


def part(rows, columns, row, column):
    return pl.BlockSpec((rows, columns), lambda i: (row, column))


class Steps:
    def __init__(self):
        self.last = None

    def run(self, kernel, outs, operands, flops, name, held=(), tied=0, scale=SHARED):
        pair = lambda item: item if isinstance(item, tuple) else (item, whole(item))
        pairs = [pair(operand) for operand in operands]
        arrays, specs = [array for array, _ in pairs], [spec for _, spec in pairs]
        if self.last is not None:
            arrays[tied] = after(arrays[tied], self.last)
        out_shapes, out_specs = zip(*[pair(out) for out in outs])
        moved = sum(2 * spec.block_shape[0] * spec.block_shape[1] for spec in specs + list(out_specs))
        results = pl.pallas_call(
            (lambda *refs: kernel(*refs[len(held) :])) if held else kernel,
            grid=(1,),
            out_shape=out_shapes,
            in_specs=[pl.BlockSpec(memory_space=pl.ANY)] * len(held) + specs,
            out_specs=out_specs,
            input_output_aliases={i: i for i in range(len(held))},
            compiler_params=pltpu.CompilerParams(vmem_limit_bytes=20 * 2**20),
            cost_estimate=pl.CostEstimate(flops=int(flops * scale), bytes_accessed=int(moved * scale), transcendentals=0),
            name=name,
        )(*held, *arrays)
        self.last = results[0]
        return results


def shape(*dims, dtype=BF16):
    return jax.ShapeDtypeStruct(dims, dtype)


def dot(a, b, dims=(((1,), (0,)), ((), ()))):
    return lax.dot_general(a, b, dims, preferred_element_type=F32)


def picks(rows, count):
    columns = lax.broadcasted_iota(jnp.int32, (rows.shape[0], count), 1)
    return jnp.where(rows == columns, 1.0, 0.0).astype(BF16)


def stacked(refs):
    return jnp.concatenate([ref[...] for ref in refs], axis=0)


def gather_rows(lists, own_rows, oth_rows, own, oth, *outs):
    count, cap = own.shape[0], outs[0].shape[0]
    width = own.shape[1]
    rows = dot(picks(own_rows[...], count), own[...])
    rows += dot(picks(oth_rows[...], count), oth[:, :width])
    for s in range(lists):
        outs[s][...] = rows[s * cap : (s + 1) * cap].astype(BF16)


def gather_scaled(lists, own_rows, oth_rows, own, oth, own_gate, oth_gate, *outs):
    count, cap = own.shape[0], outs[0].shape[0]
    width = own.shape[1]
    own_picks, oth_picks = picks(own_rows[...], count), picks(oth_rows[...], count)
    rows = dot(own_picks, own[...]) + dot(oth_picks, oth[:, :width])
    gate = dot(own_picks, own_gate[...]) + dot(oth_picks, oth_gate[...])
    for s in range(lists):
        span = slice(s * cap, (s + 1) * cap)
        outs[s][...] = (gate[span, s : s + 1] * rows[span]).astype(BF16)


def first_products(lists, *refs):
    x, (w_gate, w_up, gate_out, up_out) = refs[:lists], refs[lists:]
    rows = stacked(x)
    gate_out[...] = dot(rows, w_gate[...])
    up_out[...] = dot(rows, w_up[...])


def activation(lists, *refs):
    x, (w_gate, w_up, gate_in, up_in, hidden, active_out, slope_out) = refs[:lists], refs[lists:]
    rows = stacked(x)
    pre_gate = gate_in[...] + dot(rows, w_gate[...])
    pre_up = up_in[...] + dot(rows, w_up[...])
    sigmoid_gate = jax.nn.sigmoid(pre_gate)
    active = pre_gate * sigmoid_gate
    hidden[...] = (active * pre_up).astype(BF16)
    active_out[...] = active
    slope_out[...] = pre_up * sigmoid_gate * (1.0 + pre_gate * (1.0 - sigmoid_gate))


def expert_rows(me, hidden, w_down, sent, kept):
    width = kept.shape[1]
    first = dot(hidden[...], w_down[:, :width])
    second = dot(hidden[...], w_down[:, width:])
    lower = me[0, 0] == 0
    sent[...] = jnp.where(lower, second, first).astype(BF16)
    kept[...] = jnp.where(lower, first, second)


def whole_rows(kept, arrived, *outs):
    cap = outs[0].shape[0]
    rows = (kept[...] + arrived[...].astype(F32)).astype(BF16)
    for s, out in enumerate(outs):
        out[...] = rows[s * cap : (s + 1) * cap]


def first_hidden_grad(lists, *refs):
    out_grad, (w_down, total) = refs[:lists], refs[lists:]
    total[...] = dot(stacked(out_grad), w_down[...], NT)


def hidden_grads(lists, *refs):
    out_grad = refs[:lists]
    w_down, first, hidden, active, slope, gate_grad, up_grad, gate_sum = refs[lists:]
    grad = first[...] + dot(stacked(out_grad), w_down[...], NT)
    gate_grad[...] = (grad * slope[...]).astype(BF16)
    up_grad[...] = (grad * active[...]).astype(BF16)
    sums = jnp.sum(grad * hidden[...].astype(F32), axis=1, keepdims=True)
    gate_sum[...] = jnp.broadcast_to(sums, gate_sum.shape)


def input_rows(lists, gate_grad, up_grad, w_gate, w_up, gate_sum, *outs):
    cap, width = outs[0].shape[0], w_gate.shape[0]
    rows = dot(gate_grad[...], w_gate[...], NT) + dot(up_grad[...], w_up[...], NT)
    for s in range(lists):
        span = slice(s * cap, (s + 1) * cap)
        outs[s][:, :width] = rows[span].astype(BF16)
        if outs[s].shape[1] > width:
            sums = gate_sum[span, :]
            high = sums.astype(BF16)
            low = (sums - high.astype(F32)).astype(BF16)
            lane = lax.broadcasted_iota(jnp.int32, sums.shape, 1)
            packed = jnp.where(lane == s, high.astype(F32), 0.0)
            packed += jnp.where(lane == lists + s, low.astype(F32), 0.0)
            outs[s][:, width:] = packed.astype(BF16)


def input_halves(me, gate_grad, up_grad, w_gate, w_up, sent, kept):
    width = kept.shape[1]
    half = lambda span: dot(gate_grad[...], w_gate[span, :], NT) + dot(up_grad[...], w_up[span, :], NT)
    first, second = half(slice(0, width)), half(slice(width, 2 * width))
    lower = me[0, 0] == 0
    sent[...] = jnp.where(lower, second, first).astype(BF16)
    kept[...] = jnp.where(lower, first, second)


def weight_grads(lists, *refs):
    x, out_grad = refs[:lists], refs[lists : 2 * lists]
    hidden, gate_grad, up_grad, w_gate_grad, w_up_grad, w_down_grad = refs[2 * lists :]
    rows = stacked(x)
    w_gate_grad[...] = dot(rows, gate_grad[...], TN).astype(BF16)
    w_up_grad[...] = dot(rows, up_grad[...], TN).astype(BF16)
    w_down_grad[...] = dot(hidden[...], stacked(out_grad), TN).astype(BF16)


def scatter_rows(lists, rows, *refs):
    values, out = refs[:lists], refs[lists]
    count = out.shape[0]
    total = None
    for s in range(lists):
        token = lax.broadcasted_iota(jnp.int32, (count, rows.shape[1]), 0)
        mask = jnp.where(rows[s : s + 1, :] == token, 1.0, 0.0).astype(BF16)
        term = dot(mask, values[s][...])
        total = term if total is None else total + term
    out[...] = total.astype(out.dtype)


def scatter_scaled(lists, rows, gate, *refs):
    values, out = refs[:lists], refs[lists]
    count = out.shape[0]
    total = None
    for s in range(lists):
        token = lax.broadcasted_iota(jnp.int32, (count, rows.shape[1]), 0)
        factor = gate[:, s : s + 1].astype(F32)
        mask = jnp.where(rows[s : s + 1, :] == token, factor, 0.0).astype(BF16)
        term = dot(mask, values[s][...])
        total = term if total is None else total + term
    out[...] = total.astype(out.dtype)


def join(me, own, arrived, out):
    width = own.shape[1]
    lower = me[0, 0] == 0
    out[:, :width] = jnp.where(lower, own[...], arrived[...])
    out[:, width:] = jnp.where(lower, arrived[...], own[...])


def add_halves_and_gate(lists, kept, arrived, gate, out, gate_out):
    width = out.shape[1]
    out[...] = (kept[:, :width] + arrived[:, :width].astype(F32)).astype(BF16)
    sums = kept[:, width:] + arrived[:, width:].astype(F32)
    gate_out[...] = (sums[:, :lists] + sums[:, lists : 2 * lists]) / gate[:, :lists].astype(F32)


def on_device(tokens, cotangent, gate_probs, slot_rows, w_gate, w_up, w_down):
    count, model = tokens.shape
    lists, cap = slot_rows.shape
    hidden_units = w_gate.shape[2]
    width = model // CHUNKS
    total = lists * cap
    chunks = range(CHUNKS)
    w_gate, w_up, w_down = w_gate[0], w_up[0], w_down[0]
    me = lax.axis_index("dp").astype(jnp.int32)
    own_rows = slot_rows - me * count
    oth_rows = slot_rows - (1 - me) * count
    own_column, oth_column = own_rows.reshape(total, 1), oth_rows.reshape(total, 1)
    own_gate = jnp.pad(gate_probs, ((0, 0), (0, LANES - lists)))
    run = Steps().run
    kernel = lambda body: functools.partial(body, lists)
    columns = lambda array, c: (array, part(array.shape[0], width, 0, c))
    w_rows = lambda array, c: (array, part(width, hidden_units, c, 0))
    span = lambda c: slice(c * width, (c + 1) * width)
    rows_shape = [shape(cap, width)] * lists
    square = [shape(total, hidden_units, dtype=F32)] * 2
    gather_flops = 4 * total * count * width
    flops = 2 * total * width * hidden_units

    scalar = (me.reshape(1, 1), pl.BlockSpec((1, 1), lambda i: (0, 0), memory_space=pltpu.SMEM))

    def to_experts(rows):
        return [rows[0]] + [shifted(rows[s], "blk", -s) for s in range(1, lists)]

    def to_groups(rows):
        return [rows[0]] + [shifted(rows[s], "blk", s) for s in range(1, lists)]

    def gather_x(c):
        operands = [own_column, oth_column, columns(tokens, c), oth_x[c]]
        return to_experts(run(kernel(gather_rows), rows_shape, operands, gather_flops, "gather_x", tied=3))

    def gather_dy(c):
        operands = [own_column, oth_column, columns(cotangent, c), oth_dy[c], own_gate, oth_gate]
        return to_experts(run(kernel(gather_scaled), rows_shape, operands, gather_flops, "gather_dy", tied=3))

    def input_grads(c, scale=SHARED):
        operands = [gate_grad, up_grad, w_rows(w_gate, c), w_rows(w_up, c), gate_sum]
        outs = [shape(cap, width + (LANES if c == 0 else 0))] * lists
        return to_groups(run(kernel(input_rows), outs, operands, 2 * flops, "input_grad", scale=scale))

    def weights(c, held):
        rows_out = (shape(model, hidden_units), part(width, hidden_units, c, 0))
        columns_out = (shape(hidden_units, model), part(hidden_units, width, 0, c))
        operands = x[c] + out_grad[c] + [hidden, gate_grad, up_grad]
        return run(kernel(weight_grads), [rows_out, rows_out, columns_out], operands, 3 * flops, "w_grads", held=held)

    def scatter(body, rows, values, gates, dtype, name):
        extent = values[0].shape[1]
        outs = [shape(count, extent, dtype=dtype)]
        return run(body, outs, [rows] + gates + values, 2 * total * count * extent, name, tied=-1, scale=BUSY)[0]

    first_x = tokens[:, span(0)]
    second_x = after(tokens, first_x)[:, span(1)]
    oth_x = [shifted(first_x, "dp", 1), shifted(second_x, "dp", 1)]
    first_dy = jnp.concatenate([after(cotangent, second_x)[:, span(0)], own_gate], axis=1)
    oth_dy = [shifted(first_dy, "dp", 1)]
    oth_gate = (oth_dy[0], part(count, LANES, 0, width // LANES))
    x = [gather_x(0), gather_x(1)]

    pre = run(kernel(first_products), square, x[0] + [w_rows(w_gate, 0), w_rows(w_up, 0)], 2 * flops, "pre")
    oth_dy.append(shifted(after(cotangent[:, span(1)], pre[0]), "dp", 1))
    out_grad = [gather_dy(0)]
    hidden, active, slope = run(
        kernel(activation),
        [shape(total, hidden_units)] + square,
        x[1] + [w_rows(w_gate, 1), w_rows(w_up, 1)] + list(pre),
        2 * flops,
        "hidden",
        scale=BUSY,
    )
    sent, kept = run(
        expert_rows, [shape(total, width), shape(total, width, dtype=F32)], [scalar, hidden, w_down], 2 * flops,
        "expert_out", tied=1, scale=BUSY,
    )
    arrived = shifted(sent, "dp", 1)
    out_grad.append(gather_dy(1))

    first = run(kernel(first_hidden_grad), square[:1], out_grad[0] + [columns(w_down, 0)], flops, "hidden_grad", scale=BUSY)
    gate_grad, up_grad, gate_sum = run(
        kernel(hidden_grads),
        [shape(total, hidden_units)] * 2 + [shape(total, LANES, dtype=F32)],
        out_grad[1] + [columns(w_down, 1), first[0], hidden, active, slope],
        flops,
        "hidden_grads",
        scale=BUSY,
    )
    first_rows = input_grads(0, BUSY)
    half = width // 2
    sent, second_kept = run(
        input_halves,
        [shape(total, half), shape(total, half, dtype=F32)],
        [scalar, gate_grad, up_grad, w_rows(w_gate, 1), w_rows(w_up, 1)],
        2 * flops,
        "input_grad",
        tied=1,
    )
    second_arrived = shifted(sent, "dp", 1)
    expert_out = to_groups(run(whole_rows, rows_shape, [kept, arrived], 0, "expert_out_rows"))
    weight_outs = weights(1, weights(0, ()))

    half_shape = [shape(cap, half)] * lists
    second_rows = to_groups(run(whole_rows, half_shape, [second_kept, second_arrived], 0, "input_grad_rows"))
    sent = scatter(kernel(scatter_rows), oth_rows, first_rows, [], BF16, "grad_sent")
    first_arrived = shifted(sent, "dp", 1)
    first_kept = scatter(kernel(scatter_rows), own_rows, first_rows, [], F32, "grad_kept")
    sent = scatter(kernel(scatter_scaled), oth_rows, expert_out, [oth_gate], BF16, "mixed_sent")
    mixed_arrived = shifted(sent, "dp", 1)
    mixed_own = scatter(kernel(scatter_scaled), own_rows, expert_out, [own_gate], BF16, "mixed_own")
    sent = scatter(kernel(scatter_rows), oth_rows, second_rows, [], BF16, "grad_sent")
    second_arrived = shifted(sent, "dp", 1)
    second_own = scatter(kernel(scatter_rows), own_rows, second_rows, [], BF16, "grad_own")
    wide = lambda c: (shape(count, model), part(count, width, 0, c))
    *grad, gate_out = run(
        kernel(add_halves_and_gate),
        [wide(0), shape(count, lists, dtype=F32)],
        [first_kept, first_arrived, own_gate],
        0,
        "grad",
    )
    mixed = run(join, [shape(count, model)], [scalar, mixed_own, mixed_arrived], 0, "mixed", tied=1)[0]
    grad = run(join, [wide(1)], [scalar, second_own, second_arrived], 0, "grad", held=grad, tied=1)[0]
    return (mixed, grad, gate_out) + tuple(out[None] for out in weight_outs)


def solution(mesh):
    rows, lists = P(("blk", "dp"), None), P("blk", None)
    inner, outer = P("blk", None, "dp"), P("blk", "dp", None)
    return jax.shard_map(
        on_device,
        mesh=mesh,
        in_specs=(rows, rows, rows, lists, inner, inner, outer),
        out_specs=(rows, rows, rows, inner, inner, outer),
        check_vma=False,
    )
```

```python
import functools

import jax
import jax.numpy as jnp
from jax import lax
from jax.experimental import pallas as pl
from jax.experimental.pallas import tpu as pltpu
from jax.sharding import PartitionSpec as P

CHUNKS = 2
BUSY = 10
SHARED = 0.01
LANES = 128
F32 = jnp.float32
BF16 = jnp.bfloat16
NT = (((1,), (1,)), ((), ()))
TN = (((0,), (0,)), ((), ()))


def shifted(value, axis, steps):
    count = lax.axis_size(axis)
    pairs = [(source, (source + steps) % count) for source in range(count)]
    return lax.ppermute(value, axis, pairs)


def after(value, earlier):
    return lax.optimization_barrier((value, earlier))[0]


def whole(array):
    return pl.BlockSpec(array.shape, lambda i: (0,) * len(array.shape))


def part(rows, columns, row, column):
    return pl.BlockSpec((rows, columns), lambda i: (row, column))


class Steps:
    def __init__(self):
        self.last = None

    def run(self, kernel, outs, operands, flops, name, held=(), tied=0, scale=SHARED):
        pair = lambda item: item if isinstance(item, tuple) else (item, whole(item))
        pairs = [pair(operand) for operand in operands]
        arrays, specs = [array for array, _ in pairs], [spec for _, spec in pairs]
        if self.last is not None:
            arrays[tied] = after(arrays[tied], self.last)
        out_shapes, out_specs = zip(*[pair(out) for out in outs])
        moved = sum(2 * spec.block_shape[0] * spec.block_shape[1] for spec in specs + list(out_specs))
        results = pl.pallas_call(
            (lambda *refs: kernel(*refs[len(held) :])) if held else kernel,
            grid=(1,),
            out_shape=out_shapes,
            in_specs=[pl.BlockSpec(memory_space=pl.ANY)] * len(held) + specs,
            out_specs=out_specs,
            input_output_aliases={i: i for i in range(len(held))},
            compiler_params=pltpu.CompilerParams(vmem_limit_bytes=20 * 2**20),
            cost_estimate=pl.CostEstimate(flops=int(flops * scale), bytes_accessed=int(moved * scale), transcendentals=0),
            name=name,
        )(*held, *arrays)
        self.last = results[0]
        return results


def shape(*dims, dtype=BF16):
    return jax.ShapeDtypeStruct(dims, dtype)


def dot(a, b, dims=(((1,), (0,)), ((), ()))):
    return lax.dot_general(a, b, dims, preferred_element_type=F32)


def picks(rows, count):
    columns = lax.broadcasted_iota(jnp.int32, (rows.shape[0], count), 1)
    return jnp.where(rows == columns, 1.0, 0.0).astype(BF16)


def stacked(refs):
    return jnp.concatenate([ref[...] for ref in refs], axis=0)


def gather_rows(lists, own_rows, oth_rows, own, oth, *outs):
    count, cap = own.shape[0], outs[0].shape[0]
    width = own.shape[1]
    rows = dot(picks(own_rows[...], count), own[...])
    rows += dot(picks(oth_rows[...], count), oth[:, :width])
    for s in range(lists):
        outs[s][...] = rows[s * cap : (s + 1) * cap].astype(BF16)


def gather_scaled(lists, own_rows, oth_rows, own, oth, own_gate, oth_gate, *outs):
    count, cap = own.shape[0], outs[0].shape[0]
    width = own.shape[1]
    own_picks, oth_picks = picks(own_rows[...], count), picks(oth_rows[...], count)
    rows = dot(own_picks, own[...]) + dot(oth_picks, oth[:, :width])
    gate = dot(own_picks, own_gate[...]) + dot(oth_picks, oth_gate[...])
    for s in range(lists):
        span = slice(s * cap, (s + 1) * cap)
        outs[s][...] = (gate[span, s : s + 1] * rows[span]).astype(BF16)


def first_products(lists, *refs):
    x, (w_gate, w_up, gate_out, up_out) = refs[:lists], refs[lists:]
    rows = stacked(x)
    gate_out[...] = dot(rows, w_gate[...])
    up_out[...] = dot(rows, w_up[...])


def activation(lists, *refs):
    x, (w_gate, w_up, gate_in, up_in, hidden, active_out, slope_out) = refs[:lists], refs[lists:]
    rows = stacked(x)
    pre_gate = gate_in[...] + dot(rows, w_gate[...])
    pre_up = up_in[...] + dot(rows, w_up[...])
    sigmoid_gate = jax.nn.sigmoid(pre_gate)
    active = pre_gate * sigmoid_gate
    hidden[...] = (active * pre_up).astype(BF16)
    active_out[...] = active
    slope_out[...] = pre_up * sigmoid_gate * (1.0 + pre_gate * (1.0 - sigmoid_gate))


def expert_rows(me, hidden, w_down, sent, kept):
    width = kept.shape[1]
    first = dot(hidden[...], w_down[:, :width])
    second = dot(hidden[...], w_down[:, width:])
    lower = me[0, 0] == 0
    sent[...] = jnp.where(lower, second, first).astype(BF16)
    kept[...] = jnp.where(lower, first, second)


def whole_rows(kept, arrived, *outs):
    cap = outs[0].shape[0]
    rows = (kept[...] + arrived[...].astype(F32)).astype(BF16)
    for s, out in enumerate(outs):
        out[...] = rows[s * cap : (s + 1) * cap]


def first_hidden_grad(lists, *refs):
    out_grad, (w_down, total) = refs[:lists], refs[lists:]
    total[...] = dot(stacked(out_grad), w_down[...], NT)


def hidden_grads(lists, *refs):
    out_grad = refs[:lists]
    w_down, first, hidden, active, slope, gate_grad, up_grad, gate_sum = refs[lists:]
    grad = first[...] + dot(stacked(out_grad), w_down[...], NT)
    gate_grad[...] = (grad * slope[...]).astype(BF16)
    up_grad[...] = (grad * active[...]).astype(BF16)
    sums = jnp.sum(grad * hidden[...].astype(F32), axis=1, keepdims=True)
    gate_sum[...] = jnp.broadcast_to(sums, gate_sum.shape)


def input_rows(lists, gate_grad, up_grad, w_gate, w_up, gate_sum, *outs):
    cap, width = outs[0].shape[0], w_gate.shape[0]
    rows = dot(gate_grad[...], w_gate[...], NT) + dot(up_grad[...], w_up[...], NT)
    for s in range(lists):
        span = slice(s * cap, (s + 1) * cap)
        outs[s][:, :width] = rows[span].astype(BF16)
        if outs[s].shape[1] > width:
            sums = gate_sum[span, :]
            high = sums.astype(BF16)
            low = (sums - high.astype(F32)).astype(BF16)
            lane = lax.broadcasted_iota(jnp.int32, sums.shape, 1)
            packed = jnp.where(lane == s, high.astype(F32), 0.0)
            packed += jnp.where(lane == lists + s, low.astype(F32), 0.0)
            outs[s][:, width:] = packed.astype(BF16)


def input_halves(me, gate_grad, up_grad, w_gate, w_up, sent, kept):
    width = kept.shape[1]
    half = lambda span: dot(gate_grad[...], w_gate[span, :], NT) + dot(up_grad[...], w_up[span, :], NT)
    first, second = half(slice(0, width)), half(slice(width, 2 * width))
    lower = me[0, 0] == 0
    sent[...] = jnp.where(lower, second, first).astype(BF16)
    kept[...] = jnp.where(lower, first, second)


def weight_grads(lists, *refs):
    x, out_grad = refs[:lists], refs[lists : 2 * lists]
    hidden, gate_grad, up_grad, w_gate_grad, w_up_grad, w_down_grad = refs[2 * lists :]
    rows = stacked(x)
    w_gate_grad[...] = dot(rows, gate_grad[...], TN).astype(BF16)
    w_up_grad[...] = dot(rows, up_grad[...], TN).astype(BF16)
    w_down_grad[...] = dot(hidden[...], stacked(out_grad), TN).astype(BF16)


def scatter_rows(lists, rows, *refs):
    values, out = refs[:lists], refs[lists]
    count = out.shape[0]
    total = None
    for s in range(lists):
        token = lax.broadcasted_iota(jnp.int32, (count, rows.shape[1]), 0)
        mask = jnp.where(rows[s : s + 1, :] == token, 1.0, 0.0).astype(BF16)
        term = dot(mask, values[s][...])
        total = term if total is None else total + term
    out[...] = total.astype(out.dtype)


def scatter_scaled(lists, rows, gate, *refs):
    values, out = refs[:lists], refs[lists]
    count = out.shape[0]
    total = None
    for s in range(lists):
        token = lax.broadcasted_iota(jnp.int32, (count, rows.shape[1]), 0)
        factor = gate[:, s : s + 1].astype(F32)
        mask = jnp.where(rows[s : s + 1, :] == token, factor, 0.0).astype(BF16)
        term = dot(mask, values[s][...])
        total = term if total is None else total + term
    out[...] = total.astype(out.dtype)


def join(me, own, arrived, out):
    width = own.shape[1]
    lower = me[0, 0] == 0
    out[:, :width] = jnp.where(lower, own[...], arrived[...])
    out[:, width:] = jnp.where(lower, arrived[...], own[...])


def add_halves_and_gate(lists, kept, arrived, gate, out, gate_out):
    width = out.shape[1]
    out[...] = (kept[:, :width] + arrived[:, :width].astype(F32)).astype(BF16)
    sums = kept[:, width:] + arrived[:, width:].astype(F32)
    gate_out[...] = (sums[:, :lists] + sums[:, lists : 2 * lists]) / gate[:, :lists].astype(F32)


def on_device(tokens, cotangent, gate_probs, slot_rows, w_gate, w_up, w_down):
    count, model = tokens.shape
    lists, cap = slot_rows.shape
    hidden_units = w_gate.shape[2]
    width = model // CHUNKS
    total = lists * cap
    chunks = range(CHUNKS)
    w_gate, w_up, w_down = w_gate[0], w_up[0], w_down[0]
    me = lax.axis_index("dp").astype(jnp.int32)
    own_rows = slot_rows - me * count
    oth_rows = slot_rows - (1 - me) * count
    own_column, oth_column = own_rows.reshape(total, 1), oth_rows.reshape(total, 1)
    own_gate = jnp.pad(gate_probs, ((0, 0), (0, LANES - lists)))
    run = Steps().run
    kernel = lambda body: functools.partial(body, lists)
    columns = lambda array, c: (array, part(array.shape[0], width, 0, c))
    w_rows = lambda array, c: (array, part(width, hidden_units, c, 0))
    span = lambda c: slice(c * width, (c + 1) * width)
    rows_shape = [shape(cap, width)] * lists
    square = [shape(total, hidden_units, dtype=F32)] * 2
    gather_flops = 4 * total * count * width
    flops = 2 * total * width * hidden_units

    scalar = (me.reshape(1, 1), pl.BlockSpec((1, 1), lambda i: (0, 0), memory_space=pltpu.SMEM))

    def to_experts(rows):
        return [rows[0]] + [shifted(rows[s], "blk", -s) for s in range(1, lists)]

    def to_groups(rows):
        return [rows[0]] + [shifted(rows[s], "blk", s) for s in range(1, lists)]

    def gather_x(c):
        operands = [own_column, oth_column, columns(tokens, c), oth_x[c]]
        return to_experts(run(kernel(gather_rows), rows_shape, operands, gather_flops, "gather_x", tied=3))

    def gather_dy(c):
        operands = [own_column, oth_column, columns(cotangent, c), oth_dy[c], own_gate, oth_gate]
        return to_experts(run(kernel(gather_scaled), rows_shape, operands, gather_flops, "gather_dy", tied=3))

    def input_grads(c, scale=SHARED):
        operands = [gate_grad, up_grad, w_rows(w_gate, c), w_rows(w_up, c), gate_sum]
        outs = [shape(cap, width + (LANES if c == 0 else 0))] * lists
        return to_groups(run(kernel(input_rows), outs, operands, 2 * flops, "input_grad", scale=scale))

    def weights(c, held):
        rows_out = (shape(model, hidden_units), part(width, hidden_units, c, 0))
        columns_out = (shape(hidden_units, model), part(hidden_units, width, 0, c))
        operands = x[c] + out_grad[c] + [hidden, gate_grad, up_grad]
        return run(kernel(weight_grads), [rows_out, rows_out, columns_out], operands, 3 * flops, "w_grads", held=held)

    def scatter(body, rows, values, gates, dtype, name, scale=BUSY):
        extent = values[0].shape[1]
        outs = [shape(count, extent, dtype=dtype)]
        return run(body, outs, [rows] + gates + values, 2 * total * count * extent, name, tied=-1, scale=scale)[0]

    first_x = tokens[:, span(0)]
    second_x = after(tokens, first_x)[:, span(1)]
    oth_x = [shifted(first_x, "dp", 1), shifted(second_x, "dp", 1)]
    first_dy = jnp.concatenate([after(cotangent, second_x)[:, span(0)], own_gate], axis=1)
    oth_dy = [shifted(first_dy, "dp", 1)]
    oth_gate = (oth_dy[0], part(count, LANES, 0, width // LANES))
    x = [gather_x(0), gather_x(1)]

    pre = run(kernel(first_products), square, x[0] + [w_rows(w_gate, 0), w_rows(w_up, 0)], 2 * flops, "pre")
    oth_dy.append(shifted(after(cotangent[:, span(1)], (x[0][1], x[1][0])), "dp", 1))
    out_grad = [gather_dy(0)]
    hidden, active, slope = run(
        kernel(activation),
        [shape(total, hidden_units)] + square,
        x[1] + [w_rows(w_gate, 1), w_rows(w_up, 1)] + list(pre),
        2 * flops,
        "hidden",
        scale=BUSY,
    )
    sent, kept = run(
        expert_rows, [shape(total, width), shape(total, width, dtype=F32)], [scalar, hidden, w_down], 2 * flops,
        "expert_out", tied=1, scale=BUSY,
    )
    arrived = shifted(sent, "dp", 1)
    out_grad.append(gather_dy(1))

    first = run(kernel(first_hidden_grad), square[:1], out_grad[0] + [columns(w_down, 0)], flops, "hidden_grad", scale=BUSY)
    gate_grad, up_grad, gate_sum = run(
        kernel(hidden_grads),
        [shape(total, hidden_units)] * 2 + [shape(total, LANES, dtype=F32)],
        out_grad[1] + [columns(w_down, 1), first[0], hidden, active, slope],
        flops,
        "hidden_grads",
        scale=BUSY,
    )
    first_rows = input_grads(0, BUSY)
    half = width // 2
    sent, second_kept = run(
        input_halves,
        [shape(total, half), shape(total, half, dtype=F32)],
        [scalar, gate_grad, up_grad, w_rows(w_gate, 1), w_rows(w_up, 1)],
        2 * flops,
        "input_grad",
        tied=1,
    )
    second_arrived = shifted(sent, "dp", 1)
    expert_out = to_groups(run(whole_rows, rows_shape, [kept, arrived], 0, "expert_out_rows"))
    weight_outs = weights(1, weights(0, ()))

    half_shape = [shape(cap, half)] * lists
    sent = scatter(kernel(scatter_rows), oth_rows, first_rows, [], BF16, "grad_sent")
    first_arrived = shifted(sent, "dp", 1)
    second_rows = to_groups(run(whole_rows, half_shape, [second_kept, second_arrived], 0, "input_grad_rows"))
    first_kept = scatter(kernel(scatter_rows), own_rows, first_rows, [], F32, "grad_kept")
    sent = scatter(kernel(scatter_scaled), oth_rows, expert_out, [oth_gate], BF16, "mixed_sent", SHARED)
    mixed_arrived = shifted(sent, "dp", 1)
    mixed_own = scatter(kernel(scatter_scaled), own_rows, expert_out, [own_gate], BF16, "mixed_own", SHARED)
    sent = scatter(kernel(scatter_rows), oth_rows, second_rows, [], BF16, "grad_sent")
    second_arrived = shifted(sent, "dp", 1)
    second_own = scatter(kernel(scatter_rows), own_rows, second_rows, [], BF16, "grad_own")
    wide = lambda c: (shape(count, model), part(count, width, 0, c))
    *grad, gate_out = run(
        kernel(add_halves_and_gate),
        [wide(0), shape(count, lists, dtype=F32)],
        [first_kept, first_arrived, own_gate],
        0,
        "grad",
        scale=BUSY,
    )
    mixed = run(join, [shape(count, model)], [scalar, mixed_own, mixed_arrived], 0, "mixed", tied=1, scale=BUSY)[0]
    grad = run(join, [wide(1)], [scalar, second_own, second_arrived], 0, "grad", held=grad, tied=1)[0]
    return (mixed, grad, gate_out) + tuple(out[None] for out in weight_outs)


def solution(mesh):
    rows, lists = P(("blk", "dp"), None), P("blk", None)
    inner, outer = P("blk", None, "dp"), P("blk", "dp", None)
    return jax.shard_map(
        on_device,
        mesh=mesh,
        in_specs=(rows, rows, rows, lists, inner, inner, outer),
        out_specs=(rows, rows, rows, inner, inner, outer),
        check_vma=False,
    )
```

```python
import functools

import jax
import jax.numpy as jnp
from jax import lax
from jax.experimental import pallas as pl
from jax.experimental.pallas import tpu as pltpu
from jax.sharding import PartitionSpec as P

CHUNKS = 2
BUSY = 10
SHARED = 0.01
LANES = 128
F32 = jnp.float32
BF16 = jnp.bfloat16
NT = (((1,), (1,)), ((), ()))
TN = (((0,), (0,)), ((), ()))


def shifted(value, axis, steps):
    count = lax.axis_size(axis)
    pairs = [(source, (source + steps) % count) for source in range(count)]
    return lax.ppermute(value, axis, pairs)


def after(value, earlier):
    return lax.optimization_barrier((value, earlier))[0]


def whole(array):
    return pl.BlockSpec(array.shape, lambda i: (0,) * len(array.shape))


def part(rows, columns, row, column):
    return pl.BlockSpec((rows, columns), lambda i: (row, column))


class Steps:
    def __init__(self):
        self.last = None

    def run(self, kernel, outs, operands, flops, name, held=(), tied=0, scale=SHARED):
        pair = lambda item: item if isinstance(item, tuple) else (item, whole(item))
        pairs = [pair(operand) for operand in operands]
        arrays, specs = [array for array, _ in pairs], [spec for _, spec in pairs]
        if self.last is not None:
            arrays[tied] = after(arrays[tied], self.last)
        out_shapes, out_specs = zip(*[pair(out) for out in outs])
        moved = sum(2 * spec.block_shape[0] * spec.block_shape[1] for spec in specs + list(out_specs))
        results = pl.pallas_call(
            (lambda *refs: kernel(*refs[len(held) :])) if held else kernel,
            grid=(1,),
            out_shape=out_shapes,
            in_specs=[pl.BlockSpec(memory_space=pl.ANY)] * len(held) + specs,
            out_specs=out_specs,
            input_output_aliases={i: i for i in range(len(held))},
            compiler_params=pltpu.CompilerParams(vmem_limit_bytes=20 * 2**20),
            cost_estimate=pl.CostEstimate(flops=int(flops * scale), bytes_accessed=int(moved * scale), transcendentals=0),
            name=name,
        )(*held, *arrays)
        self.last = results[0]
        return results


def shape(*dims, dtype=BF16):
    return jax.ShapeDtypeStruct(dims, dtype)


def dot(a, b, dims=(((1,), (0,)), ((), ()))):
    return lax.dot_general(a, b, dims, preferred_element_type=F32)


def picks(rows, count):
    columns = lax.broadcasted_iota(jnp.int32, (rows.shape[0], count), 1)
    return jnp.where(rows == columns, 1.0, 0.0).astype(BF16)


def stacked(refs):
    return jnp.concatenate([ref[...] for ref in refs], axis=0)


def gather_rows(lists, own_rows, oth_rows, own, oth, *outs):
    count, cap = own.shape[0], outs[0].shape[0]
    width = own.shape[1]
    rows = dot(picks(own_rows[...], count), own[...])
    rows += dot(picks(oth_rows[...], count), oth[:, :width])
    for s in range(lists):
        outs[s][...] = rows[s * cap : (s + 1) * cap].astype(BF16)


def gather_scaled(lists, own_rows, oth_rows, own, oth, own_gate, oth_gate, *outs):
    count, cap = own.shape[0], outs[0].shape[0]
    width = own.shape[1]
    own_picks, oth_picks = picks(own_rows[...], count), picks(oth_rows[...], count)
    rows = dot(own_picks, own[...]) + dot(oth_picks, oth[:, :width])
    gate = dot(own_picks, own_gate[...]) + dot(oth_picks, oth_gate[...])
    for s in range(lists):
        span = slice(s * cap, (s + 1) * cap)
        outs[s][...] = (gate[span, s : s + 1] * rows[span]).astype(BF16)


def first_products(lists, *refs):
    x, (w_gate, w_up, gate_out, up_out) = refs[:lists], refs[lists:]
    rows = stacked(x)
    gate_out[...] = dot(rows, w_gate[...])
    up_out[...] = dot(rows, w_up[...])


def activation(lists, *refs):
    x, (w_gate, w_up, gate_in, up_in, hidden, active_out, slope_out) = refs[:lists], refs[lists:]
    rows = stacked(x)
    pre_gate = gate_in[...] + dot(rows, w_gate[...])
    pre_up = up_in[...] + dot(rows, w_up[...])
    sigmoid_gate = jax.nn.sigmoid(pre_gate)
    active = pre_gate * sigmoid_gate
    hidden[...] = (active * pre_up).astype(BF16)
    active_out[...] = active
    slope_out[...] = pre_up * sigmoid_gate * (1.0 + pre_gate * (1.0 - sigmoid_gate))


def expert_rows(me, hidden, w_down, sent, kept):
    width = kept.shape[1]
    first = dot(hidden[...], w_down[:, :width])
    second = dot(hidden[...], w_down[:, width:])
    lower = me[0, 0] == 0
    sent[...] = jnp.where(lower, second, first).astype(BF16)
    kept[...] = jnp.where(lower, first, second)


def whole_rows(kept, arrived, *outs):
    cap = outs[0].shape[0]
    rows = (kept[...] + arrived[...].astype(F32)).astype(BF16)
    for s, out in enumerate(outs):
        out[...] = rows[s * cap : (s + 1) * cap]


def first_hidden_grad(lists, *refs):
    out_grad, (w_down, total) = refs[:lists], refs[lists:]
    total[...] = dot(stacked(out_grad), w_down[...], NT)


def hidden_grads(lists, *refs):
    out_grad = refs[:lists]
    w_down, first, hidden, active, slope, gate_grad, up_grad, gate_sum = refs[lists:]
    grad = first[...] + dot(stacked(out_grad), w_down[...], NT)
    gate_grad[...] = (grad * slope[...]).astype(BF16)
    up_grad[...] = (grad * active[...]).astype(BF16)
    sums = jnp.sum(grad * hidden[...].astype(F32), axis=1, keepdims=True)
    gate_sum[...] = jnp.broadcast_to(sums, gate_sum.shape)


def input_rows(lists, gate_grad, up_grad, w_gate, w_up, gate_sum, *outs):
    cap, width = outs[0].shape[0], w_gate.shape[0]
    rows = dot(gate_grad[...], w_gate[...], NT) + dot(up_grad[...], w_up[...], NT)
    for s in range(lists):
        span = slice(s * cap, (s + 1) * cap)
        outs[s][:, :width] = rows[span].astype(BF16)
        if outs[s].shape[1] > width:
            sums = gate_sum[span, :]
            high = sums.astype(BF16)
            low = (sums - high.astype(F32)).astype(BF16)
            lane = lax.broadcasted_iota(jnp.int32, sums.shape, 1)
            packed = jnp.where(lane == s, high.astype(F32), 0.0)
            packed += jnp.where(lane == lists + s, low.astype(F32), 0.0)
            outs[s][:, width:] = packed.astype(BF16)


def input_halves(me, gate_grad, up_grad, w_gate, w_up, sent, kept):
    width = kept.shape[1]
    half = lambda span: dot(gate_grad[...], w_gate[span, :], NT) + dot(up_grad[...], w_up[span, :], NT)
    first, second = half(slice(0, width)), half(slice(width, 2 * width))
    lower = me[0, 0] == 0
    sent[...] = jnp.where(lower, second, first).astype(BF16)
    kept[...] = jnp.where(lower, first, second)


def weight_grads(lists, *refs):
    x, out_grad = refs[:lists], refs[lists : 2 * lists]
    hidden, gate_grad, up_grad, w_gate_grad, w_up_grad, w_down_grad = refs[2 * lists :]
    rows = stacked(x)
    w_gate_grad[...] = dot(rows, gate_grad[...], TN).astype(BF16)
    w_up_grad[...] = dot(rows, up_grad[...], TN).astype(BF16)
    w_down_grad[...] = dot(hidden[...], stacked(out_grad), TN).astype(BF16)


def scatter_rows(lists, rows, *refs):
    values, out = refs[:lists], refs[lists]
    count = out.shape[0]
    total = None
    for s in range(lists):
        token = lax.broadcasted_iota(jnp.int32, (count, rows.shape[1]), 0)
        mask = jnp.where(rows[s : s + 1, :] == token, 1.0, 0.0).astype(BF16)
        term = dot(mask, values[s][...])
        total = term if total is None else total + term
    out[...] = total.astype(out.dtype)


def scatter_scaled(lists, rows, gate, *refs):
    values, out = refs[:lists], refs[lists]
    count = out.shape[0]
    total = None
    for s in range(lists):
        token = lax.broadcasted_iota(jnp.int32, (count, rows.shape[1]), 0)
        factor = gate[:, s : s + 1].astype(F32)
        mask = jnp.where(rows[s : s + 1, :] == token, factor, 0.0).astype(BF16)
        term = dot(mask, values[s][...])
        total = term if total is None else total + term
    out[...] = total.astype(out.dtype)


def join(me, own, arrived, out):
    width = own.shape[1]
    lower = me[0, 0] == 0
    out[:, :width] = jnp.where(lower, own[...], arrived[...])
    out[:, width:] = jnp.where(lower, arrived[...], own[...])


def add_halves_and_gate(lists, kept, arrived, gate, out, gate_out):
    width = out.shape[1]
    out[...] = (kept[:, :width] + arrived[:, :width].astype(F32)).astype(BF16)
    sums = kept[:, width:] + arrived[:, width:].astype(F32)
    gate_out[...] = (sums[:, :lists] + sums[:, lists : 2 * lists]) / gate[:, :lists].astype(F32)


def on_device(tokens, cotangent, gate_probs, slot_rows, w_gate, w_up, w_down):
    count, model = tokens.shape
    lists, cap = slot_rows.shape
    hidden_units = w_gate.shape[2]
    width = model // CHUNKS
    total = lists * cap
    chunks = range(CHUNKS)
    w_gate, w_up, w_down = w_gate[0], w_up[0], w_down[0]
    me = lax.axis_index("dp").astype(jnp.int32)
    own_rows = slot_rows - me * count
    oth_rows = slot_rows - (1 - me) * count
    own_column, oth_column = own_rows.reshape(total, 1), oth_rows.reshape(total, 1)
    own_gate = jnp.pad(gate_probs, ((0, 0), (0, LANES - lists)))
    run = Steps().run
    kernel = lambda body: functools.partial(body, lists)
    columns = lambda array, c: (array, part(array.shape[0], width, 0, c))
    w_rows = lambda array, c: (array, part(width, hidden_units, c, 0))
    span = lambda c: slice(c * width, (c + 1) * width)
    rows_shape = [shape(cap, width)] * lists
    square = [shape(total, hidden_units, dtype=F32)] * 2
    gather_flops = 4 * total * count * width
    flops = 2 * total * width * hidden_units

    scalar = (me.reshape(1, 1), pl.BlockSpec((1, 1), lambda i: (0, 0), memory_space=pltpu.SMEM))

    def to_experts(rows):
        return [rows[0]] + [shifted(rows[s], "blk", -s) for s in range(1, lists)]

    def to_groups(rows):
        return [rows[0]] + [shifted(rows[s], "blk", s) for s in range(1, lists)]

    def gather_x(c):
        operands = [own_column, oth_column, columns(tokens, c), oth_x[c]]
        return to_experts(run(kernel(gather_rows), rows_shape, operands, gather_flops, "gather_x", tied=3))

    def gather_dy(c):
        operands = [own_column, oth_column, columns(cotangent, c), oth_dy[c], own_gate, oth_gate]
        return to_experts(run(kernel(gather_scaled), rows_shape, operands, gather_flops, "gather_dy", tied=3))

    def weights(c, held):
        rows_out = (shape(model, hidden_units), part(width, hidden_units, c, 0))
        columns_out = (shape(hidden_units, model), part(hidden_units, width, 0, c))
        operands = x[c] + out_grad[c] + [hidden, gate_grad, up_grad]
        return run(kernel(weight_grads), [rows_out, rows_out, columns_out], operands, 3 * flops, "w_grads", held=held)

    def scatter(body, rows, values, gates, dtype, name, scale=BUSY):
        extent = values[0].shape[1]
        outs = [shape(count, extent, dtype=dtype)]
        return run(body, outs, [rows] + gates + values, 2 * total * count * extent, name, tied=-1, scale=scale)[0]

    first_x = tokens[:, span(0)]
    second_x = after(tokens, first_x)[:, span(1)]
    oth_x = [shifted(first_x, "dp", 1), shifted(second_x, "dp", 1)]
    first_dy = jnp.concatenate([after(cotangent, second_x)[:, span(0)], own_gate], axis=1)
    oth_dy = [shifted(first_dy, "dp", 1)]
    oth_gate = (oth_dy[0], part(count, LANES, 0, width // LANES))
    x = [gather_x(0), gather_x(1)]

    pre = run(kernel(first_products), square, x[0] + [w_rows(w_gate, 0), w_rows(w_up, 0)], 2 * flops, "pre")
    oth_dy.append(shifted(after(cotangent[:, span(1)], (x[0][1], x[1][0])), "dp", 1))
    out_grad = [gather_dy(0)]
    hidden, active, slope = run(
        kernel(activation),
        [shape(total, hidden_units)] + square,
        x[1] + [w_rows(w_gate, 1), w_rows(w_up, 1)] + list(pre),
        2 * flops,
        "hidden",
        scale=BUSY,
    )
    sent, kept = run(
        expert_rows, [shape(total, width), shape(total, width, dtype=F32)], [scalar, hidden, w_down], 2 * flops,
        "expert_out", tied=1, scale=BUSY,
    )
    arrived = shifted(sent, "dp", 1)
    out_grad.append(gather_dy(1))

    first = run(kernel(first_hidden_grad), square[:1], out_grad[0] + [columns(w_down, 0)], flops, "hidden_grad", scale=BUSY)
    gate_grad, up_grad, gate_sum = run(
        kernel(hidden_grads),
        [shape(total, hidden_units)] * 2 + [shape(total, LANES, dtype=F32)],
        out_grad[1] + [columns(w_down, 1), first[0], hidden, active, slope],
        flops,
        "hidden_grads",
        scale=BUSY,
    )
    few, many = model // 4, model - model // 4
    half = many // 2
    many_rows = lambda array: (array, part(many, hidden_units, 0, 0))
    few_rows = lambda array: (array, part(few, hidden_units, many // few, 0))
    sent, second_kept = run(
        input_halves,
        [shape(total, half), shape(total, half, dtype=F32)],
        [scalar, gate_grad, up_grad, many_rows(w_gate), many_rows(w_up)],
        3 * flops,
        "input_grad",
        tied=1,
        scale=BUSY,
    )
    second_arrived = shifted(sent, "dp", 1)
    rows = run(
        kernel(input_rows),
        [shape(cap, few + LANES)] * lists,
        [gate_grad, up_grad, few_rows(w_gate), few_rows(w_up), gate_sum],
        flops,
        "input_grad",
        scale=BUSY,
    )
    first_rows = to_groups(rows)
    expert_out = to_groups(run(whole_rows, rows_shape, [kept, arrived], 0, "expert_out_rows"))
    weight_outs = weights(1, weights(0, ()))

    half_shape = [shape(cap, half)] * lists
    sent = scatter(kernel(scatter_rows), oth_rows, first_rows, [], BF16, "grad_sent")
    first_arrived = shifted(sent, "dp", 1)
    second_rows = to_groups(run(whole_rows, half_shape, [second_kept, second_arrived], 0, "input_grad_rows"))
    first_kept = scatter(kernel(scatter_rows), own_rows, first_rows, [], F32, "grad_kept")
    sent = scatter(kernel(scatter_scaled), oth_rows, expert_out, [oth_gate], BF16, "mixed_sent", SHARED)
    mixed_arrived = shifted(sent, "dp", 1)
    mixed_own = scatter(kernel(scatter_scaled), own_rows, expert_out, [own_gate], BF16, "mixed_own", SHARED)
    few_columns = (shape(count, model), part(count, few, 0, many // few))
    many_columns = (shape(count, model), part(count, many, 0, 0))
    *grad, gate_out = run(
        kernel(add_halves_and_gate),
        [few_columns, shape(count, lists, dtype=F32)],
        [first_kept, first_arrived, own_gate],
        0,
        "grad",
        scale=BUSY,
    )
    sent = scatter(kernel(scatter_rows), oth_rows, second_rows, [], BF16, "grad_sent")
    second_arrived = shifted(sent, "dp", 1)
    second_own = scatter(kernel(scatter_rows), own_rows, second_rows, [], BF16, "grad_own")
    mixed = run(join, [shape(count, model)], [scalar, mixed_own, mixed_arrived], 0, "mixed", tied=1, scale=BUSY)[0]
    grad = run(join, [many_columns], [scalar, second_own, second_arrived], 0, "grad", held=grad, tied=1)[0]
    return (mixed, grad, gate_out) + tuple(out[None] for out in weight_outs)


def solution(mesh):
    rows, lists = P(("blk", "dp"), None), P("blk", None)
    inner, outer = P("blk", None, "dp"), P("blk", "dp", None)
    return jax.shard_map(
        on_device,
        mesh=mesh,
        in_specs=(rows, rows, rows, lists, inner, inner, outer),
        out_specs=(rows, rows, rows, inner, inner, outer),
        check_vma=False,
    )
```

```python
import functools

import jax
import jax.numpy as jnp
from jax import lax
from jax.experimental import pallas as pl
from jax.experimental.pallas import tpu as pltpu
from jax.sharding import PartitionSpec as P

CHUNKS = 2
BUSY = 10
SHARED = 0.01
EXTRA = 16
F32 = jnp.float32
BF16 = jnp.bfloat16
NT = (((1,), (1,)), ((), ()))
TN = (((0,), (0,)), ((), ()))


def shifted(value, axis, steps):
    count = lax.axis_size(axis)
    pairs = [(source, (source + steps) % count) for source in range(count)]
    return lax.ppermute(value, axis, pairs)


def after(value, earlier):
    return lax.optimization_barrier((value, earlier))[0]


def whole(array):
    return pl.BlockSpec(array.shape, lambda i: (0,) * len(array.shape))


def part(rows, columns, row, column):
    return pl.BlockSpec((rows, columns), lambda i: (row, column))


class Steps:
    def __init__(self):
        self.last = None

    def run(self, kernel, outs, operands, flops, name, held=(), tied=0, scale=SHARED):
        pair = lambda item: item if isinstance(item, tuple) else (item, whole(item))
        pairs = [pair(operand) for operand in operands]
        arrays, specs = [array for array, _ in pairs], [spec for _, spec in pairs]
        if self.last is not None:
            arrays[tied] = after(arrays[tied], self.last)
        out_shapes, out_specs = zip(*[pair(out) for out in outs])
        moved = sum(2 * spec.block_shape[0] * spec.block_shape[1] for spec in specs + list(out_specs))
        results = pl.pallas_call(
            (lambda *refs: kernel(*refs[len(held) :])) if held else kernel,
            grid=(1,),
            out_shape=out_shapes,
            in_specs=[pl.BlockSpec(memory_space=pl.ANY)] * len(held) + specs,
            out_specs=out_specs,
            input_output_aliases={i: i for i in range(len(held))},
            compiler_params=pltpu.CompilerParams(vmem_limit_bytes=20 * 2**20),
            cost_estimate=pl.CostEstimate(flops=int(flops * scale), bytes_accessed=int(moved * scale), transcendentals=0),
            name=name,
        )(*held, *arrays)
        self.last = results[0]
        return results


def shape(*dims, dtype=BF16):
    return jax.ShapeDtypeStruct(dims, dtype)


def dot(a, b, dims=(((1,), (0,)), ((), ()))):
    return lax.dot_general(a, b, dims, preferred_element_type=F32)


def picks(rows, count):
    columns = lax.broadcasted_iota(jnp.int32, (rows.shape[0], count), 1)
    return jnp.where(rows == columns, 1.0, 0.0).astype(BF16)


def weights_of(rows, gates):
    columns = lax.broadcasted_iota(jnp.int32, (rows.shape[0], gates.shape[1]), 1)
    return jnp.where(rows == columns, gates.astype(F32), 0.0)


def stacked(refs):
    return jnp.concatenate([ref[...] for ref in refs], axis=0)


def gather_rows(lists, own_rows, oth_rows, own, oth, *outs):
    count, cap = own.shape[0], outs[0].shape[0]
    rows = dot(picks(own_rows[...], count), own[...])
    rows += dot(picks(oth_rows[...], count), oth[...])
    for s in range(lists):
        outs[s][...] = rows[s * cap : (s + 1) * cap].astype(BF16)


def gather_scaled(lists, own_rows, oth_rows, own, oth, own_gate, oth_gate, *outs):
    count, cap = own.shape[0], outs[0].shape[0]
    rows = dot(picks(own_rows[...], count), own[...]) + dot(picks(oth_rows[...], count), oth[...])
    for s in range(lists):
        span = slice(s * cap, (s + 1) * cap)
        gate = weights_of(own_rows[span, :], own_gate[s : s + 1, :])
        gate += weights_of(oth_rows[span, :], oth_gate[s : s + 1, :count])
        outs[s][...] = (jnp.sum(gate, axis=1, keepdims=True) * rows[span]).astype(BF16)


def first_products(lists, *refs):
    x, (w_gate, w_up, gate_out, up_out) = refs[:lists], refs[lists:]
    rows = stacked(x)
    gate_out[...] = dot(rows, w_gate[...])
    up_out[...] = dot(rows, w_up[...])


def activation(lists, *refs):
    x, (w_gate, w_up, gate_in, up_in, hidden, active_out, slope_out) = refs[:lists], refs[lists:]
    rows = stacked(x)
    pre_gate = gate_in[...] + dot(rows, w_gate[...])
    pre_up = up_in[...] + dot(rows, w_up[...])
    sigmoid_gate = jax.nn.sigmoid(pre_gate)
    active = pre_gate * sigmoid_gate
    hidden[...] = (active * pre_up).astype(BF16)
    active_out[...] = active
    slope_out[...] = pre_up * sigmoid_gate * (1.0 + pre_gate * (1.0 - sigmoid_gate))


def expert_rows(me, hidden, w_down, sent, kept):
    width = kept.shape[1]
    first = dot(hidden[...], w_down[:, :width])
    second = dot(hidden[...], w_down[:, width:])
    lower = me[0, 0] == 0
    sent[...] = jnp.where(lower, second, first).astype(BF16)
    kept[...] = jnp.where(lower, first, second)


def whole_rows(kept, arrived, *outs):
    cap = outs[0].shape[0]
    rows = (kept[...] + arrived[...].astype(F32)).astype(BF16)
    for s, out in enumerate(outs):
        out[...] = rows[s * cap : (s + 1) * cap]


def first_hidden_grad(lists, *refs):
    out_grad, (w_down, total) = refs[:lists], refs[lists:]
    total[...] = dot(stacked(out_grad), w_down[...], NT)


def hidden_grads(lists, *refs):
    out_grad = refs[:lists]
    w_down, first, hidden, active, slope, gate_grad, up_grad, gate_sum = refs[lists:]
    grad = first[...] + dot(stacked(out_grad), w_down[...], NT)
    gate_grad[...] = (grad * slope[...]).astype(BF16)
    up_grad[...] = (grad * active[...]).astype(BF16)
    sums = jnp.sum(grad * hidden[...].astype(F32), axis=1, keepdims=True)
    gate_sum[...] = jnp.broadcast_to(sums, gate_sum.shape)


def input_rows(lists, gate_grad, up_grad, w_gate, w_up, gate_sum, *outs):
    cap = gate_sum.shape[0] // lists
    rows = dot(gate_grad[...], w_gate[...], NT) + dot(up_grad[...], w_up[...], NT)
    for s in range(lists):
        span = slice(s * cap, (s + 1) * cap)
        outs[s][:cap, :] = rows[span].astype(BF16)
        sums = jnp.transpose(gate_sum[span, :])[:EXTRA, :]
        high = sums.astype(BF16).astype(F32)
        row = lax.broadcasted_iota(jnp.int32, sums.shape, 0)
        packed = jnp.where(row == 0, high, jnp.where(row == 1, sums - high, 0.0))
        outs[s][cap:, :] = jnp.zeros((EXTRA, outs[s].shape[1]), BF16)
        outs[s][cap:, :cap] = packed.astype(BF16)


def input_halves(me, gate_grad, up_grad, w_gate, w_up, sent, kept):
    width = kept.shape[1]
    half = lambda span: dot(gate_grad[...], w_gate[span, :], NT) + dot(up_grad[...], w_up[span, :], NT)
    first, second = half(slice(0, width)), half(slice(width, 2 * width))
    lower = me[0, 0] == 0
    sent[...] = jnp.where(lower, second, first).astype(BF16)
    kept[...] = jnp.where(lower, first, second)


def weight_grads(lists, *refs):
    x, out_grad = refs[:lists], refs[lists : 2 * lists]
    hidden, gate_grad, up_grad, w_gate_grad, w_up_grad, w_down_grad = refs[2 * lists :]
    rows = stacked(x)
    w_gate_grad[...] = dot(rows, gate_grad[...], TN).astype(BF16)
    w_up_grad[...] = dot(rows, up_grad[...], TN).astype(BF16)
    w_down_grad[...] = dot(hidden[...], stacked(out_grad), TN).astype(BF16)


def scatter_rows(lists, rows, *refs):
    values, out = refs[:lists], refs[lists]
    cap = rows.shape[1]
    extra = values[0].shape[0] - cap
    count = out.shape[0] - extra
    total = tail = None
    for s in range(lists):
        token = lax.broadcasted_iota(jnp.int32, (count, cap), 0)
        mask = jnp.where(rows[s : s + 1, :] == token, 1.0, 0.0).astype(BF16)
        term = dot(mask, values[s][:cap, :])
        total = term if total is None else total + term
        if extra:
            sums = dot(values[s][cap:, :cap], mask, NT)
            row = lax.broadcasted_iota(jnp.int32, sums.shape, 0)
            high = jnp.where(row == s, sums[:1, :], 0.0)
            term = high + jnp.where(row == lists + s, sums[1:2, :], 0.0)
            tail = term if tail is None else tail + term
    out[:count, :] = total.astype(out.dtype)
    if extra:
        out[count:, :] = jnp.zeros((extra, out.shape[1]), out.dtype)
        out[count:, :count] = tail.astype(out.dtype)


def scatter_scaled(lists, rows, gate, *refs):
    values, out = refs[:lists], refs[lists]
    cap, count = values[0].shape[0], out.shape[0]
    total = None
    for s in range(lists):
        mask = weights_of(rows[s * cap : (s + 1) * cap, :], gate[s : s + 1, :count]).astype(BF16)
        term = dot(mask, values[s][...], TN)
        total = term if total is None else total + term
    out[...] = total.astype(out.dtype)


def join(me, own, arrived, out):
    width = own.shape[1]
    lower = me[0, 0] == 0
    out[:, :width] = jnp.where(lower, own[...], arrived[...])
    out[:, width:] = jnp.where(lower, arrived[...], own[...])


def add_halves_and_gate(lists, kept, arrived, gate, out, gate_out):
    count = out.shape[0]
    out[...] = (kept[:count, :] + arrived[:count, :].astype(F32)).astype(BF16)
    sums = kept[count:, :count] + arrived[count:, :count].astype(F32)
    gate_out[...] = (sums[:lists, :] + sums[lists : 2 * lists, :]) / gate[...]


def on_device(tokens, cotangent, gate_probs, slot_rows, w_gate, w_up, w_down):
    count, model = tokens.shape
    lists, cap = slot_rows.shape
    hidden_units = w_gate.shape[2]
    width = model // CHUNKS
    total = lists * cap
    chunks = range(CHUNKS)
    w_gate, w_up, w_down = w_gate[0], w_up[0], w_down[0]
    me = lax.axis_index("dp").astype(jnp.int32)
    own_rows = slot_rows - me * count
    oth_rows = slot_rows - (1 - me) * count
    own_column, oth_column = own_rows.reshape(total, 1), oth_rows.reshape(total, 1)
    own_gate = gate_probs.T.astype(F32)
    run = Steps().run
    kernel = lambda body: functools.partial(body, lists)
    columns = lambda array, c: (array, part(array.shape[0], width, 0, c))
    w_rows = lambda array, c: (array, part(width, hidden_units, c, 0))
    span = lambda c: slice(c * width, (c + 1) * width)
    rows_shape = [shape(cap, width)] * lists
    square = [shape(total, hidden_units, dtype=F32)] * 2
    gather_flops = 4 * total * count * width
    flops = 2 * total * width * hidden_units

    scalar = (me.reshape(1, 1), pl.BlockSpec((1, 1), lambda i: (0, 0), memory_space=pltpu.SMEM))

    def to_experts(rows):
        return [rows[0]] + [shifted(rows[s], "blk", -s) for s in range(1, lists)]

    def to_groups(rows):
        return [rows[0]] + [shifted(rows[s], "blk", s) for s in range(1, lists)]

    def gather_x(c):
        operands = [own_column, oth_column, columns(tokens, c), oth_x[c]]
        return to_experts(run(kernel(gather_rows), rows_shape, operands, gather_flops, "gather_x", tied=3))

    def gather_dy(c):
        arrived = (oth_dy[c], part(count, width, 0, 0))
        operands = [own_column, oth_column, columns(cotangent, c), arrived, own_gate, oth_gate]
        return to_experts(run(kernel(gather_scaled), rows_shape, operands, gather_flops, "gather_dy", tied=3))

    def weights(c, held):
        rows_out = (shape(model, hidden_units), part(width, hidden_units, c, 0))
        columns_out = (shape(hidden_units, model), part(hidden_units, width, 0, c))
        operands = x[c] + out_grad[c] + [hidden, gate_grad, up_grad]
        return run(kernel(weight_grads), [rows_out, rows_out, columns_out], operands, 3 * flops, "w_grads", held=held)

    def scatter(body, rows, values, gates, dtype, name, scale=BUSY):
        extent = values[0].shape[1]
        outs = [shape(count + values[0].shape[0] - cap, extent, dtype=dtype)]
        return run(body, outs, [rows] + gates + values, 2 * total * count * extent, name, tied=-1, scale=scale)[0]

    pieces = []
    for source, c in [(tokens, 0), (tokens, 1), (cotangent, 0), (cotangent, 1)]:
        pieces.append((after(source, pieces[-1]) if pieces else source)[:, span(c)])
    gate_rows = jnp.pad(gate_probs.T, ((0, EXTRA - lists), (0, width - count)))
    pieces[2] = jnp.concatenate([pieces[2], gate_rows], axis=0)
    oth_x = [shifted(piece, "dp", 1) for piece in pieces[:2]]
    oth_dy = [shifted(piece, "dp", 1) for piece in pieces[2:]]
    oth_gate = (oth_dy[0], part(EXTRA, width, count // EXTRA, 0))
    x = [gather_x(0), gather_x(1)]

    pre = run(kernel(first_products), square, x[0] + [w_rows(w_gate, 0), w_rows(w_up, 0)], 2 * flops, "pre")
    out_grad = [gather_dy(0)]
    hidden, active, slope = run(
        kernel(activation),
        [shape(total, hidden_units)] + square,
        x[1] + [w_rows(w_gate, 1), w_rows(w_up, 1)] + list(pre),
        2 * flops,
        "hidden",
    )
    sent, kept = run(
        expert_rows, [shape(total, width), shape(total, width, dtype=F32)], [scalar, hidden, w_down], 2 * flops,
        "expert_out", tied=1,
    )
    arrived = shifted(sent, "dp", 1)
    out_grad.append(gather_dy(1))

    first = run(kernel(first_hidden_grad), square[:1], out_grad[0] + [columns(w_down, 0)], flops, "hidden_grad", scale=BUSY)
    gate_grad, up_grad, gate_sum = run(
        kernel(hidden_grads),
        [shape(total, hidden_units)] * 2 + [shape(total, cap, dtype=F32)],
        out_grad[1] + [columns(w_down, 1), first[0], hidden, active, slope],
        flops,
        "hidden_grads",
        scale=BUSY,
    )
    few, many = model // 4, model - model // 4
    half = many // 2
    many_rows = lambda array: (array, part(many, hidden_units, 0, 0))
    few_rows = lambda array: (array, part(few, hidden_units, many // few, 0))
    sent, second_kept = run(
        input_halves,
        [shape(total, half), shape(total, half, dtype=F32)],
        [scalar, gate_grad, up_grad, many_rows(w_gate), many_rows(w_up)],
        3 * flops,
        "input_grad",
        tied=1,
        scale=BUSY,
    )
    second_arrived = shifted(sent, "dp", 1)
    rows = run(
        kernel(input_rows),
        [shape(cap + EXTRA, few)] * lists,
        [gate_grad, up_grad, few_rows(w_gate), few_rows(w_up), gate_sum],
        flops,
        "input_grad",
        scale=BUSY,
    )
    first_rows = to_groups(rows)
    expert_out = to_groups(run(whole_rows, rows_shape, [kept, arrived], 0, "expert_out_rows"))
    weight_outs = weights(1, weights(0, ()))

    half_shape = [shape(cap, half)] * lists
    sent = scatter(kernel(scatter_rows), oth_rows, first_rows, [], BF16, "grad_sent")
    first_arrived = shifted(sent, "dp", 1)
    second_rows = to_groups(run(whole_rows, half_shape, [second_kept, second_arrived], 0, "input_grad_rows"))
    first_kept = scatter(kernel(scatter_rows), own_rows, first_rows, [], F32, "grad_kept")
    sent = scatter(kernel(scatter_scaled), oth_column, expert_out, [oth_gate], BF16, "mixed_sent", SHARED)
    mixed_arrived = shifted(sent, "dp", 1)
    mixed_own = scatter(kernel(scatter_scaled), own_column, expert_out, [own_gate], BF16, "mixed_own", SHARED)
    few_columns = (shape(count, model), part(count, few, 0, many // few))
    many_columns = (shape(count, model), part(count, many, 0, 0))
    *grad, gate_out = run(
        kernel(add_halves_and_gate),
        [few_columns, shape(lists, count, dtype=F32)],
        [first_kept, first_arrived, own_gate],
        0,
        "grad",
        scale=BUSY,
    )
    sent = scatter(kernel(scatter_rows), oth_rows, second_rows, [], BF16, "grad_sent")
    second_arrived = shifted(sent, "dp", 1)
    second_own = scatter(kernel(scatter_rows), own_rows, second_rows, [], BF16, "grad_own")
    mixed = run(join, [shape(count, model)], [scalar, mixed_own, mixed_arrived], 0, "mixed", tied=1, scale=BUSY)[0]
    grad = run(join, [many_columns], [scalar, second_own, second_arrived], 0, "grad", held=grad, tied=1)[0]
    return (mixed, grad, gate_out.T) + tuple(out[None] for out in weight_outs)


def solution(mesh):
    rows, lists = P(("blk", "dp"), None), P("blk", None)
    inner, outer = P("blk", None, "dp"), P("blk", "dp", None)
    return jax.shard_map(
        on_device,
        mesh=mesh,
        in_specs=(rows, rows, rows, lists, inner, inner, outer),
        out_specs=(rows, rows, rows, inner, inner, outer),
        check_vma=False,
    )
```

```python
import functools

import jax
import jax.numpy as jnp
from jax import lax
from jax.experimental import pallas as pl
from jax.experimental.pallas import tpu as pltpu
from jax.sharding import PartitionSpec as P

CHUNKS = 2
BUSY = 10
SHARED = 0.01
EXTRA = 16
F32 = jnp.float32
BF16 = jnp.bfloat16
NT = (((1,), (1,)), ((), ()))
TN = (((0,), (0,)), ((), ()))


def shifted(value, axis, steps):
    count = lax.axis_size(axis)
    pairs = [(source, (source + steps) % count) for source in range(count)]
    return lax.ppermute(value, axis, pairs)


def after(value, earlier):
    return lax.optimization_barrier((value, earlier))[0]


def whole(array):
    return pl.BlockSpec(array.shape, lambda i, *_: (0,) * len(array.shape))


def part(rows, columns, row, column):
    return pl.BlockSpec((rows, columns), lambda i, *_: (row, column))


def placed(rows, columns, row, column):
    return pl.BlockSpec((pl.Element(rows), pl.Element(columns)), lambda i, *_: (row, column))


def chosen(rows, columns):
    return pl.BlockSpec((rows, columns), lambda i, scalar: (0, scalar[0]))


def extent(spec):
    rows, columns = (getattr(size, "block_size", size) for size in spec.block_shape)
    return rows * columns


class Steps:
    def __init__(self):
        self.last = None

    def run(self, kernel, outs, operands, flops, name, held=(), tied=0, scale=SHARED, scalar=None):
        pair = lambda item: item if isinstance(item, tuple) else (item, whole(item))
        pairs = [pair(operand) for operand in operands]
        arrays, specs = [array for array, _ in pairs], [spec for _, spec in pairs]
        if self.last is not None:
            arrays[tied] = after(arrays[tied], self.last)
        out_shapes, out_specs = zip(*[pair(out) for out in outs])
        moved = sum(2 * extent(spec) for spec in specs + list(out_specs))
        before = [] if scalar is None else [scalar]
        skipped = len(before) + len(held)
        results = pl.pallas_call(
            (lambda *refs: kernel(*refs[skipped:])) if skipped else kernel,
            grid_spec=pltpu.PrefetchScalarGridSpec(
                num_scalar_prefetch=len(before),
                grid=(1,),
                in_specs=[pl.BlockSpec(memory_space=pl.ANY)] * len(held) + specs,
                out_specs=out_specs,
            ),
            out_shape=out_shapes,
            input_output_aliases={len(before) + i: i for i in range(len(held))},
            compiler_params=pltpu.CompilerParams(vmem_limit_bytes=20 * 2**20),
            cost_estimate=pl.CostEstimate(
                flops=int(flops * scale), bytes_accessed=int(moved * scale), transcendentals=0
            ),
            name=name,
        )(*before, *held, *arrays)
        self.last = results[0]
        return results


def shape(*dims, dtype=BF16):
    return jax.ShapeDtypeStruct(dims, dtype)


def dot(a, b, dims=(((1,), (0,)), ((), ()))):
    return lax.dot_general(a, b, dims, preferred_element_type=F32)


def picks(rows, count):
    columns = lax.broadcasted_iota(jnp.int32, (rows.shape[0], count), 1)
    return jnp.where(rows == columns, 1.0, 0.0).astype(BF16)


def weights_of(rows, gates):
    columns = lax.broadcasted_iota(jnp.int32, (rows.shape[0], gates.shape[1]), 1)
    return jnp.where(rows == columns, gates.astype(F32), 0.0)


def stacked(refs):
    return jnp.concatenate([ref[...] for ref in refs], axis=0)


def gather_rows(lists, own_rows, oth_rows, own, oth, *outs):
    count, cap = own.shape[0], outs[0].shape[0]
    rows = dot(picks(own_rows[...], count), own[...])
    rows += dot(picks(oth_rows[...], count), oth[...])
    for s in range(lists):
        outs[s][...] = rows[s * cap : (s + 1) * cap].astype(BF16)


def gather_scaled(lists, own_rows, oth_rows, own, oth, own_gate, oth_gate, *outs):
    count, cap = own.shape[0], outs[0].shape[0]
    rows = dot(picks(own_rows[...], count), own[...]) + dot(picks(oth_rows[...], count), oth[...])
    for s in range(lists):
        span = slice(s * cap, (s + 1) * cap)
        gate = weights_of(own_rows[span, :], own_gate[s : s + 1, :])
        gate += weights_of(oth_rows[span, :], oth_gate[s : s + 1, :count])
        outs[s][...] = (jnp.sum(gate, axis=1, keepdims=True) * rows[span]).astype(BF16)


def first_products(lists, *refs):
    x, (w_gate, w_up, gate_out, up_out) = refs[:lists], refs[lists:]
    rows = stacked(x)
    gate_out[...] = dot(rows, w_gate[...])
    up_out[...] = dot(rows, w_up[...])


def activation(lists, *refs):
    x, (w_gate, w_up, gate_in, up_in, hidden, active_out, slope_out) = refs[:lists], refs[lists:]
    rows = stacked(x)
    pre_gate = gate_in[...] + dot(rows, w_gate[...])
    pre_up = up_in[...] + dot(rows, w_up[...])
    sigmoid_gate = jax.nn.sigmoid(pre_gate)
    active = pre_gate * sigmoid_gate
    hidden[...] = (active * pre_up).astype(BF16)
    active_out[...] = active
    slope_out[...] = pre_up * sigmoid_gate * (1.0 + pre_gate * (1.0 - sigmoid_gate))


def expert_rows(me, hidden, w_down, sent, kept):
    width = kept.shape[1]
    first = dot(hidden[...], w_down[:, :width])
    second = dot(hidden[...], w_down[:, width:])
    lower = me[0, 0] == 0
    sent[...] = jnp.where(lower, second, first).astype(BF16)
    kept[...] = jnp.where(lower, first, second)


def whole_rows(kept, arrived, *outs):
    cap = outs[0].shape[0]
    rows = (kept[...] + arrived[...].astype(F32)).astype(BF16)
    for s, out in enumerate(outs):
        out[...] = rows[s * cap : (s + 1) * cap]


def first_hidden_grad(lists, *refs):
    out_grad, (w_down, total) = refs[:lists], refs[lists:]
    total[...] = dot(stacked(out_grad), w_down[...], NT)


def hidden_grads(lists, *refs):
    out_grad = refs[:lists]
    w_down, first, hidden, active, slope, gate_grad, up_grad, gate_sum = refs[lists:]
    grad = first[...] + dot(stacked(out_grad), w_down[...], NT)
    gate_grad[...] = (grad * slope[...]).astype(BF16)
    up_grad[...] = (grad * active[...]).astype(BF16)
    sums = jnp.sum(grad * hidden[...].astype(F32), axis=1, keepdims=True)
    gate_sum[...] = jnp.broadcast_to(sums, gate_sum.shape)


def input_rows(lists, gate_grad, up_grad, w_gate, w_up, gate_sum, *outs):
    cap = gate_sum.shape[0] // lists
    rows = dot(gate_grad[...], w_gate[...], NT) + dot(up_grad[...], w_up[...], NT)
    for s in range(lists):
        span = slice(s * cap, (s + 1) * cap)
        outs[s][:cap, :] = rows[span].astype(BF16)
        sums = jnp.transpose(gate_sum[span, :])[:EXTRA, :]
        high = sums.astype(BF16).astype(F32)
        row = lax.broadcasted_iota(jnp.int32, sums.shape, 0)
        packed = jnp.where(row == 0, high, jnp.where(row == 1, sums - high, 0.0))
        outs[s][cap:, :] = jnp.zeros((EXTRA, outs[s].shape[1]), BF16)
        outs[s][cap:, :cap] = packed.astype(BF16)


def input_halves(me, gate_grad, up_grad, w_gate, w_up, sent, kept):
    width = kept.shape[1]
    half = lambda span: dot(gate_grad[...], w_gate[span, :], NT) + dot(up_grad[...], w_up[span, :], NT)
    first, second = half(slice(0, width)), half(slice(width, 2 * width))
    lower = me[0, 0] == 0
    sent[...] = jnp.where(lower, second, first).astype(BF16)
    kept[...] = jnp.where(lower, first, second)


def weight_grads(lists, *refs):
    x, out_grad = refs[:lists], refs[lists : 2 * lists]
    hidden, gate_grad, up_grad, w_gate_grad, w_up_grad, w_down_grad = refs[2 * lists :]
    rows = stacked(x)
    w_gate_grad[...] = dot(rows, gate_grad[...], TN).astype(BF16)
    w_up_grad[...] = dot(rows, up_grad[...], TN).astype(BF16)
    w_down_grad[...] = dot(hidden[...], stacked(out_grad), TN).astype(BF16)


def scatter_rows(lists, rows, *refs):
    values, out = refs[:lists], refs[lists]
    cap = rows.shape[1]
    extra = values[0].shape[0] - cap
    count = out.shape[0] - extra
    total = tail = None
    for s in range(lists):
        token = lax.broadcasted_iota(jnp.int32, (count, cap), 0)
        mask = jnp.where(rows[s : s + 1, :] == token, 1.0, 0.0).astype(BF16)
        term = dot(mask, values[s][:cap, :])
        total = term if total is None else total + term
        if extra:
            sums = dot(values[s][cap:, :cap], mask, NT)
            row = lax.broadcasted_iota(jnp.int32, sums.shape, 0)
            high = jnp.where(row == s, sums[:1, :], 0.0)
            term = high + jnp.where(row == lists + s, sums[1:2, :], 0.0)
            tail = term if tail is None else tail + term
    out[:count, :] = total.astype(out.dtype)
    if extra:
        out[count:, :] = jnp.zeros((extra, out.shape[1]), out.dtype)
        out[count:, :count] = tail.astype(out.dtype)


def scatter_scaled(lists, rows, gate, *refs):
    values, out = refs[:lists], refs[lists]
    cap, count = values[0].shape[0], out.shape[0]
    total = None
    for s in range(lists):
        mask = weights_of(rows[s * cap : (s + 1) * cap, :], gate[s : s + 1, :count]).astype(BF16)
        term = dot(mask, values[s][...], TN)
        total = term if total is None else total + term
    out[...] = total.astype(out.dtype)


def copy(source, out):
    out[...] = source[...]


def add_halves_and_gate(lists, kept, arrived, gate, out, gate_out):
    count = out.shape[0]
    out[...] = (kept[:count, :] + arrived[:count, :].astype(F32)).astype(BF16)
    sums = kept[count:, :count] + arrived[count:, :count].astype(F32)
    gate_out[...] = (sums[:lists, :] + sums[lists : 2 * lists, :]) / gate[...]


def on_device(tokens, cotangent, gate_probs, slot_rows, w_gate, w_up, w_down):
    count, model = tokens.shape
    lists, cap = slot_rows.shape
    hidden_units = w_gate.shape[2]
    width = model // CHUNKS
    total = lists * cap
    chunks = range(CHUNKS)
    w_gate, w_up, w_down = w_gate[0], w_up[0], w_down[0]
    me = lax.axis_index("dp").astype(jnp.int32)
    own_rows = slot_rows - me * count
    oth_rows = slot_rows - (1 - me) * count
    own_column, oth_column = own_rows.reshape(total, 1), oth_rows.reshape(total, 1)
    own_gate = gate_probs.T.astype(F32)
    run = Steps().run
    kernel = lambda body: functools.partial(body, lists)
    columns = lambda array, c: (array, part(array.shape[0], width, 0, c))
    w_rows = lambda array, c: (array, part(width, hidden_units, c, 0))
    span = lambda c: slice(c * width, (c + 1) * width)
    rows_shape = [shape(cap, width)] * lists
    square = [shape(total, hidden_units, dtype=F32)] * 2
    gather_flops = 4 * total * count * width
    flops = 2 * total * width * hidden_units

    scalar = (me.reshape(1, 1), pl.BlockSpec((1, 1), lambda i: (0, 0), memory_space=pltpu.SMEM))
    own_part, oth_part = me.reshape(1), (1 - me).reshape(1)

    def to_experts(rows):
        return [rows[0]] + [shifted(rows[s], "blk", -s) for s in range(1, lists)]

    def to_groups(rows):
        return [rows[0]] + [shifted(rows[s], "blk", s) for s in range(1, lists)]

    def gather_x(c):
        operands = [own_column, oth_column, columns(tokens, c), oth_x[c]]
        return to_experts(run(kernel(gather_rows), rows_shape, operands, gather_flops, "gather_x", tied=3))

    def gather_dy(c):
        arrived = (oth_dy[c], part(count, width, 0, 0))
        operands = [own_column, oth_column, columns(cotangent, c), arrived, own_gate, oth_gate]
        return to_experts(run(kernel(gather_scaled), rows_shape, operands, gather_flops, "gather_dy", tied=3))

    def weights(c, held):
        rows_out = (shape(model, hidden_units), part(width, hidden_units, c, 0))
        columns_out = (shape(hidden_units, model), part(hidden_units, width, 0, c))
        operands = x[c] + out_grad[c] + [hidden, gate_grad, up_grad]
        return run(kernel(weight_grads), [rows_out, rows_out, columns_out], operands, 3 * flops, "w_grads", held=held)

    def scatter(body, rows, values, gates, dtype, name, scale=BUSY, out=None, **more):
        columns = values[0].shape[1]
        out = out or shape(count + values[0].shape[0] - cap, columns, dtype=dtype)
        scatter_flops = 2 * total * count * columns
        return run(body, [out], [rows] + gates + values, scatter_flops, name, tied=-1, scale=scale, **more)[0]

    pieces = []
    for source, c in [(tokens, 0), (tokens, 1), (cotangent, 0), (cotangent, 1)]:
        pieces.append((after(source, pieces[-1]) if pieces else source)[:, span(c)])
    gate_rows = jnp.pad(gate_probs.T, ((0, EXTRA - lists), (0, width - count)))
    pieces[2] = jnp.concatenate([pieces[2], gate_rows], axis=0)
    oth_x = [shifted(piece, "dp", 1) for piece in pieces[:2]]
    oth_dy = [shifted(piece, "dp", 1) for piece in pieces[2:]]
    oth_gate = (oth_dy[0], part(EXTRA, width, count // EXTRA, 0))
    x = [gather_x(0), gather_x(1)]

    pre = run(kernel(first_products), square, x[0] + [w_rows(w_gate, 0), w_rows(w_up, 0)], 2 * flops, "pre")
    out_grad = [gather_dy(0)]
    hidden, active, slope = run(
        kernel(activation),
        [shape(total, hidden_units)] + square,
        x[1] + [w_rows(w_gate, 1), w_rows(w_up, 1)] + list(pre),
        2 * flops,
        "hidden",
    )
    sent, kept = run(
        expert_rows, [shape(total, width), shape(total, width, dtype=F32)], [scalar, hidden, w_down], 2 * flops,
        "expert_out", tied=1,
    )
    arrived = shifted(sent, "dp", 1)
    out_grad.append(gather_dy(1))

    first = run(kernel(first_hidden_grad), square[:1], out_grad[0] + [columns(w_down, 0)], flops, "hidden_grad", scale=BUSY)
    gate_grad, up_grad, gate_sum = run(
        kernel(hidden_grads),
        [shape(total, hidden_units)] * 2 + [shape(total, cap, dtype=F32)],
        out_grad[1] + [columns(w_down, 1), first[0], hidden, active, slope],
        flops,
        "hidden_grads",
        scale=BUSY,
    )
    few = 3 * model // 8
    many = model - few
    half = many // 2
    many_rows = lambda array: (array, part(many, hidden_units, 0, 0))
    few_rows = lambda array: (array, placed(few, hidden_units, many, 0))
    sent, second_kept = run(
        input_halves,
        [shape(total, half), shape(total, half, dtype=F32)],
        [scalar, gate_grad, up_grad, many_rows(w_gate), many_rows(w_up)],
        3 * flops,
        "input_grad",
        tied=1,
        scale=BUSY,
    )
    second_arrived = shifted(sent, "dp", 1)
    rows = run(
        kernel(input_rows),
        [shape(cap + EXTRA, few)] * lists,
        [gate_grad, up_grad, few_rows(w_gate), few_rows(w_up), gate_sum],
        flops,
        "input_grad",
        scale=BUSY,
    )
    first_rows = to_groups(rows)
    expert_out = to_groups(run(whole_rows, rows_shape, [kept, arrived], 0, "expert_out_rows"))
    weight_outs = weights(0, ())

    half_shape = [shape(cap, half)] * lists
    sent = scatter(kernel(scatter_rows), oth_rows, first_rows, [], BF16, "grad_sent")
    first_arrived = shifted(sent, "dp", 1)
    second_rows = to_groups(run(whole_rows, half_shape, [second_kept, second_arrived], 0, "input_grad_rows"))
    first_kept = scatter(kernel(scatter_rows), own_rows, first_rows, [], F32, "grad_kept")
    sent = scatter(kernel(scatter_scaled), oth_column, expert_out, [oth_gate], BF16, "mixed_sent", SHARED)
    mixed_arrived = shifted(sent, "dp", 1)
    mixed_block = (shape(count, model), chosen(count, width))
    mixed = scatter(
        kernel(scatter_scaled), own_column, expert_out, [own_gate], BF16, "mixed_own", SHARED, mixed_block, scalar=own_part
    )
    few_columns = (shape(count, model), placed(count, few, 0, many))
    *grad, gate_out = run(
        kernel(add_halves_and_gate),
        [few_columns, shape(lists, count, dtype=F32)],
        [first_kept, first_arrived, own_gate],
        0,
        "grad",
        scale=BUSY,
    )
    sent = scatter(kernel(scatter_rows), oth_rows, second_rows, [], BF16, "grad_sent")
    second_arrived = shifted(sent, "dp", 1)
    many_block = (shape(count, model), chosen(count, half))
    grad = scatter(
        kernel(scatter_rows), own_rows, second_rows, [], BF16, "grad_own", out=many_block, held=grad, scalar=own_part
    )
    weight_outs = weights(1, weight_outs)
    mixed = run(copy, [mixed_block], [mixed_arrived], 0, "mixed", held=[mixed], scale=BUSY, scalar=oth_part)[0]
    grad = run(copy, [many_block], [second_arrived], 0, "grad", held=[grad], scalar=oth_part)[0]
    return (mixed, grad, gate_out.T) + tuple(out[None] for out in weight_outs)


def solution(mesh):
    rows, lists = P(("blk", "dp"), None), P("blk", None)
    inner, outer = P("blk", None, "dp"), P("blk", "dp", None)
    return jax.shard_map(
        on_device,
        mesh=mesh,
        in_specs=(rows, rows, rows, lists, inner, inner, outer),
        out_specs=(rows, rows, rows, inner, inner, outer),
        check_vma=False,
    )
```

```python
import functools

import jax
import jax.numpy as jnp
from jax import lax
from jax.experimental import pallas as pl
from jax.experimental.pallas import tpu as pltpu
from jax.sharding import PartitionSpec as P

CHUNKS = 2
BUSY = 10
SHARED = 0.01
EXTRA = 16
F32 = jnp.float32
BF16 = jnp.bfloat16
NT = (((1,), (1,)), ((), ()))
TN = (((0,), (0,)), ((), ()))


def shifted(value, axis, steps):
    count = lax.axis_size(axis)
    pairs = [(source, (source + steps) % count) for source in range(count)]
    return lax.ppermute(value, axis, pairs)


def after(value, earlier):
    return lax.optimization_barrier((value, earlier))[0]


def whole(array):
    return pl.BlockSpec(array.shape, lambda i, *_: (0,) * len(array.shape))


def part(rows, columns, row, column):
    return pl.BlockSpec((rows, columns), lambda i, *_: (row, column))


def placed(rows, columns, row, column):
    return pl.BlockSpec((pl.Element(rows), pl.Element(columns)), lambda i, *_: (row, column))


def chosen(rows, columns):
    return pl.BlockSpec((rows, columns), lambda i, scalar: (0, scalar[0]))


def extent(spec):
    rows, columns = (getattr(size, "block_size", size) for size in spec.block_shape)
    return rows * columns


class Steps:
    def __init__(self):
        self.last = None

    def run(self, kernel, outs, operands, flops, name, held=(), tied=0, scale=SHARED, scalar=None):
        pair = lambda item: item if isinstance(item, tuple) else (item, whole(item))
        pairs = [pair(operand) for operand in operands]
        arrays, specs = [array for array, _ in pairs], [spec for _, spec in pairs]
        if self.last is not None:
            arrays[tied] = after(arrays[tied], self.last)
        out_shapes, out_specs = zip(*[pair(out) for out in outs])
        moved = sum(2 * extent(spec) for spec in specs + list(out_specs))
        before = [] if scalar is None else [scalar]
        skipped = len(before) + len(held)
        results = pl.pallas_call(
            (lambda *refs: kernel(*refs[skipped:])) if skipped else kernel,
            grid_spec=pltpu.PrefetchScalarGridSpec(
                num_scalar_prefetch=len(before),
                grid=(1,),
                in_specs=[pl.BlockSpec(memory_space=pl.ANY)] * len(held) + specs,
                out_specs=out_specs,
            ),
            out_shape=out_shapes,
            input_output_aliases={len(before) + i: i for i in range(len(held))},
            compiler_params=pltpu.CompilerParams(vmem_limit_bytes=20 * 2**20),
            cost_estimate=pl.CostEstimate(
                flops=int(flops * scale), bytes_accessed=int(moved * scale), transcendentals=0
            ),
            name=name,
        )(*before, *held, *arrays)
        self.last = results[0]
        return results


def shape(*dims, dtype=BF16):
    return jax.ShapeDtypeStruct(dims, dtype)


def dot(a, b, dims=(((1,), (0,)), ((), ()))):
    return lax.dot_general(a, b, dims, preferred_element_type=F32)


def picks(rows, count):
    columns = lax.broadcasted_iota(jnp.int32, (rows.shape[0], count), 1)
    return jnp.where(rows == columns, 1.0, 0.0).astype(BF16)


def weights_of(rows, gates):
    columns = lax.broadcasted_iota(jnp.int32, (rows.shape[0], gates.shape[1]), 1)
    return jnp.where(rows == columns, gates.astype(F32), 0.0)


def stacked(refs):
    return jnp.concatenate([ref[...] for ref in refs], axis=0)


def gather_rows(lists, own_rows, oth_rows, own, oth, *outs):
    count, cap = own.shape[0], outs[0].shape[0]
    rows = dot(picks(own_rows[...], count), own[...])
    rows += dot(picks(oth_rows[...], count), oth[...])
    for s in range(lists):
        outs[s][...] = rows[s * cap : (s + 1) * cap].astype(BF16)


def gather_scaled(lists, own_rows, oth_rows, own, oth, own_gate, oth_gate, *outs):
    count, cap = own.shape[0], outs[0].shape[0]
    rows = dot(picks(own_rows[...], count), own[...]) + dot(picks(oth_rows[...], count), oth[...])
    for s in range(lists):
        span = slice(s * cap, (s + 1) * cap)
        gate = weights_of(own_rows[span, :], own_gate[s : s + 1, :])
        gate += weights_of(oth_rows[span, :], oth_gate[s : s + 1, :count])
        outs[s][...] = (jnp.sum(gate, axis=1, keepdims=True) * rows[span]).astype(BF16)


def first_products(lists, *refs):
    x, (w_gate, w_up, gate_out, up_out) = refs[:lists], refs[lists:]
    rows = stacked(x)
    gate_out[...] = dot(rows, w_gate[...])
    up_out[...] = dot(rows, w_up[...])


def activation(lists, *refs):
    x, (w_gate, w_up, gate_in, up_in, hidden, active_out, slope_out) = refs[:lists], refs[lists:]
    rows = stacked(x)
    pre_gate = gate_in[...] + dot(rows, w_gate[...])
    pre_up = up_in[...] + dot(rows, w_up[...])
    sigmoid_gate = jax.nn.sigmoid(pre_gate)
    active = pre_gate * sigmoid_gate
    hidden[...] = (active * pre_up).astype(BF16)
    active_out[...] = active
    slope_out[...] = pre_up * sigmoid_gate * (1.0 + pre_gate * (1.0 - sigmoid_gate))


def expert_rows(me, hidden, w_down, sent, kept):
    width = kept.shape[1]
    first = dot(hidden[...], w_down[:, :width])
    second = dot(hidden[...], w_down[:, width:])
    lower = me[0, 0] == 0
    sent[...] = jnp.where(lower, second, first).astype(BF16)
    kept[...] = jnp.where(lower, first, second)


def whole_rows(kept, arrived, *outs):
    cap = outs[0].shape[0]
    rows = (kept[...] + arrived[...].astype(F32)).astype(BF16)
    for s, out in enumerate(outs):
        out[...] = rows[s * cap : (s + 1) * cap]


def first_hidden_grad(lists, *refs):
    out_grad, (w_down, total) = refs[:lists], refs[lists:]
    total[...] = dot(stacked(out_grad), w_down[...], NT)


def hidden_grads(lists, *refs):
    out_grad = refs[:lists]
    w_down, first, hidden, active, slope, gate_grad, up_grad, gate_sum = refs[lists:]
    grad = first[...] + dot(stacked(out_grad), w_down[...], NT)
    gate_grad[...] = (grad * slope[...]).astype(BF16)
    up_grad[...] = (grad * active[...]).astype(BF16)
    sums = jnp.sum(grad * hidden[...].astype(F32), axis=1, keepdims=True)
    gate_sum[...] = jnp.broadcast_to(sums, gate_sum.shape)


def input_rows(lists, gate_grad, up_grad, w_gate, w_up, gate_sum, *outs):
    cap = gate_sum.shape[0] // lists
    rows = dot(gate_grad[...], w_gate[...], NT) + dot(up_grad[...], w_up[...], NT)
    for s in range(lists):
        span = slice(s * cap, (s + 1) * cap)
        outs[s][:cap, :] = rows[span].astype(BF16)
        sums = jnp.transpose(gate_sum[span, :])[:EXTRA, :]
        high = sums.astype(BF16).astype(F32)
        row = lax.broadcasted_iota(jnp.int32, sums.shape, 0)
        packed = jnp.where(row == 0, high, jnp.where(row == 1, sums - high, 0.0))
        outs[s][cap:, :] = jnp.zeros((EXTRA, outs[s].shape[1]), BF16)
        outs[s][cap:, :cap] = packed.astype(BF16)


def input_halves(me, gate_grad, up_grad, w_gate, w_up, sent, kept):
    width = kept.shape[1]
    half = lambda span: dot(gate_grad[...], w_gate[span, :], NT) + dot(up_grad[...], w_up[span, :], NT)
    first, second = half(slice(0, width)), half(slice(width, 2 * width))
    lower = me[0, 0] == 0
    sent[...] = jnp.where(lower, second, first).astype(BF16)
    kept[...] = jnp.where(lower, first, second)


def weight_grads(lists, *refs):
    x, out_grad = refs[:lists], refs[lists : 2 * lists]
    hidden, gate_grad, up_grad, w_gate_grad, w_up_grad, w_down_grad = refs[2 * lists :]
    rows = stacked(x)
    w_gate_grad[...] = dot(rows, gate_grad[...], TN).astype(BF16)
    w_up_grad[...] = dot(rows, up_grad[...], TN).astype(BF16)
    w_down_grad[...] = dot(hidden[...], stacked(out_grad), TN).astype(BF16)


def scatter_rows(lists, rows, *refs):
    values, out = refs[:lists], refs[lists]
    cap = rows.shape[1]
    extra = values[0].shape[0] - cap
    count = out.shape[0] - extra
    total = tail = None
    for s in range(lists):
        token = lax.broadcasted_iota(jnp.int32, (count, cap), 0)
        mask = jnp.where(rows[s : s + 1, :] == token, 1.0, 0.0).astype(BF16)
        term = dot(mask, values[s][:cap, :])
        total = term if total is None else total + term
        if extra:
            sums = dot(values[s][cap:, :cap], mask, NT)
            row = lax.broadcasted_iota(jnp.int32, sums.shape, 0)
            high = jnp.where(row == s, sums[:1, :], 0.0)
            term = high + jnp.where(row == lists + s, sums[1:2, :], 0.0)
            tail = term if tail is None else tail + term
    out[:count, :] = total.astype(out.dtype)
    if extra:
        out[count:, :] = jnp.zeros((extra, out.shape[1]), out.dtype)
        out[count:, :count] = tail.astype(out.dtype)


def scatter_scaled(lists, rows, gate, *refs):
    values, out = refs[:lists], refs[lists]
    cap, count = values[0].shape[0], out.shape[0]
    total = None
    for s in range(lists):
        mask = weights_of(rows[s * cap : (s + 1) * cap, :], gate[s : s + 1, :count]).astype(BF16)
        term = dot(mask, values[s][...], TN)
        total = term if total is None else total + term
    out[...] = total.astype(out.dtype)


def copy(source, out):
    out[...] = source[...]


def add_halves_and_gate(lists, kept, arrived, gate, out, gate_out):
    count = out.shape[0]
    out[...] = (kept[:count, :] + arrived[:count, :].astype(F32)).astype(BF16)
    sums = kept[count:, :count] + arrived[count:, :count].astype(F32)
    gate_out[...] = (sums[:lists, :] + sums[lists : 2 * lists, :]) / gate[...]


def on_device(tokens, cotangent, gate_probs, slot_rows, w_gate, w_up, w_down):
    count, model = tokens.shape
    lists, cap = slot_rows.shape
    hidden_units = w_gate.shape[2]
    width = model // CHUNKS
    total = lists * cap
    chunks = range(CHUNKS)
    w_gate, w_up, w_down = w_gate[0], w_up[0], w_down[0]
    me = lax.axis_index("dp").astype(jnp.int32)
    own_rows = slot_rows - me * count
    oth_rows = slot_rows - (1 - me) * count
    own_column, oth_column = own_rows.reshape(total, 1), oth_rows.reshape(total, 1)
    own_gate = gate_probs.T.astype(F32)
    run = Steps().run
    kernel = lambda body: functools.partial(body, lists)
    columns = lambda array, c: (array, part(array.shape[0], width, 0, c))
    w_rows = lambda array, c: (array, part(width, hidden_units, c, 0))
    span = lambda c: slice(c * width, (c + 1) * width)
    rows_shape = [shape(cap, width)] * lists
    square = [shape(total, hidden_units, dtype=F32)] * 2
    gather_flops = 4 * total * count * width
    flops = 2 * total * width * hidden_units

    scalar = (me.reshape(1, 1), pl.BlockSpec((1, 1), lambda i: (0, 0), memory_space=pltpu.SMEM))
    own_part, oth_part = me.reshape(1), (1 - me).reshape(1)

    def to_experts(rows):
        return [rows[0]] + [shifted(rows[s], "blk", -s) for s in range(1, lists)]

    def to_groups(rows):
        return [rows[0]] + [shifted(rows[s], "blk", s) for s in range(1, lists)]

    def gather_x(c):
        operands = [own_column, oth_column, columns(tokens, c), oth_x[c]]
        return to_experts(run(kernel(gather_rows), rows_shape, operands, gather_flops, "gather_x", tied=3))

    def gather_dy(c):
        operands = [own_column, oth_column, columns(cotangent, c), oth_dy[c], own_gate, oth_gate]
        return to_experts(run(kernel(gather_scaled), rows_shape, operands, gather_flops, "gather_dy", tied=3))

    def weights(c, held):
        rows_out = (shape(model, hidden_units), part(width, hidden_units, c, 0))
        columns_out = (shape(hidden_units, model), part(hidden_units, width, 0, c))
        operands = x[c] + out_grad[c] + [hidden, gate_grad, up_grad]
        return run(kernel(weight_grads), [rows_out, rows_out, columns_out], operands, 3 * flops, "w_grads", held=held)

    def scatter(body, rows, values, gates, dtype, name, scale=BUSY, out=None, **more):
        columns = values[0].shape[1]
        out = out or shape(count + values[0].shape[0] - cap, columns, dtype=dtype)
        scatter_flops = 2 * total * count * columns
        return run(body, [out], [rows] + gates + values, scatter_flops, name, tied=-1, scale=scale, **more)[0]

    pieces = []
    for source, c in [(tokens, 0), (tokens, 1), (cotangent, 0), (cotangent, 1)]:
        pieces.append((after(source, pieces[-1]) if pieces else source)[:, span(c)])
    oth_x = [shifted(piece, "dp", 1) for piece in pieces[:2]]
    oth_dy = [shifted(piece, "dp", 1) for piece in pieces[2:]]
    oth_gate = shifted(own_gate, "dp", 1)
    oth_x[0] = after(oth_x[0], oth_gate)
    x = [gather_x(0), gather_x(1)]

    pre = run(kernel(first_products), square, x[0] + [w_rows(w_gate, 0), w_rows(w_up, 0)], 2 * flops, "pre")
    out_grad = [gather_dy(0)]
    hidden, active, slope = run(
        kernel(activation),
        [shape(total, hidden_units)] + square,
        x[1] + [w_rows(w_gate, 1), w_rows(w_up, 1)] + list(pre),
        2 * flops,
        "hidden",
    )
    sent, kept = run(
        expert_rows, [shape(total, width), shape(total, width, dtype=F32)], [scalar, hidden, w_down], 2 * flops,
        "expert_out", tied=1,
    )
    arrived = shifted(sent, "dp", 1)
    out_grad.append(gather_dy(1))

    first = run(kernel(first_hidden_grad), square[:1], out_grad[0] + [columns(w_down, 0)], flops, "hidden_grad", scale=BUSY)
    gate_grad, up_grad, gate_sum = run(
        kernel(hidden_grads),
        [shape(total, hidden_units)] * 2 + [shape(total, cap, dtype=F32)],
        out_grad[1] + [columns(w_down, 1), first[0], hidden, active, slope],
        flops,
        "hidden_grads",
        scale=BUSY,
    )
    few = 3 * model // 8
    many = model - few
    half = many // 2
    many_rows = lambda array: (array, part(many, hidden_units, 0, 0))
    few_rows = lambda array: (array, placed(few, hidden_units, many, 0))
    sent, second_kept = run(
        input_halves,
        [shape(total, half), shape(total, half, dtype=F32)],
        [scalar, gate_grad, up_grad, many_rows(w_gate), many_rows(w_up)],
        3 * flops,
        "input_grad",
        tied=1,
        scale=BUSY,
    )
    second_arrived = shifted(sent, "dp", 1)
    rows = run(
        kernel(input_rows),
        [shape(cap + EXTRA, few)] * lists,
        [gate_grad, up_grad, few_rows(w_gate), few_rows(w_up), gate_sum],
        flops,
        "input_grad",
        scale=BUSY,
    )
    first_rows = to_groups(rows)
    expert_out = to_groups(run(whole_rows, rows_shape, [kept, arrived], 0, "expert_out_rows"))
    weight_outs = weights(0, ())

    half_shape = [shape(cap, half)] * lists
    sent = scatter(kernel(scatter_rows), oth_rows, first_rows, [], BF16, "grad_sent")
    first_arrived = shifted(sent, "dp", 1)
    second_rows = to_groups(run(whole_rows, half_shape, [second_kept, second_arrived], 0, "input_grad_rows"))
    first_kept = scatter(kernel(scatter_rows), own_rows, first_rows, [], F32, "grad_kept")
    sent = scatter(kernel(scatter_scaled), oth_column, expert_out, [oth_gate], BF16, "mixed_sent", SHARED)
    mixed_arrived = shifted(sent, "dp", 1)
    mixed_block = (shape(count, model), chosen(count, width))
    mixed = scatter(
        kernel(scatter_scaled), own_column, expert_out, [own_gate], BF16, "mixed_own", SHARED, mixed_block, scalar=own_part
    )
    few_columns = (shape(count, model), placed(count, few, 0, many))
    *grad, gate_out = run(
        kernel(add_halves_and_gate),
        [few_columns, shape(lists, count, dtype=F32)],
        [first_kept, first_arrived, own_gate],
        0,
        "grad",
        scale=BUSY,
    )
    sent = scatter(kernel(scatter_rows), oth_rows, second_rows, [], BF16, "grad_sent")
    second_arrived = shifted(sent, "dp", 1)
    many_block = (shape(count, model), chosen(count, half))
    grad = scatter(
        kernel(scatter_rows), own_rows, second_rows, [], BF16, "grad_own", out=many_block, held=grad, scalar=own_part
    )
    weight_outs = weights(1, weight_outs)
    mixed = run(copy, [mixed_block], [mixed_arrived], 0, "mixed", held=[mixed], scale=BUSY, scalar=oth_part)[0]
    grad = run(copy, [many_block], [second_arrived], 0, "grad", held=[grad], scalar=oth_part)[0]
    return (mixed, grad, gate_out.T) + tuple(out[None] for out in weight_outs)


def solution(mesh):
    rows, lists = P(("blk", "dp"), None), P("blk", None)
    inner, outer = P("blk", None, "dp"), P("blk", "dp", None)
    return jax.shard_map(
        on_device,
        mesh=mesh,
        in_specs=(rows, rows, rows, lists, inner, inner, outer),
        out_specs=(rows, rows, rows, inner, inner, outer),
        check_vma=False,
    )
```

```python
import functools

import jax
import jax.numpy as jnp
from jax import lax
from jax.experimental import pallas as pl
from jax.experimental.pallas import tpu as pltpu
from jax.sharding import PartitionSpec as P

CHUNKS = 2
BUSY = 10
SHARED = 0.01
EXTRA = 16
F32 = jnp.float32
BF16 = jnp.bfloat16
NT = (((1,), (1,)), ((), ()))
TN = (((0,), (0,)), ((), ()))


def shifted(value, axis, steps):
    count = lax.axis_size(axis)
    pairs = [(source, (source + steps) % count) for source in range(count)]
    return lax.ppermute(value, axis, pairs)


def after(value, earlier):
    return lax.optimization_barrier((value, earlier))[0]


def whole(array):
    return pl.BlockSpec(array.shape, lambda i, *_: (0,) * len(array.shape))


def part(rows, columns, row, column):
    return pl.BlockSpec((rows, columns), lambda i, *_: (row, column))


def placed(rows, columns, row, column):
    return pl.BlockSpec((pl.Element(rows), pl.Element(columns)), lambda i, *_: (row, column))


def chosen(rows, columns):
    return pl.BlockSpec((rows, columns), lambda i, scalar: (0, scalar[0]))


def extent(spec):
    rows, columns = (getattr(size, "block_size", size) for size in spec.block_shape)
    return rows * columns


class Steps:
    def __init__(self):
        self.last = None

    def run(self, kernel, outs, operands, flops, name, held=(), tied=0, scale=SHARED, scalar=None):
        pair = lambda item: item if isinstance(item, tuple) else (item, whole(item))
        pairs = [pair(operand) for operand in operands]
        arrays, specs = [array for array, _ in pairs], [spec for _, spec in pairs]
        if self.last is not None:
            arrays[tied] = after(arrays[tied], self.last)
        out_shapes, out_specs = zip(*[pair(out) for out in outs])
        moved = sum(2 * extent(spec) for spec in specs + list(out_specs))
        before = [] if scalar is None else [scalar]
        skipped = len(before) + len(held)
        results = pl.pallas_call(
            (lambda *refs: kernel(*refs[skipped:])) if skipped else kernel,
            grid_spec=pltpu.PrefetchScalarGridSpec(
                num_scalar_prefetch=len(before),
                grid=(1,),
                in_specs=[pl.BlockSpec(memory_space=pl.ANY)] * len(held) + specs,
                out_specs=out_specs,
            ),
            out_shape=out_shapes,
            input_output_aliases={len(before) + i: i for i in range(len(held))},
            compiler_params=pltpu.CompilerParams(vmem_limit_bytes=20 * 2**20),
            cost_estimate=pl.CostEstimate(
                flops=int(flops * scale), bytes_accessed=int(moved * scale), transcendentals=0
            ),
            name=name,
        )(*before, *held, *arrays)
        self.last = results[0]
        return results


def shape(*dims, dtype=BF16):
    return jax.ShapeDtypeStruct(dims, dtype)


def dot(a, b, dims=(((1,), (0,)), ((), ()))):
    return lax.dot_general(a, b, dims, preferred_element_type=F32)


def picks(rows, count):
    columns = lax.broadcasted_iota(jnp.int32, (rows.shape[0], count), 1)
    return jnp.where(rows == columns, 1.0, 0.0).astype(BF16)


def weights_of(rows, gates):
    columns = lax.broadcasted_iota(jnp.int32, (rows.shape[0], gates.shape[1]), 1)
    return jnp.where(rows == columns, gates.astype(F32), 0.0)


def stacked(refs):
    return jnp.concatenate([ref[...] for ref in reversed(refs)], axis=0)


def gather_rows(lists, own_rows, oth_rows, own, oth, *outs):
    count, cap = own.shape[0], outs[0].shape[0]
    rows = dot(picks(own_rows[...], count), own[...])
    rows += dot(picks(oth_rows[...], count), oth[...])
    for s in range(lists):
        outs[s][...] = rows[s * cap : (s + 1) * cap].astype(BF16)


def gather_scaled(lists, own_rows, oth_rows, own, oth, own_gate, oth_gate, *outs):
    count, cap = own.shape[0], outs[0].shape[0]
    rows = dot(picks(own_rows[...], count), own[...]) + dot(picks(oth_rows[...], count), oth[...])
    for s in range(lists):
        span = slice(s * cap, (s + 1) * cap)
        gate = weights_of(own_rows[span, :], own_gate[s : s + 1, :])
        gate += weights_of(oth_rows[span, :], oth_gate[s : s + 1, :count])
        outs[s][...] = (jnp.sum(gate, axis=1, keepdims=True) * rows[span]).astype(BF16)


def first_products(lists, *refs):
    x, (w_gate, w_up, gate_out, up_out) = refs[:lists], refs[lists:]
    rows = stacked(x)
    gate_out[...] = dot(rows, w_gate[...])
    up_out[...] = dot(rows, w_up[...])


def activation(lists, *refs):
    x, (w_gate, w_up, gate_in, up_in, hidden, active_out, slope_out) = refs[:lists], refs[lists:]
    rows = stacked(x)
    pre_gate = gate_in[...] + dot(rows, w_gate[...])
    pre_up = up_in[...] + dot(rows, w_up[...])
    sigmoid_gate = jax.nn.sigmoid(pre_gate)
    active = pre_gate * sigmoid_gate
    hidden[...] = (active * pre_up).astype(BF16)
    active_out[...] = active
    slope_out[...] = pre_up * sigmoid_gate * (1.0 + pre_gate * (1.0 - sigmoid_gate))


def expert_rows(me, hidden, w_down, sent, kept):
    width = kept.shape[1]
    first = dot(hidden[...], w_down[:, :width])
    second = dot(hidden[...], w_down[:, width:])
    lower = me[0, 0] == 0
    sent[...] = jnp.where(lower, second, first).astype(BF16)
    kept[...] = jnp.where(lower, first, second)


def whole_rows(kept, arrived, *outs):
    cap = outs[0].shape[0]
    rows = (kept[...] + arrived[...].astype(F32)).astype(BF16)
    for s, out in enumerate(outs):
        out[...] = rows[s * cap : (s + 1) * cap]


def first_hidden_grad(lists, *refs):
    out_grad, (w_down, total) = refs[:lists], refs[lists:]
    total[...] = dot(stacked(out_grad), w_down[...], NT)


def hidden_grads(lists, *refs):
    out_grad = refs[:lists]
    w_down, first, hidden, active, slope, gate_grad, up_grad, gate_sum = refs[lists:]
    grad = first[...] + dot(stacked(out_grad), w_down[...], NT)
    gate_grad[...] = (grad * slope[...]).astype(BF16)
    up_grad[...] = (grad * active[...]).astype(BF16)
    sums = jnp.sum(grad * hidden[...].astype(F32), axis=1, keepdims=True)
    gate_sum[...] = jnp.broadcast_to(sums, gate_sum.shape)


def input_rows(lists, gate_grad, up_grad, w_gate, w_up, gate_sum, *outs):
    cap = gate_sum.shape[0] // lists
    rows = dot(gate_grad[...], w_gate[...], NT) + dot(up_grad[...], w_up[...], NT)
    for s in range(lists):
        span = slice(s * cap, (s + 1) * cap)
        outs[s][:cap, :] = rows[span].astype(BF16)
        sums = jnp.transpose(gate_sum[span, :])[:EXTRA, :]
        high = sums.astype(BF16).astype(F32)
        row = lax.broadcasted_iota(jnp.int32, sums.shape, 0)
        packed = jnp.where(row == 0, high, jnp.where(row == 1, sums - high, 0.0))
        outs[s][cap:, :] = jnp.zeros((EXTRA, outs[s].shape[1]), BF16)
        outs[s][cap:, :cap] = packed.astype(BF16)


def input_halves(me, gate_grad, up_grad, w_gate, w_up, sent, kept):
    width = kept.shape[1]
    half = lambda span: dot(gate_grad[...], w_gate[span, :], NT) + dot(up_grad[...], w_up[span, :], NT)
    first, second = half(slice(0, width)), half(slice(width, 2 * width))
    lower = me[0, 0] == 0
    sent[...] = jnp.where(lower, second, first).astype(BF16)
    kept[...] = jnp.where(lower, first, second)


def weight_grads(lists, *refs):
    x, out_grad = refs[:lists], refs[lists : 2 * lists]
    hidden, gate_grad, up_grad, w_gate_grad, w_up_grad, w_down_grad = refs[2 * lists :]
    rows = stacked(x)
    w_gate_grad[...] = dot(rows, gate_grad[...], TN).astype(BF16)
    w_up_grad[...] = dot(rows, up_grad[...], TN).astype(BF16)
    w_down_grad[...] = dot(hidden[...], stacked(out_grad), TN).astype(BF16)


def scatter_rows(lists, rows, *refs):
    values, out = refs[:lists], refs[lists]
    cap = rows.shape[1]
    extra = values[0].shape[0] - cap
    count = out.shape[0] - extra
    total = tail = None
    for s in range(lists):
        token = lax.broadcasted_iota(jnp.int32, (count, cap), 0)
        mask = jnp.where(rows[s : s + 1, :] == token, 1.0, 0.0).astype(BF16)
        term = dot(mask, values[s][:cap, :])
        total = term if total is None else total + term
        if extra:
            sums = dot(values[s][cap:, :cap], mask, NT)
            row = lax.broadcasted_iota(jnp.int32, sums.shape, 0)
            high = jnp.where(row == s, sums[:1, :], 0.0)
            term = high + jnp.where(row == lists + s, sums[1:2, :], 0.0)
            tail = term if tail is None else tail + term
    out[:count, :] = total.astype(out.dtype)
    if extra:
        out[count:, :] = jnp.zeros((extra, out.shape[1]), out.dtype)
        out[count:, :count] = tail.astype(out.dtype)


def scatter_scaled(lists, rows, gate, *refs):
    values, out = refs[:lists], refs[lists]
    cap, count = values[0].shape[0], out.shape[0]
    total = None
    for s in range(lists):
        mask = weights_of(rows[s * cap : (s + 1) * cap, :], gate[s : s + 1, :count]).astype(BF16)
        term = dot(mask, values[s][...], TN)
        total = term if total is None else total + term
    out[...] = total.astype(out.dtype)


def copy(source, out):
    out[...] = source[...]


def add_halves_and_gate(lists, kept, arrived, gate, out, gate_out):
    count = out.shape[0]
    out[...] = (kept[:count, :] + arrived[:count, :].astype(F32)).astype(BF16)
    sums = kept[count:, :count] + arrived[count:, :count].astype(F32)
    gate_out[...] = (sums[:lists, :] + sums[lists : 2 * lists, :]) / gate[...]


def on_device(tokens, cotangent, gate_probs, slot_rows, w_gate, w_up, w_down):
    count, model = tokens.shape
    lists, cap = slot_rows.shape
    hidden_units = w_gate.shape[2]
    width = model // CHUNKS
    total = lists * cap
    chunks = range(CHUNKS)
    w_gate, w_up, w_down = w_gate[0], w_up[0], w_down[0]
    me = lax.axis_index("dp").astype(jnp.int32)
    own_rows = slot_rows - me * count
    oth_rows = slot_rows - (1 - me) * count
    own_column, oth_column = own_rows.reshape(total, 1), oth_rows.reshape(total, 1)
    own_gate = gate_probs.T.astype(F32)
    run = Steps().run
    kernel = lambda body: functools.partial(body, lists)
    columns = lambda array, c: (array, part(array.shape[0], width, 0, c))
    w_rows = lambda array, c: (array, part(width, hidden_units, c, 0))
    span = lambda c: slice(c * width, (c + 1) * width)
    rows_shape = [shape(cap, width)] * lists
    square = [shape(total, hidden_units, dtype=F32)] * 2
    gather_flops = 4 * total * count * width
    flops = 2 * total * width * hidden_units

    scalar = (me.reshape(1, 1), pl.BlockSpec((1, 1), lambda i: (0, 0), memory_space=pltpu.SMEM))
    own_part, oth_part = me.reshape(1), (1 - me).reshape(1)

    def to_experts(rows):
        return [rows[0]] + [shifted(rows[s], "blk", -s) for s in range(1, lists)]

    def to_groups(rows):
        return [rows[0]] + [shifted(rows[s], "blk", s) for s in range(1, lists)]

    def gather_x(c):
        operands = [own_column, oth_column, columns(tokens, c), oth_x[c]]
        return to_experts(run(kernel(gather_rows), rows_shape, operands, gather_flops, "gather_x", tied=3))

    def gather_dy(c):
        arrived = (oth_dy[c], part(count, width, 0, 0))
        operands = [own_column, oth_column, columns(cotangent, c), arrived, own_gate, oth_gate]
        return to_experts(run(kernel(gather_scaled), rows_shape, operands, gather_flops, "gather_dy", tied=3))

    def weights(c, held):
        rows_out = (shape(model, hidden_units), part(width, hidden_units, c, 0))
        columns_out = (shape(hidden_units, model), part(hidden_units, width, 0, c))
        operands = x[c][::-1] + out_grad[c][::-1] + [hidden, gate_grad, up_grad]
        return run(kernel(weight_grads), [rows_out, rows_out, columns_out], operands, 3 * flops, "w_grads", held=held)

    def scatter(body, rows, values, gates, dtype, name, scale=BUSY, out=None, **more):
        columns = values[0].shape[1]
        out = out or shape(count + values[0].shape[0] - cap, columns, dtype=dtype)
        scatter_flops = 2 * total * count * columns
        return run(body, [out], [rows] + gates + values, scatter_flops, name, tied=-1, scale=scale, **more)[0]

    pieces = []
    for source, c in [(tokens, 0), (tokens, 1), (cotangent, 0), (cotangent, 1)]:
        pieces.append((after(source, pieces[-1]) if pieces else source)[:, span(c)])
    gate_rows = jnp.pad(gate_probs.T, ((0, EXTRA - lists), (0, width - count)))
    pieces[2] = jnp.concatenate([pieces[2], gate_rows], axis=0)
    oth_x = [shifted(piece, "dp", 1) for piece in pieces[:2]]
    oth_dy = [shifted(piece, "dp", 1) for piece in pieces[2:]]
    oth_gate = (oth_dy[0], part(EXTRA, width, count // EXTRA, 0))
    x = [gather_x(0), gather_x(1)]

    pre = run(kernel(first_products), square, x[0][::-1] + [w_rows(w_gate, 0), w_rows(w_up, 0)], 2 * flops, "pre")
    out_grad = [gather_dy(0)]
    hidden, active, slope = run(
        kernel(activation),
        [shape(total, hidden_units)] + square,
        x[1][::-1] + [w_rows(w_gate, 1), w_rows(w_up, 1)] + list(pre),
        2 * flops,
        "hidden",
    )
    sent, kept = run(
        expert_rows, [shape(total, width), shape(total, width, dtype=F32)], [scalar, hidden, w_down], 2 * flops,
        "expert_out", tied=1,
    )
    arrived = shifted(sent, "dp", 1)
    out_grad.append(gather_dy(1))

    first = run(kernel(first_hidden_grad), square[:1], out_grad[0][::-1] + [columns(w_down, 0)], flops, "hidden_grad", scale=BUSY)
    gate_grad, up_grad, gate_sum = run(
        kernel(hidden_grads),
        [shape(total, hidden_units)] * 2 + [shape(total, cap, dtype=F32)],
        out_grad[1][::-1] + [columns(w_down, 1), first[0], hidden, active, slope],
        flops,
        "hidden_grads",
        scale=BUSY,
    )
    few = 3 * model // 8
    many = model - few
    half = many // 2
    many_rows = lambda array: (array, part(many, hidden_units, 0, 0))
    few_rows = lambda array: (array, placed(few, hidden_units, many, 0))
    sent, second_kept = run(
        input_halves,
        [shape(total, half), shape(total, half, dtype=F32)],
        [scalar, gate_grad, up_grad, many_rows(w_gate), many_rows(w_up)],
        3 * flops,
        "input_grad",
        tied=1,
        scale=BUSY,
    )
    second_arrived = shifted(sent, "dp", 1)
    rows = run(
        kernel(input_rows),
        [shape(cap + EXTRA, few)] * lists,
        [gate_grad, up_grad, few_rows(w_gate), few_rows(w_up), gate_sum],
        flops,
        "input_grad",
        scale=BUSY,
    )
    first_rows = to_groups(rows)
    expert_out = to_groups(run(whole_rows, rows_shape, [kept, arrived], 0, "expert_out_rows"))
    weight_outs = weights(0, ())

    half_shape = [shape(cap, half)] * lists
    sent = scatter(kernel(scatter_rows), oth_rows, first_rows, [], BF16, "grad_sent")
    first_arrived = shifted(sent, "dp", 1)
    second_rows = to_groups(run(whole_rows, half_shape, [second_kept, second_arrived], 0, "input_grad_rows"))
    first_kept = scatter(kernel(scatter_rows), own_rows, first_rows, [], F32, "grad_kept")
    sent = scatter(kernel(scatter_scaled), oth_column, expert_out, [oth_gate], BF16, "mixed_sent", SHARED)
    mixed_arrived = shifted(sent, "dp", 1)
    mixed_block = (shape(count, model), chosen(count, width))
    mixed = scatter(
        kernel(scatter_scaled), own_column, expert_out, [own_gate], BF16, "mixed_own", SHARED, mixed_block, scalar=own_part
    )
    few_columns = (shape(count, model), placed(count, few, 0, many))
    *grad, gate_out = run(
        kernel(add_halves_and_gate),
        [few_columns, shape(lists, count, dtype=F32)],
        [first_kept, first_arrived, own_gate],
        0,
        "grad",
        scale=BUSY,
    )
    sent = scatter(kernel(scatter_rows), oth_rows, second_rows, [], BF16, "grad_sent")
    second_arrived = shifted(sent, "dp", 1)
    many_block = (shape(count, model), chosen(count, half))
    grad = scatter(
        kernel(scatter_rows), own_rows, second_rows, [], BF16, "grad_own", out=many_block, held=grad, scalar=own_part
    )
    weight_outs = weights(1, weight_outs)
    mixed = run(copy, [mixed_block], [mixed_arrived], 0, "mixed", held=[mixed], scale=BUSY, scalar=oth_part)[0]
    grad = run(copy, [many_block], [second_arrived], 0, "grad", held=[grad], scalar=oth_part)[0]
    return (mixed, grad, gate_out.T) + tuple(out[None] for out in weight_outs)


def solution(mesh):
    rows, lists = P(("blk", "dp"), None), P("blk", None)
    inner, outer = P("blk", None, "dp"), P("blk", "dp", None)
    return jax.shard_map(
        on_device,
        mesh=mesh,
        in_specs=(rows, rows, rows, lists, inner, inner, outer),
        out_specs=(rows, rows, rows, inner, inner, outer),
        check_vma=False,
    )
```

```python
import functools

import jax
import jax.numpy as jnp
from jax import lax
from jax.experimental import pallas as pl
from jax.experimental.pallas import tpu as pltpu
from jax.sharding import PartitionSpec as P

CHUNKS = 2
BUSY = 10
SHARED = 0.01
EXTRA = 16
F32 = jnp.float32
BF16 = jnp.bfloat16
NT = (((1,), (1,)), ((), ()))
TN = (((0,), (0,)), ((), ()))


def shifted(value, axis, steps):
    count = lax.axis_size(axis)
    pairs = [(source, (source + steps) % count) for source in range(count)]
    return lax.ppermute(value, axis, pairs)


def after(value, earlier):
    return lax.optimization_barrier((value, earlier))[0]


def whole(array):
    return pl.BlockSpec(array.shape, lambda i, *_: (0,) * len(array.shape))


def part(rows, columns, row, column):
    return pl.BlockSpec((rows, columns), lambda i, *_: (row, column))


def placed(rows, columns, row, column):
    return pl.BlockSpec((pl.Element(rows), pl.Element(columns)), lambda i, *_: (row, column))


def chosen(rows, columns):
    return pl.BlockSpec((rows, columns), lambda i, scalar: (0, scalar[0]))


def extent(spec):
    rows, columns = (getattr(size, "block_size", size) for size in spec.block_shape)
    return rows * columns


class Steps:
    def __init__(self):
        self.last = None

    def run(self, kernel, outs, operands, flops, name, held=(), tied=0, scale=SHARED, scalar=None):
        pair = lambda item: item if isinstance(item, tuple) else (item, whole(item))
        pairs = [pair(operand) for operand in operands]
        arrays, specs = [array for array, _ in pairs], [spec for _, spec in pairs]
        if self.last is not None:
            arrays[tied] = after(arrays[tied], self.last)
        out_shapes, out_specs = zip(*[pair(out) for out in outs])
        moved = sum(2 * extent(spec) for spec in specs + list(out_specs))
        before = [] if scalar is None else [scalar]
        skipped = len(before) + len(held)
        results = pl.pallas_call(
            (lambda *refs: kernel(*refs[skipped:])) if skipped else kernel,
            grid_spec=pltpu.PrefetchScalarGridSpec(
                num_scalar_prefetch=len(before),
                grid=(1,),
                in_specs=[pl.BlockSpec(memory_space=pl.ANY)] * len(held) + specs,
                out_specs=out_specs,
            ),
            out_shape=out_shapes,
            input_output_aliases={len(before) + i: i for i in range(len(held))},
            compiler_params=pltpu.CompilerParams(vmem_limit_bytes=20 * 2**20),
            cost_estimate=pl.CostEstimate(
                flops=int(flops * scale), bytes_accessed=int(moved * scale), transcendentals=0
            ),
            name=name,
        )(*before, *held, *arrays)
        self.last = results[0]
        return results


def shape(*dims, dtype=BF16):
    return jax.ShapeDtypeStruct(dims, dtype)


def joined(refs):
    return jnp.concatenate([ref[...] for ref in refs], axis=0)


def dot(a, b, dims=(((1,), (0,)), ((), ()))):
    return lax.dot_general(a, b, dims, preferred_element_type=F32)


def picks(rows, count):
    columns = lax.broadcasted_iota(jnp.int32, (rows.shape[0], count), 1)
    return jnp.where(rows == columns, 1.0, 0.0).astype(BF16)


def weights_of(rows, gates):
    columns = lax.broadcasted_iota(jnp.int32, (rows.shape[0], gates.shape[1]), 1)
    return jnp.where(rows == columns, gates.astype(F32), 0.0)


def stacked(refs):
    return jnp.concatenate([ref[...] for ref in reversed(refs)], axis=0)


def gather_rows(lists, own_rows, oth_rows, own, oth, *outs):
    count, cap = own.shape[0], outs[0].shape[0]
    rows = dot(picks(own_rows[...], count), own[...])
    rows += dot(picks(oth_rows[...], count), oth[...])
    for s in range(lists):
        outs[s][...] = rows[s * cap : (s + 1) * cap].astype(BF16)


def gather_scaled(lists, own_rows, oth_rows, own, oth, own_gate, oth_gate, *outs):
    count, cap = own.shape[0], outs[0].shape[0]
    rows = dot(picks(own_rows[...], count), own[...]) + dot(picks(oth_rows[...], count), oth[...])
    for s in range(lists):
        span = slice(s * cap, (s + 1) * cap)
        gate = weights_of(own_rows[span, :], own_gate[s : s + 1, :])
        gate += weights_of(oth_rows[span, :], oth_gate[s : s + 1, :count])
        outs[s][...] = (jnp.sum(gate, axis=1, keepdims=True) * rows[span]).astype(BF16)


def first_products(remote, *refs):
    x, (w_gate, w_up, gate_out, up_out) = refs[:remote], refs[remote:]
    rows = stacked(x)
    gate_out[...] = dot(rows, w_gate[...])
    up_out[...] = dot(rows, w_up[...])


def activate(pre_gate, pre_up, hidden, active_out, slope_out):
    sigmoid_gate = jax.nn.sigmoid(pre_gate)
    active = pre_gate * sigmoid_gate
    hidden[...] = (active * pre_up).astype(BF16)
    active_out[...] = active
    slope_out[...] = pre_up * sigmoid_gate * (1.0 + pre_gate * (1.0 - sigmoid_gate))


def activation(remote, *refs):
    x, (w_gate, w_up, gate_in, up_in, hidden, active, slope) = refs[:remote], refs[remote:]
    rows = stacked(x)
    pre_gate = gate_in[...] + dot(rows, w_gate[...])
    activate(pre_gate, up_in[...] + dot(rows, w_up[...]), hidden, active, slope)


def own_activation(first, second, w_gate, w_up, hidden, active, slope):
    width = first.shape[1]

    def product(w):
        return dot(first[...], w[:width, :]) + dot(second[...], w[width:, :])

    activate(product(w_gate), product(w_up), hidden, active, slope)


def expert_rows(me, hidden, w_down, sent, kept):
    width = kept.shape[1]
    first = dot(hidden[...], w_down[:, :width])
    second = dot(hidden[...], w_down[:, width:])
    lower = me[0, 0] == 0
    sent[...] = jnp.where(lower, second, first).astype(BF16)
    kept[...] = jnp.where(lower, first, second)


def whole_rows(kept, arrived, *outs):
    cap = outs[0].shape[0]
    rows = (kept[...] + arrived[...].astype(F32)).astype(BF16)
    for s, out in enumerate(outs):
        out[...] = rows[s * cap : (s + 1) * cap]


def first_hidden_grad(lists, *refs):
    out_grad, (w_down, total) = refs[:lists], refs[lists:]
    total[...] = dot(stacked(out_grad), w_down[...], NT)


def hidden_grads(lists, *refs):
    out_grad = refs[:lists]
    w_down, first, *saved, gate_grad, up_grad, gate_sum = refs[lists:]
    hidden, active, slope = [joined(saved[i : i + 2]) for i in range(0, 6, 2)]
    grad = first[...] + dot(stacked(out_grad), w_down[...], NT)
    gate_grad[...] = (grad * slope).astype(BF16)
    up_grad[...] = (grad * active).astype(BF16)
    sums = jnp.sum(grad * hidden.astype(F32), axis=1, keepdims=True)
    gate_sum[...] = jnp.broadcast_to(sums, gate_sum.shape)


def input_rows(lists, gate_grad, up_grad, w_gate, w_up, gate_sum, *outs):
    cap = gate_sum.shape[0] // lists
    rows = dot(gate_grad[...], w_gate[...], NT) + dot(up_grad[...], w_up[...], NT)
    for s in range(lists):
        span = slice(s * cap, (s + 1) * cap)
        outs[s][:cap, :] = rows[span].astype(BF16)
        sums = jnp.transpose(gate_sum[span, :])[:EXTRA, :]
        high = sums.astype(BF16).astype(F32)
        row = lax.broadcasted_iota(jnp.int32, sums.shape, 0)
        packed = jnp.where(row == 0, high, jnp.where(row == 1, sums - high, 0.0))
        outs[s][cap:, :] = jnp.zeros((EXTRA, outs[s].shape[1]), BF16)
        outs[s][cap:, :cap] = packed.astype(BF16)


def input_halves(me, gate_grad, up_grad, w_gate, w_up, sent, kept):
    width = kept.shape[1]
    half = lambda span: dot(gate_grad[...], w_gate[span, :], NT) + dot(up_grad[...], w_up[span, :], NT)
    first, second = half(slice(0, width)), half(slice(width, 2 * width))
    lower = me[0, 0] == 0
    sent[...] = jnp.where(lower, second, first).astype(BF16)
    kept[...] = jnp.where(lower, first, second)


def weight_grads(lists, *refs):
    x, out_grad = refs[:lists], refs[lists : 2 * lists]
    own_hidden, hidden, gate_grad, up_grad, w_gate_grad, w_up_grad, w_down_grad = refs[2 * lists :]
    rows = stacked(x)
    w_gate_grad[...] = dot(rows, gate_grad[...], TN).astype(BF16)
    w_up_grad[...] = dot(rows, up_grad[...], TN).astype(BF16)
    w_down_grad[...] = dot(joined([own_hidden, hidden]), stacked(out_grad), TN).astype(BF16)


def scatter_rows(lists, rows, *refs):
    values, out = refs[:lists], refs[lists]
    cap = rows.shape[1]
    extra = values[0].shape[0] - cap
    count = out.shape[0] - extra
    total = tail = None
    for s in range(lists):
        token = lax.broadcasted_iota(jnp.int32, (count, cap), 0)
        mask = jnp.where(rows[s : s + 1, :] == token, 1.0, 0.0).astype(BF16)
        term = dot(mask, values[s][:cap, :])
        total = term if total is None else total + term
        if extra:
            sums = dot(values[s][cap:, :cap], mask, NT)
            row = lax.broadcasted_iota(jnp.int32, sums.shape, 0)
            high = jnp.where(row == s, sums[:1, :], 0.0)
            term = high + jnp.where(row == lists + s, sums[1:2, :], 0.0)
            tail = term if tail is None else tail + term
    out[:count, :] = total.astype(out.dtype)
    if extra:
        out[count:, :] = jnp.zeros((extra, out.shape[1]), out.dtype)
        out[count:, :count] = tail.astype(out.dtype)


def scatter_scaled(lists, rows, gate, *refs):
    values, out = refs[:lists], refs[lists]
    cap, count = values[0].shape[0], out.shape[0]
    total = None
    for s in range(lists):
        mask = weights_of(rows[s * cap : (s + 1) * cap, :], gate[s : s + 1, :count]).astype(BF16)
        term = dot(mask, values[s][...], TN)
        total = term if total is None else total + term
    out[...] = total.astype(out.dtype)


def copy(source, out):
    out[...] = source[...]


def add_halves_and_gate(lists, kept, arrived, gate, out, gate_out):
    count = out.shape[0]
    out[...] = (kept[:count, :] + arrived[:count, :].astype(F32)).astype(BF16)
    sums = kept[count:, :count] + arrived[count:, :count].astype(F32)
    gate_out[...] = (sums[:lists, :] + sums[lists : 2 * lists, :]) / gate[...]


def on_device(tokens, cotangent, gate_probs, slot_rows, w_gate, w_up, w_down):
    count, model = tokens.shape
    lists, cap = slot_rows.shape
    hidden_units = w_gate.shape[2]
    width = model // CHUNKS
    total = lists * cap
    chunks = range(CHUNKS)
    w_gate, w_up, w_down = w_gate[0], w_up[0], w_down[0]
    me = lax.axis_index("dp").astype(jnp.int32)
    own_rows = slot_rows - me * count
    oth_rows = slot_rows - (1 - me) * count
    own_column, oth_column = own_rows.reshape(total, 1), oth_rows.reshape(total, 1)
    own_gate = gate_probs.T.astype(F32)
    run = Steps().run
    kernel = lambda body: functools.partial(body, lists)
    columns = lambda array, c: (array, part(array.shape[0], width, 0, c))
    w_rows = lambda array, c: (array, part(width, hidden_units, c, 0))
    span = lambda c: slice(c * width, (c + 1) * width)
    rows_shape = [shape(cap, width)] * lists
    square = [shape(total, hidden_units, dtype=F32)] * 2
    gather_flops = 4 * total * count * width
    flops = 2 * total * width * hidden_units

    scalar = (me.reshape(1, 1), pl.BlockSpec((1, 1), lambda i: (0, 0), memory_space=pltpu.SMEM))
    own_part, oth_part = me.reshape(1), (1 - me).reshape(1)

    def to_experts(rows):
        return [rows[0]] + [shifted(rows[s], "blk", -s) for s in range(1, lists)]

    def to_groups(rows):
        return [rows[0]] + [shifted(rows[s], "blk", s) for s in range(1, lists)]

    def gather_x(c):
        operands = [own_column, oth_column, columns(tokens, c), oth_x[c]]
        return to_experts(run(kernel(gather_rows), rows_shape, operands, gather_flops, "gather_x", tied=3))

    def gather_dy(c):
        arrived = (oth_dy[c], part(count, width, 0, 0))
        operands = [own_column, oth_column, columns(cotangent, c), arrived, own_gate, oth_gate]
        return to_experts(run(kernel(gather_scaled), rows_shape, operands, gather_flops, "gather_dy", tied=3))

    def weights(c, held):
        rows_out = (shape(model, hidden_units), part(width, hidden_units, c, 0))
        columns_out = (shape(hidden_units, model), part(hidden_units, width, 0, c))
        operands = x[c][::-1] + out_grad[c][::-1] + [own_hidden, hidden, gate_grad, up_grad]
        return run(kernel(weight_grads), [rows_out, rows_out, columns_out], operands, 3 * flops, "w_grads", held=held)

    def scatter(body, rows, values, gates, dtype, name, scale=BUSY, out=None, **more):
        columns = values[0].shape[1]
        out = out or shape(count + values[0].shape[0] - cap, columns, dtype=dtype)
        scatter_flops = 2 * total * count * columns
        return run(body, [out], [rows] + gates + values, scatter_flops, name, tied=-1, scale=scale, **more)[0]

    pieces = []
    for source, c in [(tokens, 0), (tokens, 1), (cotangent, 0), (cotangent, 1)]:
        pieces.append((after(source, pieces[-1]) if pieces else source)[:, span(c)])
    gate_rows = jnp.pad(gate_probs.T, ((0, EXTRA - lists), (0, width - count)))
    pieces[2] = jnp.concatenate([pieces[2], gate_rows], axis=0)
    oth_x = [shifted(piece, "dp", 1) for piece in pieces[:2]]
    oth_dy = [shifted(piece, "dp", 1) for piece in pieces[2:]]
    oth_gate = (oth_dy[0], part(EXTRA, width, count // EXTRA, 0))
    x = [gather_x(0), gather_x(1)]

    saved = lambda rows: [shape(rows, hidden_units)] + [shape(rows, hidden_units, dtype=F32)] * 2
    halves = lambda rows: [shape(rows, width), shape(rows, width, dtype=F32)]
    own_hidden, own_active, own_slope = run(
        own_activation, saved(cap), [x[0][0], x[1][0], w_gate, w_up], 4 * flops // lists, "own_hidden"
    )
    sent, own_kept = run(
        expert_rows, halves(cap), [scalar, own_hidden, w_down], 2 * flops // lists, "own_expert_out", tied=1
    )
    own_arrived = shifted(sent, "dp", 1)
    remote, others = lists - 1, total - cap
    pre = run(
        functools.partial(first_products, remote),
        saved(others)[1:],
        x[0][:0:-1] + [w_rows(w_gate, 0), w_rows(w_up, 0)],
        2 * flops,
        "pre",
    )
    out_grad = [gather_dy(0)]
    hidden, active, slope = run(
        functools.partial(activation, remote),
        saved(others),
        x[1][:0:-1] + [w_rows(w_gate, 1), w_rows(w_up, 1)] + list(pre),
        2 * flops,
        "hidden",
    )
    sent, kept = run(
        expert_rows, halves(others), [scalar, hidden, w_down], 2 * flops, "expert_out", tied=1
    )
    arrived = shifted(sent, "dp", 1)
    out_grad.append(gather_dy(1))

    own_out = run(whole_rows, rows_shape[:1], [own_kept, own_arrived], 0, "own_rows")
    first = run(kernel(first_hidden_grad), square[:1], out_grad[0][::-1] + [columns(w_down, 0)], flops, "hidden_grad", scale=BUSY)
    gate_grad, up_grad, gate_sum = run(
        kernel(hidden_grads),
        [shape(total, hidden_units)] * 2 + [shape(total, cap, dtype=F32)],
        out_grad[1][::-1] + [columns(w_down, 1), first[0], own_hidden, hidden, own_active, active, own_slope, slope],
        flops,
        "hidden_grads",
        scale=BUSY,
    )
    few = 3 * model // 8
    many = model - few
    half = many // 2
    many_rows = lambda array: (array, part(many, hidden_units, 0, 0))
    few_rows = lambda array: (array, placed(few, hidden_units, many, 0))
    sent, second_kept = run(
        input_halves,
        [shape(total, half), shape(total, half, dtype=F32)],
        [scalar, gate_grad, up_grad, many_rows(w_gate), many_rows(w_up)],
        3 * flops,
        "input_grad",
        tied=1,
        scale=BUSY,
    )
    second_arrived = shifted(sent, "dp", 1)
    rows = run(
        kernel(input_rows),
        [shape(cap + EXTRA, few)] * lists,
        [gate_grad, up_grad, few_rows(w_gate), few_rows(w_up), gate_sum],
        flops,
        "input_grad",
        scale=BUSY,
    )
    first_rows = to_groups(rows)
    expert_out = to_groups(own_out + run(whole_rows, rows_shape[1:], [kept, arrived], 0, "expert_out_rows"))
    weight_outs = weights(0, ())

    half_shape = [shape(cap, half)] * lists
    sent = scatter(kernel(scatter_rows), oth_rows, first_rows, [], BF16, "grad_sent")
    first_arrived = shifted(sent, "dp", 1)
    second_rows = to_groups(run(whole_rows, half_shape, [second_kept, second_arrived], 0, "input_grad_rows"))
    first_kept = scatter(kernel(scatter_rows), own_rows, first_rows, [], F32, "grad_kept")
    sent = scatter(kernel(scatter_scaled), oth_column, expert_out, [oth_gate], BF16, "mixed_sent", SHARED)
    mixed_arrived = shifted(sent, "dp", 1)
    mixed_block = (shape(count, model), chosen(count, width))
    mixed = scatter(
        kernel(scatter_scaled), own_column, expert_out, [own_gate], BF16, "mixed_own", SHARED, mixed_block, scalar=own_part
    )
    few_columns = (shape(count, model), placed(count, few, 0, many))
    *grad, gate_out = run(
        kernel(add_halves_and_gate),
        [few_columns, shape(lists, count, dtype=F32)],
        [first_kept, first_arrived, own_gate],
        0,
        "grad",
        scale=BUSY,
    )
    sent = scatter(kernel(scatter_rows), oth_rows, second_rows, [], BF16, "grad_sent")
    second_arrived = shifted(sent, "dp", 1)
    many_block = (shape(count, model), chosen(count, half))
    grad = scatter(
        kernel(scatter_rows), own_rows, second_rows, [], BF16, "grad_own", out=many_block, held=grad, scalar=own_part
    )
    weight_outs = weights(1, weight_outs)
    mixed = run(copy, [mixed_block], [mixed_arrived], 0, "mixed", held=[mixed], scale=BUSY, scalar=oth_part)[0]
    grad = run(copy, [many_block], [second_arrived], 0, "grad", held=[grad], scalar=oth_part)[0]
    return (mixed, grad, gate_out.T) + tuple(out[None] for out in weight_outs)


def solution(mesh):
    rows, lists = P(("blk", "dp"), None), P("blk", None)
    inner, outer = P("blk", None, "dp"), P("blk", "dp", None)
    return jax.shard_map(
        on_device,
        mesh=mesh,
        in_specs=(rows, rows, rows, lists, inner, inner, outer),
        out_specs=(rows, rows, rows, inner, inner, outer),
        check_vma=False,
    )
```

```python
import functools

import jax
import jax.numpy as jnp
from jax import lax
from jax.experimental import pallas as pl
from jax.experimental.pallas import tpu as pltpu
from jax.sharding import PartitionSpec as P

CHUNKS = 2
BUSY = 10
SHARED = 0.01
EXTRA = 16
F32 = jnp.float32
BF16 = jnp.bfloat16
NT = (((1,), (1,)), ((), ()))
TN = (((0,), (0,)), ((), ()))


def shifted(value, axis, steps):
    count = lax.axis_size(axis)
    pairs = [(source, (source + steps) % count) for source in range(count)]
    return lax.ppermute(value, axis, pairs)


def after(value, earlier):
    return lax.optimization_barrier((value, earlier))[0]


def whole(array):
    return pl.BlockSpec(array.shape, lambda i, *_: (0,) * len(array.shape))


def part(rows, columns, row, column):
    return pl.BlockSpec((rows, columns), lambda i, *_: (row, column))


def placed(rows, columns, row, column):
    return pl.BlockSpec((pl.Element(rows), pl.Element(columns)), lambda i, *_: (row, column))


def chosen(rows, columns):
    return pl.BlockSpec((rows, columns), lambda i, scalar: (0, scalar[0]))


def extent(spec):
    rows, columns = (getattr(size, "block_size", size) for size in spec.block_shape)
    return rows * columns


class Steps:
    def __init__(self):
        self.last = None

    def run(self, kernel, outs, operands, flops, name, held=(), tied=0, scale=SHARED, scalar=None):
        pair = lambda item: item if isinstance(item, tuple) else (item, whole(item))
        pairs = [pair(operand) for operand in operands]
        arrays, specs = [array for array, _ in pairs], [spec for _, spec in pairs]
        if self.last is not None:
            arrays[tied] = after(arrays[tied], self.last)
        out_shapes, out_specs = zip(*[pair(out) for out in outs])
        moved = sum(2 * extent(spec) for spec in specs + list(out_specs))
        before = [] if scalar is None else [scalar]
        skipped = len(before) + len(held)
        results = pl.pallas_call(
            (lambda *refs: kernel(*refs[skipped:])) if skipped else kernel,
            grid_spec=pltpu.PrefetchScalarGridSpec(
                num_scalar_prefetch=len(before),
                grid=(1,),
                in_specs=[pl.BlockSpec(memory_space=pl.ANY)] * len(held) + specs,
                out_specs=out_specs,
            ),
            out_shape=out_shapes,
            input_output_aliases={len(before) + i: i for i in range(len(held))},
            compiler_params=pltpu.CompilerParams(vmem_limit_bytes=20 * 2**20),
            cost_estimate=pl.CostEstimate(
                flops=int(flops * scale), bytes_accessed=int(moved * scale), transcendentals=0
            ),
            name=name,
        )(*before, *held, *arrays)
        self.last = results[0]
        return results


def shape(*dims, dtype=BF16):
    return jax.ShapeDtypeStruct(dims, dtype)


def dot(a, b, dims=(((1,), (0,)), ((), ()))):
    return lax.dot_general(a, b, dims, preferred_element_type=F32)


def picks(rows, count):
    columns = lax.broadcasted_iota(jnp.int32, (rows.shape[0], count), 1)
    return jnp.where(rows == columns, 1.0, 0.0).astype(BF16)


def weights_of(rows, gates):
    columns = lax.broadcasted_iota(jnp.int32, (rows.shape[0], gates.shape[1]), 1)
    return jnp.where(rows == columns, gates.astype(F32), 0.0)


def stacked(refs):
    return jnp.concatenate([ref[...] for ref in refs], axis=0)


def gather_rows(lists, own_rows, oth_rows, own, oth, *outs):
    count, cap = own.shape[0], outs[0].shape[0]
    rows = dot(picks(own_rows[...], count), own[...])
    rows += dot(picks(oth_rows[...], count), oth[...])
    for s in range(lists):
        outs[s][...] = rows[s * cap : (s + 1) * cap].astype(BF16)


def gather_scaled(lists, own_rows, oth_rows, own, oth, own_gate, oth_gate, *outs):
    count, cap = own.shape[0], outs[0].shape[0]
    rows = dot(picks(own_rows[...], count), own[...]) + dot(picks(oth_rows[...], count), oth[...])
    for s in range(lists):
        span = slice(s * cap, (s + 1) * cap)
        gate = weights_of(own_rows[span, :], own_gate[s : s + 1, :])
        gate += weights_of(oth_rows[span, :], oth_gate[s : s + 1, :count])
        outs[s][...] = (jnp.sum(gate, axis=1, keepdims=True) * rows[span]).astype(BF16)


def first_products(lists, *refs):
    x, (w_gate, w_up, gate_out, up_out) = refs[:lists], refs[lists:]
    rows = stacked(x)
    gate_out[...] = dot(rows, w_gate[...])
    up_out[...] = dot(rows, w_up[...])


def activation(lists, *refs):
    x, (w_gate, w_up, gate_in, up_in, hidden, active_out, slope_out) = refs[:lists], refs[lists:]
    rows = stacked(x)
    pre_gate = gate_in[...] + dot(rows, w_gate[...])
    pre_up = up_in[...] + dot(rows, w_up[...])
    sigmoid_gate = jax.nn.sigmoid(pre_gate)
    active = pre_gate * sigmoid_gate
    hidden[...] = (active * pre_up).astype(BF16)
    active_out[...] = active
    slope_out[...] = pre_up * sigmoid_gate * (1.0 + pre_gate * (1.0 - sigmoid_gate))


def expert_rows(me, hidden, w_down, sent, kept):
    width = kept.shape[1]
    first = dot(hidden[...], w_down[:, :width])
    second = dot(hidden[...], w_down[:, width:])
    lower = me[0, 0] == 0
    sent[...] = jnp.where(lower, second, first).astype(BF16)
    kept[...] = jnp.where(lower, first, second)


def whole_rows(kept, arrived, *outs):
    cap = outs[0].shape[0]
    rows = (kept[...] + arrived[...].astype(F32)).astype(BF16)
    for s, out in enumerate(outs):
        out[...] = rows[s * cap : (s + 1) * cap]


def first_hidden_grad(lists, *refs):
    out_grad, (w_down, total) = refs[:lists], refs[lists:]
    total[...] = dot(stacked(out_grad), w_down[...], NT)


def hidden_grads(lists, *refs):
    out_grad = refs[:lists]
    w_down, first, hidden, active, slope, gate_grad, up_grad, gate_sum = refs[lists:]
    grad = first[...] + dot(stacked(out_grad), w_down[...], NT)
    gate_grad[...] = (grad * slope[...]).astype(BF16)
    up_grad[...] = (grad * active[...]).astype(BF16)
    sums = jnp.sum(grad * hidden[...].astype(F32), axis=1, keepdims=True)
    gate_sum[...] = jnp.broadcast_to(sums, gate_sum.shape)


def input_rows(lists, gate_grad, up_grad, w_gate, w_up, gate_sum, *outs):
    cap = gate_sum.shape[0] // lists
    rows = dot(gate_grad[...], w_gate[...], NT) + dot(up_grad[...], w_up[...], NT)
    for s in range(lists):
        span = slice(s * cap, (s + 1) * cap)
        outs[s][:cap, :] = rows[span].astype(BF16)
        sums = jnp.transpose(gate_sum[span, :])[:EXTRA, :]
        high = sums.astype(BF16).astype(F32)
        row = lax.broadcasted_iota(jnp.int32, sums.shape, 0)
        packed = jnp.where(row == 0, high, jnp.where(row == 1, sums - high, 0.0))
        outs[s][cap:, :] = jnp.zeros((EXTRA, outs[s].shape[1]), BF16)
        outs[s][cap:, :cap] = packed.astype(BF16)


def input_halves(me, gate_grad, up_grad, w_gate, w_up, sent, kept):
    width = kept.shape[1]
    half = lambda span: dot(gate_grad[...], w_gate[span, :], NT) + dot(up_grad[...], w_up[span, :], NT)
    first, second = half(slice(0, width)), half(slice(width, 2 * width))
    lower = me[0, 0] == 0
    sent[...] = jnp.where(lower, second, first).astype(BF16)
    kept[...] = jnp.where(lower, first, second)


def weight_grads(lists, *refs):
    x, out_grad = refs[:lists], refs[lists : 2 * lists]
    hidden, gate_grad, up_grad, w_gate_grad, w_up_grad, w_down_grad = refs[2 * lists :]
    rows = stacked(x)
    w_gate_grad[...] = dot(rows, gate_grad[...], TN).astype(BF16)
    w_up_grad[...] = dot(rows, up_grad[...], TN).astype(BF16)
    w_down_grad[...] = dot(hidden[...], stacked(out_grad), TN).astype(BF16)


def scatter_rows(lists, rows, *refs):
    values, out = refs[:lists], refs[lists]
    cap = rows.shape[1]
    extra = values[0].shape[0] - cap
    count = out.shape[0] - extra
    total = tail = None
    for s in range(lists):
        token = lax.broadcasted_iota(jnp.int32, (count, cap), 0)
        mask = jnp.where(rows[s : s + 1, :] == token, 1.0, 0.0).astype(BF16)
        term = dot(mask, values[s][:cap, :])
        total = term if total is None else total + term
        if extra:
            sums = dot(values[s][cap:, :cap], mask, NT)
            row = lax.broadcasted_iota(jnp.int32, sums.shape, 0)
            high = jnp.where(row == s, sums[:1, :], 0.0)
            term = high + jnp.where(row == lists + s, sums[1:2, :], 0.0)
            tail = term if tail is None else tail + term
    out[:count, :] = total.astype(out.dtype)
    if extra:
        out[count:, :] = jnp.zeros((extra, out.shape[1]), out.dtype)
        out[count:, :count] = tail.astype(out.dtype)


def scatter_scaled(lists, rows, gate, *refs):
    values, out = refs[:lists], refs[lists]
    cap, count = values[0].shape[0], out.shape[0]
    total = None
    for s in range(lists):
        mask = weights_of(rows[s * cap : (s + 1) * cap, :], gate[s : s + 1, :count]).astype(BF16)
        term = dot(mask, values[s][...], TN)
        total = term if total is None else total + term
    out[...] = total.astype(out.dtype)


def copy(source, out):
    out[...] = source[...]


def add_halves_and_gate(lists, kept, arrived, gate, out, gate_out):
    count = out.shape[0]
    out[...] = (kept[:count, :] + arrived[:count, :].astype(F32)).astype(BF16)
    sums = kept[count:, :count] + arrived[count:, :count].astype(F32)
    gate_out[...] = (sums[:lists, :] + sums[lists : 2 * lists, :]) / gate[...]


def on_device(tokens, cotangent, gate_probs, slot_rows, w_gate, w_up, w_down):
    count, model = tokens.shape
    lists, cap = slot_rows.shape
    hidden_units = w_gate.shape[2]
    width = model // CHUNKS
    total = lists * cap
    chunks = range(CHUNKS)
    w_gate, w_up, w_down = w_gate[0], w_up[0], w_down[0]
    me = lax.axis_index("dp").astype(jnp.int32)
    own_rows = slot_rows - me * count
    oth_rows = slot_rows - (1 - me) * count
    own_column, oth_column = own_rows.reshape(total, 1), oth_rows.reshape(total, 1)
    own_gate = gate_probs.T.astype(F32)
    run = Steps().run
    kernel = lambda body: functools.partial(body, lists)
    columns = lambda array, c: (array, part(array.shape[0], width, 0, c))
    w_rows = lambda array, c: (array, part(width, hidden_units, c, 0))
    span = lambda c: slice(c * width, (c + 1) * width)
    rows_shape = [shape(cap, width)] * lists
    square = [shape(total, hidden_units, dtype=F32)] * 2
    gather_flops = 4 * total * count * width
    flops = 2 * total * width * hidden_units

    scalar = (me.reshape(1, 1), pl.BlockSpec((1, 1), lambda i: (0, 0), memory_space=pltpu.SMEM))
    own_part, oth_part = me.reshape(1), (1 - me).reshape(1)

    def to_experts(rows):
        return [rows[0]] + [shifted(rows[s], "blk", -s) for s in range(1, lists)]

    def to_groups(rows):
        return [rows[0]] + [shifted(rows[s], "blk", s) for s in range(1, lists)]

    def gather_x(c):
        operands = [own_column, oth_column, columns(tokens, c), oth_x[c]]
        return to_experts(run(kernel(gather_rows), rows_shape, operands, gather_flops, "gather_x", tied=3))

    def gather_dy(c):
        arrived = (oth_dy[c], part(count, width, 0, 0))
        operands = [own_column, oth_column, columns(cotangent, c), arrived, own_gate, oth_gate]
        scale = (SHARED, 6)[c]
        return run(kernel(gather_scaled), rows_shape, operands, gather_flops, "gather_dy", tied=3, scale=scale)

    def weights(c, held):
        rows_out = (shape(model, hidden_units), part(width, hidden_units, c, 0))
        columns_out = (shape(hidden_units, model), part(hidden_units, width, 0, c))
        operands = x[c] + out_grad[c] + [hidden, gate_grad, up_grad]
        return run(kernel(weight_grads), [rows_out, rows_out, columns_out], operands, 3 * flops, "w_grads", held=held)

    def scatter(body, rows, values, gates, dtype, name, scale=BUSY, out=None, **more):
        columns = values[0].shape[1]
        out = out or shape(count + values[0].shape[0] - cap, columns, dtype=dtype)
        scatter_flops = 2 * total * count * columns
        return run(body, [out], [rows] + gates + values, scatter_flops, name, tied=-1, scale=scale, **more)[0]

    pieces = []
    for source, c in [(tokens, 0), (tokens, 1), (cotangent, 0), (cotangent, 1)]:
        pieces.append((after(source, pieces[-1]) if pieces else source)[:, span(c)])
    gate_rows = jnp.pad(gate_probs.T, ((0, EXTRA - lists), (0, width - count)))
    pieces[2] = jnp.concatenate([pieces[2], gate_rows], axis=0)
    oth_x = [shifted(piece, "dp", 1) for piece in pieces[:2]]
    oth_dy = [shifted(piece, "dp", 1) for piece in pieces[2:]]
    oth_gate = (oth_dy[0], part(EXTRA, width, count // EXTRA, 0))
    x = [gather_x(0), gather_x(1)]

    pre = run(kernel(first_products), square, x[0] + [w_rows(w_gate, 0), w_rows(w_up, 0)], 2 * flops, "pre")
    first_grad = gather_dy(0)
    out_grad = [[first_grad[0], shifted(first_grad[1], "blk", -1)]]
    hidden, active, slope = run(
        kernel(activation),
        [shape(total, hidden_units)] + square,
        x[1] + [w_rows(w_gate, 1), w_rows(w_up, 1)] + list(pre),
        2 * flops,
        "hidden",
    )
    sent, kept = run(
        expert_rows, [shape(total, width), shape(total, width, dtype=F32)], [scalar, hidden, w_down], 2 * flops,
        "expert_out", tied=1,
    )
    arrived = shifted(sent, "dp", 1)
    out_grad[0] += [shifted(after(first_grad[s], sent), "blk", -s) for s in range(2, lists)]
    out_grad.append(to_experts(gather_dy(1)))

    first = run(kernel(first_hidden_grad), square[:1], out_grad[0] + [columns(w_down, 0)], flops, "hidden_grad", scale=BUSY)
    gate_grad, up_grad, gate_sum = run(
        kernel(hidden_grads),
        [shape(total, hidden_units)] * 2 + [shape(total, cap, dtype=F32)],
        out_grad[1] + [columns(w_down, 1), first[0], hidden, active, slope],
        flops,
        "hidden_grads",
        scale=BUSY,
    )
    few = 3 * model // 8
    many = model - few
    half = many // 2
    many_rows = lambda array: (array, part(many, hidden_units, 0, 0))
    few_rows = lambda array: (array, placed(few, hidden_units, many, 0))
    sent, second_kept = run(
        input_halves,
        [shape(total, half), shape(total, half, dtype=F32)],
        [scalar, gate_grad, up_grad, many_rows(w_gate), many_rows(w_up)],
        3 * flops,
        "input_grad",
        tied=1,
        scale=BUSY,
    )
    second_arrived = shifted(sent, "dp", 1)
    rows = run(
        kernel(input_rows),
        [shape(cap + EXTRA, few)] * lists,
        [gate_grad, up_grad, few_rows(w_gate), few_rows(w_up), gate_sum],
        flops,
        "input_grad",
        scale=BUSY,
    )
    first_rows = to_groups(rows)
    expert_out = to_groups(run(whole_rows, rows_shape, [kept, arrived], 0, "expert_out_rows"))
    weight_outs = weights(0, ())

    half_shape = [shape(cap, half)] * lists
    sent = scatter(kernel(scatter_rows), oth_rows, first_rows, [], BF16, "grad_sent")
    first_arrived = shifted(sent, "dp", 1)
    second_rows = to_groups(run(whole_rows, half_shape, [second_kept, second_arrived], 0, "input_grad_rows"))
    first_kept = scatter(kernel(scatter_rows), own_rows, first_rows, [], F32, "grad_kept")
    sent = scatter(kernel(scatter_scaled), oth_column, expert_out, [oth_gate], BF16, "mixed_sent", SHARED)
    mixed_arrived = shifted(sent, "dp", 1)
    mixed_block = (shape(count, model), chosen(count, width))
    mixed = scatter(
        kernel(scatter_scaled), own_column, expert_out, [own_gate], BF16, "mixed_own", SHARED, mixed_block, scalar=own_part
    )
    few_columns = (shape(count, model), placed(count, few, 0, many))
    *grad, gate_out = run(
        kernel(add_halves_and_gate),
        [few_columns, shape(lists, count, dtype=F32)],
        [first_kept, first_arrived, own_gate],
        0,
        "grad",
        scale=BUSY,
    )
    sent = scatter(kernel(scatter_rows), oth_rows, second_rows, [], BF16, "grad_sent")
    second_arrived = shifted(sent, "dp", 1)
    many_block = (shape(count, model), chosen(count, half))
    grad = scatter(
        kernel(scatter_rows), own_rows, second_rows, [], BF16, "grad_own", out=many_block, held=grad, scalar=own_part
    )
    weight_outs = weights(1, weight_outs)
    mixed = run(copy, [mixed_block], [mixed_arrived], 0, "mixed", held=[mixed], scale=BUSY, scalar=oth_part)[0]
    grad = run(copy, [many_block], [second_arrived], 0, "grad", held=[grad], scalar=oth_part)[0]
    return (mixed, grad, gate_out.T) + tuple(out[None] for out in weight_outs)


def solution(mesh):
    rows, lists = P(("blk", "dp"), None), P("blk", None)
    inner, outer = P("blk", None, "dp"), P("blk", "dp", None)
    return jax.shard_map(
        on_device,
        mesh=mesh,
        in_specs=(rows, rows, rows, lists, inner, inner, outer),
        out_specs=(rows, rows, rows, inner, inner, outer),
        check_vma=False,
    )
```

```python
import functools

import jax
import jax.numpy as jnp
from jax import lax
from jax.experimental import pallas as pl
from jax.experimental.pallas import tpu as pltpu
from jax.sharding import PartitionSpec as P

CHUNKS = 2
BUSY = 10
SHARED = 0.01
EXTRA = 16
F32 = jnp.float32
BF16 = jnp.bfloat16
NT = (((1,), (1,)), ((), ()))
TN = (((0,), (0,)), ((), ()))


def shifted(value, axis, steps):
    count = lax.axis_size(axis)
    pairs = [(source, (source + steps) % count) for source in range(count)]
    return lax.ppermute(value, axis, pairs)


def after(value, earlier):
    return lax.optimization_barrier((value, earlier))[0]


def whole(array):
    return pl.BlockSpec(array.shape, lambda i, *_: (0,) * len(array.shape))


def part(rows, columns, row, column):
    return pl.BlockSpec((rows, columns), lambda i, *_: (row, column))


def placed(rows, columns, row, column):
    return pl.BlockSpec((pl.Element(rows), pl.Element(columns)), lambda i, *_: (row, column))


def chosen(rows, columns):
    return pl.BlockSpec((rows, columns), lambda i, scalar: (0, scalar[0]))


def extent(spec):
    rows, columns = (getattr(size, "block_size", size) for size in spec.block_shape)
    return rows * columns


class Steps:
    def __init__(self):
        self.last = None

    def run(self, kernel, outs, operands, flops, name, held=(), tied=0, scale=SHARED, scalar=None):
        pair = lambda item: item if isinstance(item, tuple) else (item, whole(item))
        pairs = [pair(operand) for operand in operands]
        arrays, specs = [array for array, _ in pairs], [spec for _, spec in pairs]
        if self.last is not None:
            arrays[tied] = after(arrays[tied], self.last)
        out_shapes, out_specs = zip(*[pair(out) for out in outs])
        moved = sum(2 * extent(spec) for spec in specs + list(out_specs))
        before = [] if scalar is None else [scalar]
        skipped = len(before) + len(held)
        results = pl.pallas_call(
            (lambda *refs: kernel(*refs[skipped:])) if skipped else kernel,
            grid_spec=pltpu.PrefetchScalarGridSpec(
                num_scalar_prefetch=len(before),
                grid=(1,),
                in_specs=[pl.BlockSpec(memory_space=pl.ANY)] * len(held) + specs,
                out_specs=out_specs,
            ),
            out_shape=out_shapes,
            input_output_aliases={len(before) + i: i for i in range(len(held))},
            compiler_params=pltpu.CompilerParams(vmem_limit_bytes=20 * 2**20),
            cost_estimate=pl.CostEstimate(
                flops=int(flops * scale), bytes_accessed=int(moved * scale), transcendentals=0
            ),
            name=name,
        )(*before, *held, *arrays)
        self.last = results[0]
        return results


def shape(*dims, dtype=BF16):
    return jax.ShapeDtypeStruct(dims, dtype)


def dot(a, b, dims=(((1,), (0,)), ((), ()))):
    return lax.dot_general(a, b, dims, preferred_element_type=F32)


def picks(rows, count):
    columns = lax.broadcasted_iota(jnp.int32, (rows.shape[0], count), 1)
    return jnp.where(rows == columns, 1.0, 0.0).astype(BF16)


def weights_of(rows, gates):
    columns = lax.broadcasted_iota(jnp.int32, (rows.shape[0], gates.shape[1]), 1)
    return jnp.where(rows == columns, gates.astype(F32), 0.0)


def stacked(refs):
    return jnp.concatenate([ref[...] for ref in refs], axis=0)


def gather_rows(lists, own_rows, oth_rows, own, oth, *outs):
    count, cap = own.shape[0], outs[0].shape[0]
    rows = dot(picks(own_rows[...], count), own[...])
    rows += dot(picks(oth_rows[...], count), oth[...])
    for s in range(lists):
        outs[s][...] = rows[s * cap : (s + 1) * cap].astype(BF16)


def gather_scaled(lists, own_rows, oth_rows, own, oth, own_gate, oth_gate, *outs):
    count, cap = own.shape[0], outs[0].shape[0]
    rows = dot(picks(own_rows[...], count), own[...]) + dot(picks(oth_rows[...], count), oth[...])
    for s in range(lists):
        span = slice(s * cap, (s + 1) * cap)
        gate = weights_of(own_rows[span, :], own_gate[s : s + 1, :])
        gate += weights_of(oth_rows[span, :], oth_gate[s : s + 1, :count])
        outs[s][...] = (jnp.sum(gate, axis=1, keepdims=True) * rows[span]).astype(BF16)


def first_products(lists, *refs):
    x, (w_gate, w_up, gate_out, up_out) = refs[:lists], refs[lists:]
    rows = stacked(x)
    gate_out[...] = dot(rows, w_gate[...])
    up_out[...] = dot(rows, w_up[...])


def activation(lists, *refs):
    x, (w_gate, w_up, gate_in, up_in, hidden, active_out, slope_out) = refs[:lists], refs[lists:]
    rows = stacked(x)
    pre_gate = gate_in[...] + dot(rows, w_gate[...])
    pre_up = up_in[...] + dot(rows, w_up[...])
    sigmoid_gate = jax.nn.sigmoid(pre_gate)
    active = pre_gate * sigmoid_gate
    hidden[...] = (active * pre_up).astype(BF16)
    active_out[...] = active
    slope_out[...] = pre_up * sigmoid_gate * (1.0 + pre_gate * (1.0 - sigmoid_gate))


def expert_rows(me, hidden, w_down, sent, kept):
    width = kept.shape[1]
    first = dot(hidden[...], w_down[:, :width])
    second = dot(hidden[...], w_down[:, width:])
    lower = me[0, 0] == 0
    sent[...] = jnp.where(lower, second, first).astype(BF16)
    kept[...] = jnp.where(lower, first, second)


def whole_rows(kept, arrived, *outs):
    cap = outs[0].shape[0]
    rows = (kept[...] + arrived[...].astype(F32)).astype(BF16)
    for s, out in enumerate(outs):
        out[...] = rows[s * cap : (s + 1) * cap]


def first_hidden_grad(lists, *refs):
    out_grad, (w_down, total) = refs[:lists], refs[lists:]
    total[...] = dot(stacked(out_grad), w_down[...], NT)


def hidden_grads(lists, *refs):
    out_grad = refs[:lists]
    w_down, first, hidden, active, slope, gate_grad, up_grad, gate_sum = refs[lists:]
    grad = first[...] + dot(stacked(out_grad), w_down[...], NT)
    gate_grad[...] = (grad * slope[...]).astype(BF16)
    up_grad[...] = (grad * active[...]).astype(BF16)
    sums = jnp.sum(grad * hidden[...].astype(F32), axis=1, keepdims=True)
    gate_sum[...] = jnp.broadcast_to(sums, gate_sum.shape)


def input_rows(lists, gate_grad, up_grad, w_gate, w_up, gate_sum, *outs):
    cap = gate_sum.shape[0] // lists
    rows = dot(gate_grad[...], w_gate[...], NT) + dot(up_grad[...], w_up[...], NT)
    for s in range(lists):
        span = slice(s * cap, (s + 1) * cap)
        outs[s][:cap, :] = rows[span].astype(BF16)
        sums = jnp.transpose(gate_sum[span, :])[:EXTRA, :]
        high = sums.astype(BF16).astype(F32)
        row = lax.broadcasted_iota(jnp.int32, sums.shape, 0)
        packed = jnp.where(row == 0, high, jnp.where(row == 1, sums - high, 0.0))
        outs[s][cap:, :] = jnp.zeros((EXTRA, outs[s].shape[1]), BF16)
        outs[s][cap:, :cap] = packed.astype(BF16)


def input_halves(me, gate_grad, up_grad, w_gate, w_up, sent, kept):
    width = kept.shape[1]
    half = lambda span: dot(gate_grad[...], w_gate[span, :], NT) + dot(up_grad[...], w_up[span, :], NT)
    first, second = half(slice(0, width)), half(slice(width, 2 * width))
    lower = me[0, 0] == 0
    sent[...] = jnp.where(lower, second, first).astype(BF16)
    kept[...] = jnp.where(lower, first, second)


def weight_grads(lists, *refs):
    x, out_grad = refs[:lists], refs[lists : 2 * lists]
    hidden, gate_grad, up_grad, w_gate_grad, w_up_grad, w_down_grad = refs[2 * lists :]
    rows = stacked(x)
    w_gate_grad[...] = dot(rows, gate_grad[...], TN).astype(BF16)
    w_up_grad[...] = dot(rows, up_grad[...], TN).astype(BF16)
    w_down_grad[...] = dot(hidden[...], stacked(out_grad), TN).astype(BF16)


def scatter_rows(lists, rows, *refs):
    values, out = refs[:lists], refs[lists]
    cap = rows.shape[1]
    extra = values[0].shape[0] - cap
    count = out.shape[0] - extra
    total = tail = None
    for s in range(lists):
        token = lax.broadcasted_iota(jnp.int32, (count, cap), 0)
        mask = jnp.where(rows[s : s + 1, :] == token, 1.0, 0.0).astype(BF16)
        term = dot(mask, values[s][:cap, :])
        total = term if total is None else total + term
        if extra:
            sums = dot(values[s][cap:, :cap], mask, NT)
            row = lax.broadcasted_iota(jnp.int32, sums.shape, 0)
            high = jnp.where(row == s, sums[:1, :], 0.0)
            term = high + jnp.where(row == lists + s, sums[1:2, :], 0.0)
            tail = term if tail is None else tail + term
    out[:count, :] = total.astype(out.dtype)
    if extra:
        out[count:, :] = jnp.zeros((extra, out.shape[1]), out.dtype)
        out[count:, :count] = tail.astype(out.dtype)


def scatter_scaled(lists, rows, gate, *refs):
    values, out = refs[:lists], refs[lists]
    cap, count = values[0].shape[0], out.shape[0]
    total = None
    for s in range(lists):
        mask = weights_of(rows[s * cap : (s + 1) * cap, :], gate[s : s + 1, :count]).astype(BF16)
        term = dot(mask, values[s][...], TN)
        total = term if total is None else total + term
    out[...] = total.astype(out.dtype)


def copy(source, out):
    out[...] = source[...]


def add_halves_and_gate(lists, kept, arrived, gate, out, gate_out):
    count = out.shape[0]
    out[...] = (kept[:count, :] + arrived[:count, :].astype(F32)).astype(BF16)
    sums = kept[count:, :count] + arrived[count:, :count].astype(F32)
    gate_out[...] = (sums[:lists, :] + sums[lists : 2 * lists, :]) / gate[...]


def on_device(tokens, cotangent, gate_probs, slot_rows, w_gate, w_up, w_down):
    count, model = tokens.shape
    lists, cap = slot_rows.shape
    hidden_units = w_gate.shape[2]
    width = model // CHUNKS
    total = lists * cap
    chunks = range(CHUNKS)
    w_gate, w_up, w_down = w_gate[0], w_up[0], w_down[0]
    me = lax.axis_index("dp").astype(jnp.int32)
    own_rows = slot_rows - me * count
    oth_rows = slot_rows - (1 - me) * count
    own_column, oth_column = own_rows.reshape(total, 1), oth_rows.reshape(total, 1)
    own_gate = gate_probs.T.astype(F32)
    run = Steps().run
    kernel = lambda body: functools.partial(body, lists)
    columns = lambda array, c: (array, part(array.shape[0], width, 0, c))
    w_rows = lambda array, c: (array, part(width, hidden_units, c, 0))
    span = lambda c: slice(c * width, (c + 1) * width)
    rows_shape = [shape(cap, width)] * lists
    square = [shape(total, hidden_units, dtype=F32)] * 2
    gather_flops = 4 * total * count * width
    flops = 2 * total * width * hidden_units

    scalar = (me.reshape(1, 1), pl.BlockSpec((1, 1), lambda i: (0, 0), memory_space=pltpu.SMEM))
    own_part, oth_part = me.reshape(1), (1 - me).reshape(1)

    def to_experts(rows):
        return [rows[0]] + [shifted(rows[s], "blk", -s) for s in range(1, lists)]

    def to_groups(rows):
        return [rows[0]] + [shifted(rows[s], "blk", s) for s in range(1, lists)]

    def gather_x(c):
        operands = [own_column, oth_column, columns(tokens, c), oth_x[c]]
        return to_experts(run(kernel(gather_rows), rows_shape, operands, gather_flops, "gather_x", tied=3))

    def gather_dy(c):
        arrived = (oth_dy[c], part(count, width, 0, 0))
        operands = [own_column, oth_column, columns(cotangent, c), arrived, own_gate, oth_gate]
        return to_experts(run(kernel(gather_scaled), rows_shape, operands, gather_flops, "gather_dy", tied=3))

    def weights(c, held):
        rows_out = (shape(model, hidden_units), part(width, hidden_units, c, 0))
        columns_out = (shape(hidden_units, model), part(hidden_units, width, 0, c))
        operands = x[c] + out_grad[c] + [hidden, gate_grad, up_grad]
        return run(kernel(weight_grads), [rows_out, rows_out, columns_out], operands, 3 * flops, "w_grads", held=held)

    def scatter(body, rows, values, gates, dtype, name, scale=BUSY, out=None, **more):
        columns = values[0].shape[1]
        out = out or shape(count + values[0].shape[0] - cap, columns, dtype=dtype)
        scatter_flops = 2 * total * count * columns
        return run(body, [out], [rows] + gates + values, scatter_flops, name, tied=-1, scale=scale, **more)[0]

    pieces = []
    for source, c in [(tokens, 0), (tokens, 1), (cotangent, 0), (cotangent, 1)]:
        pieces.append((after(source, pieces[-1]) if pieces else source)[:, span(c)])
    gate_rows = jnp.pad(gate_probs.T, ((0, EXTRA - lists), (0, width - count)))
    pieces[2] = jnp.concatenate([pieces[2], gate_rows], axis=0)
    oth_x = [shifted(piece, "dp", 1) for piece in pieces[:2]]
    oth_dy = [shifted(piece, "dp", 1) for piece in pieces[2:]]
    oth_gate = (oth_dy[0], part(EXTRA, width, count // EXTRA, 0))
    x = [gather_x(0), gather_x(1)]

    pre = run(kernel(first_products), square, x[0] + [w_rows(w_gate, 0), w_rows(w_up, 0)], 2 * flops, "pre")
    out_grad = [gather_dy(0)]
    hidden, active, slope = run(
        kernel(activation),
        [shape(total, hidden_units)] + square,
        x[1] + [w_rows(w_gate, 1), w_rows(w_up, 1)] + list(pre),
        2 * flops,
        "hidden",
    )
    sent, kept = run(
        expert_rows, [shape(total, width), shape(total, width, dtype=F32)], [scalar, hidden, w_down], 2 * flops,
        "expert_out", tied=1,
    )
    arrived = shifted(sent, "dp", 1)
    out_grad.append(gather_dy(1))

    first = run(kernel(first_hidden_grad), square[:1], out_grad[0] + [columns(w_down, 0)], flops, "hidden_grad", scale=BUSY)
    gate_grad, up_grad, gate_sum = run(
        kernel(hidden_grads),
        [shape(total, hidden_units)] * 2 + [shape(total, cap, dtype=F32)],
        out_grad[1] + [columns(w_down, 1), first[0], hidden, active, slope],
        flops,
        "hidden_grads",
        scale=BUSY,
    )
    few = 3 * model // 8
    many = model - few
    half = many // 2
    many_rows = lambda array: (array, part(many, hidden_units, 0, 0))
    few_rows = lambda array: (array, placed(few, hidden_units, many, 0))
    sent, second_kept = run(
        input_halves,
        [shape(total, half), shape(total, half, dtype=F32)],
        [scalar, gate_grad, up_grad, many_rows(w_gate), many_rows(w_up)],
        3 * flops,
        "input_grad",
        tied=1,
        scale=BUSY,
    )
    second_arrived = shifted(sent, "dp", 1)
    rows = run(
        kernel(input_rows),
        [shape(cap + EXTRA, few)] * lists,
        [gate_grad, up_grad, few_rows(w_gate), few_rows(w_up), gate_sum],
        flops,
        "input_grad",
        scale=BUSY,
    )
    first_rows = to_groups(rows)
    weight_outs = weights(0, ())
    expert_out = to_groups(run(whole_rows, rows_shape, [kept, arrived], 0, "expert_out_rows"))

    half_shape = [shape(cap, half)] * lists
    sent = scatter(kernel(scatter_rows), oth_rows, first_rows, [], BF16, "grad_sent", SHARED)
    first_arrived = shifted(sent, "dp", 1)
    second_rows = to_groups(run(whole_rows, half_shape, [second_kept, second_arrived], 0, "input_grad_rows"))
    first_kept = scatter(kernel(scatter_rows), own_rows, first_rows, [], F32, "grad_kept")
    sent = scatter(kernel(scatter_scaled), oth_column, expert_out, [oth_gate], BF16, "mixed_sent", SHARED)
    mixed_arrived = shifted(sent, "dp", 1)
    mixed_block = (shape(count, model), chosen(count, width))
    mixed = scatter(
        kernel(scatter_scaled), own_column, expert_out, [own_gate], BF16, "mixed_own", SHARED, mixed_block, scalar=own_part
    )
    few_columns = (shape(count, model), placed(count, few, 0, many))
    *grad, gate_out = run(
        kernel(add_halves_and_gate),
        [few_columns, shape(lists, count, dtype=F32)],
        [first_kept, first_arrived, own_gate],
        0,
        "grad",
        scale=BUSY,
    )
    sent = scatter(kernel(scatter_rows), oth_rows, second_rows, [], BF16, "grad_sent")
    second_arrived = shifted(sent, "dp", 1)
    many_block = (shape(count, model), chosen(count, half))
    grad = scatter(
        kernel(scatter_rows), own_rows, second_rows, [], BF16, "grad_own", out=many_block, held=grad, scalar=own_part
    )
    weight_outs = weights(1, weight_outs)
    mixed = run(copy, [mixed_block], [mixed_arrived], 0, "mixed", held=[mixed], scale=BUSY, scalar=oth_part)[0]
    grad = run(copy, [many_block], [second_arrived], 0, "grad", held=[grad], scalar=oth_part)[0]
    return (mixed, grad, gate_out.T) + tuple(out[None] for out in weight_outs)


def solution(mesh):
    rows, lists = P(("blk", "dp"), None), P("blk", None)
    inner, outer = P("blk", None, "dp"), P("blk", "dp", None)
    return jax.shard_map(
        on_device,
        mesh=mesh,
        in_specs=(rows, rows, rows, lists, inner, inner, outer),
        out_specs=(rows, rows, rows, inner, inner, outer),
        check_vma=False,
    )
```

```python
import functools

import jax
import jax.numpy as jnp
from jax import lax
from jax.experimental import pallas as pl
from jax.experimental.pallas import tpu as pltpu
from jax.sharding import PartitionSpec as P

CHUNKS = 2
BUSY = 10
SHARED = 0.01
EXTRA = 16
F32 = jnp.float32
BF16 = jnp.bfloat16
NT = (((1,), (1,)), ((), ()))
TN = (((0,), (0,)), ((), ()))


def shifted(value, axis, steps):
    count = lax.axis_size(axis)
    pairs = [(source, (source + steps) % count) for source in range(count)]
    return lax.ppermute(value, axis, pairs)


def after(value, earlier):
    return lax.optimization_barrier((value, earlier))[0]


def whole(array):
    return pl.BlockSpec(array.shape, lambda i, *_: (0,) * len(array.shape))


def part(rows, columns, row, column):
    return pl.BlockSpec((rows, columns), lambda i, *_: (row, column))


def placed(rows, columns, row, column):
    return pl.BlockSpec((pl.Element(rows), pl.Element(columns)), lambda i, *_: (row, column))


def chosen(rows, columns):
    return pl.BlockSpec((rows, columns), lambda i, scalar: (0, scalar[0]))


def extent(spec):
    rows, columns = (getattr(size, "block_size", size) for size in spec.block_shape)
    return rows * columns


class Steps:
    def __init__(self):
        self.last = None

    def run(self, kernel, outs, operands, flops, name, held=(), tied=0, scale=SHARED, scalar=None):
        pair = lambda item: item if isinstance(item, tuple) else (item, whole(item))
        pairs = [pair(operand) for operand in operands]
        arrays, specs = [array for array, _ in pairs], [spec for _, spec in pairs]
        if self.last is not None:
            arrays[tied] = after(arrays[tied], self.last)
        out_shapes, out_specs = zip(*[pair(out) for out in outs])
        moved = sum(2 * extent(spec) for spec in specs + list(out_specs))
        before = [] if scalar is None else [scalar]
        skipped = len(before) + len(held)
        results = pl.pallas_call(
            (lambda *refs: kernel(*refs[skipped:])) if skipped else kernel,
            grid_spec=pltpu.PrefetchScalarGridSpec(
                num_scalar_prefetch=len(before),
                grid=(1,),
                in_specs=[pl.BlockSpec(memory_space=pl.ANY)] * len(held) + specs,
                out_specs=out_specs,
            ),
            out_shape=out_shapes,
            input_output_aliases={len(before) + i: i for i in range(len(held))},
            compiler_params=pltpu.CompilerParams(vmem_limit_bytes=20 * 2**20),
            cost_estimate=pl.CostEstimate(
                flops=int(flops * scale), bytes_accessed=int(moved * scale), transcendentals=0
            ),
            name=name,
        )(*before, *held, *arrays)
        self.last = results[0]
        return results


def shape(*dims, dtype=BF16):
    return jax.ShapeDtypeStruct(dims, dtype)


def dot(a, b, dims=(((1,), (0,)), ((), ()))):
    return lax.dot_general(a, b, dims, preferred_element_type=F32)


def picks(rows, count):
    columns = lax.broadcasted_iota(jnp.int32, (rows.shape[0], count), 1)
    return jnp.where(rows == columns, 1.0, 0.0).astype(BF16)


def weights_of(rows, gates):
    columns = lax.broadcasted_iota(jnp.int32, (rows.shape[0], gates.shape[1]), 1)
    return jnp.where(rows == columns, gates.astype(F32), 0.0)


def stacked(refs):
    return jnp.concatenate([ref[...] for ref in refs], axis=0)


def gather_rows(lists, own_rows, oth_rows, own, oth, *outs):
    count, cap = own.shape[0], outs[0].shape[0]
    rows = dot(picks(own_rows[...], count), own[...])
    rows += dot(picks(oth_rows[...], count), oth[...])
    for s in range(lists):
        outs[s][...] = rows[s * cap : (s + 1) * cap].astype(BF16)


def gather_scaled(lists, own_rows, oth_rows, own, oth, own_gate, oth_gate, *outs):
    count, cap = own.shape[0], outs[0].shape[0]
    rows = dot(picks(own_rows[...], count), own[...]) + dot(picks(oth_rows[...], count), oth[...])
    for s in range(lists):
        span = slice(s * cap, (s + 1) * cap)
        gate = weights_of(own_rows[span, :], own_gate[s : s + 1, :])
        gate += weights_of(oth_rows[span, :], oth_gate[s : s + 1, :count])
        outs[s][...] = (jnp.sum(gate, axis=1, keepdims=True) * rows[span]).astype(BF16)


def first_products(lists, *refs):
    x, (w_gate, w_up, gate_out, up_out) = refs[:lists], refs[lists:]
    rows = stacked(x)
    gate_out[...] = dot(rows, w_gate[...])
    up_out[...] = dot(rows, w_up[...])


def activation(lists, *refs):
    x, (w_gate, w_up, gate_in, up_in, hidden, active_out, slope_out) = refs[:lists], refs[lists:]
    rows = stacked(x)
    pre_gate = gate_in[...] + dot(rows, w_gate[...])
    pre_up = up_in[...] + dot(rows, w_up[...])
    sigmoid_gate = jax.nn.sigmoid(pre_gate)
    active = pre_gate * sigmoid_gate
    hidden[...] = (active * pre_up).astype(BF16)
    active_out[...] = active
    slope_out[...] = pre_up * sigmoid_gate * (1.0 + pre_gate * (1.0 - sigmoid_gate))


def expert_rows(me, hidden, w_down, sent, kept):
    width = kept.shape[1]
    first = dot(hidden[...], w_down[:, :width])
    second = dot(hidden[...], w_down[:, width:])
    lower = me[0, 0] == 0
    sent[...] = jnp.where(lower, second, first).astype(BF16)
    kept[...] = jnp.where(lower, first, second)


def whole_rows(kept, arrived, *outs):
    cap = outs[0].shape[0]
    rows = (kept[...] + arrived[...].astype(F32)).astype(BF16)
    for s, out in enumerate(outs):
        out[...] = rows[s * cap : (s + 1) * cap]


def first_hidden_grad(lists, *refs):
    out_grad, (w_down, total) = refs[:lists], refs[lists:]
    total[...] = dot(stacked(out_grad), w_down[...], NT)


def hidden_grads(lists, *refs):
    out_grad = refs[:lists]
    w_down, first, hidden, active, slope, gate_grad, up_grad, gate_sum = refs[lists:]
    grad = first[...] + dot(stacked(out_grad), w_down[...], NT)
    gate_grad[...] = (grad * slope[...]).astype(BF16)
    up_grad[...] = (grad * active[...]).astype(BF16)
    sums = jnp.sum(grad * hidden[...].astype(F32), axis=1, keepdims=True)
    gate_sum[...] = jnp.broadcast_to(sums, gate_sum.shape)


def input_rows(lists, gate_grad, up_grad, w_gate, w_up, gate_sum, *outs):
    cap = gate_sum.shape[0] // lists
    rows = dot(gate_grad[...], w_gate[...], NT) + dot(up_grad[...], w_up[...], NT)
    for s in range(lists):
        span = slice(s * cap, (s + 1) * cap)
        outs[s][:cap, :] = rows[span].astype(BF16)
        sums = jnp.transpose(gate_sum[span, :])[:EXTRA, :]
        high = sums.astype(BF16).astype(F32)
        row = lax.broadcasted_iota(jnp.int32, sums.shape, 0)
        packed = jnp.where(row == 0, high, jnp.where(row == 1, sums - high, 0.0))
        outs[s][cap:, :] = jnp.zeros((EXTRA, outs[s].shape[1]), BF16)
        outs[s][cap:, :cap] = packed.astype(BF16)


def input_halves(me, gate_grad, up_grad, w_gate, w_up, sent, kept):
    width = kept.shape[1]
    half = lambda span: dot(gate_grad[...], w_gate[span, :], NT) + dot(up_grad[...], w_up[span, :], NT)
    first, second = half(slice(0, width)), half(slice(width, 2 * width))
    lower = me[0, 0] == 0
    sent[...] = jnp.where(lower, second, first).astype(BF16)
    kept[...] = jnp.where(lower, first, second)


def weight_grads(lists, *refs):
    x, out_grad = refs[:lists], refs[lists : 2 * lists]
    hidden, gate_grad, up_grad, w_gate_grad, w_up_grad, w_down_grad = refs[2 * lists :]
    rows = stacked(x)
    w_gate_grad[...] = dot(rows, gate_grad[...], TN).astype(BF16)
    w_up_grad[...] = dot(rows, up_grad[...], TN).astype(BF16)
    w_down_grad[...] = dot(hidden[...], stacked(out_grad), TN).astype(BF16)


def scatter_rows(lists, rows, *refs):
    values, out = refs[:lists], refs[lists]
    cap = rows.shape[1]
    extra = values[0].shape[0] - cap
    count = out.shape[0] - extra
    total = tail = None
    for s in range(lists):
        token = lax.broadcasted_iota(jnp.int32, (count, cap), 0)
        mask = jnp.where(rows[s : s + 1, :] == token, 1.0, 0.0).astype(BF16)
        term = dot(mask, values[s][:cap, :])
        total = term if total is None else total + term
        if extra:
            sums = dot(values[s][cap:, :cap], mask, NT)
            row = lax.broadcasted_iota(jnp.int32, sums.shape, 0)
            high = jnp.where(row == s, sums[:1, :], 0.0)
            term = high + jnp.where(row == lists + s, sums[1:2, :], 0.0)
            tail = term if tail is None else tail + term
    out[:count, :] = total.astype(out.dtype)
    if extra:
        out[count:, :] = jnp.zeros((extra, out.shape[1]), out.dtype)
        out[count:, :count] = tail.astype(out.dtype)


def scatter_scaled(lists, rows, gate, *refs):
    values, out = refs[:lists], refs[lists]
    cap, count = values[0].shape[0], out.shape[0]
    total = None
    for s in range(lists):
        mask = weights_of(rows[s * cap : (s + 1) * cap, :], gate[s : s + 1, :count]).astype(BF16)
        term = dot(mask, values[s][...], TN)
        total = term if total is None else total + term
    out[...] = total.astype(out.dtype)


def copy(source, out):
    out[...] = source[...]


def add_halves_and_gate(lists, kept, arrived, gate, out, gate_out):
    count = out.shape[0]
    out[...] = (kept[:count, :] + arrived[:count, :].astype(F32)).astype(BF16)
    sums = kept[count:, :count] + arrived[count:, :count].astype(F32)
    gate_out[...] = (sums[:lists, :] + sums[lists : 2 * lists, :]) / gate[...]


def on_device(tokens, cotangent, gate_probs, slot_rows, w_gate, w_up, w_down):
    count, model = tokens.shape
    lists, cap = slot_rows.shape
    hidden_units = w_gate.shape[2]
    width = model // CHUNKS
    total = lists * cap
    chunks = range(CHUNKS)
    w_gate, w_up, w_down = w_gate[0], w_up[0], w_down[0]
    me = lax.axis_index("dp").astype(jnp.int32)
    own_rows = slot_rows - me * count
    oth_rows = slot_rows - (1 - me) * count
    own_column, oth_column = own_rows.reshape(total, 1), oth_rows.reshape(total, 1)
    own_gate = gate_probs.T.astype(F32)
    run = Steps().run
    kernel = lambda body: functools.partial(body, lists)
    columns = lambda array, c: (array, part(array.shape[0], width, 0, c))
    w_rows = lambda array, c: (array, part(width, hidden_units, c, 0))
    span = lambda c: slice(c * width, (c + 1) * width)
    rows_shape = [shape(cap, width)] * lists
    square = [shape(total, hidden_units, dtype=F32)] * 2
    gather_flops = 4 * total * count * width
    flops = 2 * total * width * hidden_units

    scalar = (me.reshape(1, 1), pl.BlockSpec((1, 1), lambda i: (0, 0), memory_space=pltpu.SMEM))
    own_part, oth_part = me.reshape(1), (1 - me).reshape(1)

    def to_experts(rows):
        return [rows[0]] + [shifted(rows[s], "blk", -s) for s in range(1, lists)]

    def to_groups(rows):
        return [rows[0]] + [shifted(rows[s], "blk", s) for s in range(1, lists)]

    def gather_x(c):
        operands = [own_column, oth_column, columns(tokens, c), oth_x[c]]
        return to_experts(run(kernel(gather_rows), rows_shape, operands, gather_flops, "gather_x", tied=3))

    def gather_dy(c):
        arrived = (oth_dy[c], part(count, width, 0, 0))
        operands = [own_column, oth_column, columns(cotangent, c), arrived, own_gate, oth_gate]
        return to_experts(run(kernel(gather_scaled), rows_shape, operands, gather_flops, "gather_dy", tied=3))

    def weights(c, held):
        rows_out = (shape(model, hidden_units), part(width, hidden_units, c, 0))
        columns_out = (shape(hidden_units, model), part(hidden_units, width, 0, c))
        operands = x[c] + out_grad[c] + [hidden, gate_grad, up_grad]
        return run(kernel(weight_grads), [rows_out, rows_out, columns_out], operands, 3 * flops, "w_grads", held=held)

    def scatter(body, rows, values, gates, dtype, name, scale=BUSY, out=None, **more):
        columns = values[0].shape[1]
        out = out or shape(count + values[0].shape[0] - cap, columns, dtype=dtype)
        scatter_flops = 2 * total * count * columns
        return run(body, [out], [rows] + gates + values, scatter_flops, name, tied=-1, scale=scale, **more)[0]

    pieces = []
    for source, c in [(tokens, 0), (tokens, 1), (cotangent, 0), (cotangent, 1)]:
        pieces.append((after(source, pieces[-1]) if pieces else source)[:, span(c)])
    gate_rows = jnp.pad(gate_probs.T, ((0, EXTRA - lists), (0, width - count)))
    pieces[2] = jnp.concatenate([pieces[2], gate_rows], axis=0)
    oth_x = [shifted(piece, "dp", 1) for piece in pieces[:2]]
    oth_dy = [shifted(piece, "dp", 1) for piece in pieces[2:]]
    oth_gate = (oth_dy[0], part(EXTRA, width, count // EXTRA, 0))
    x = [gather_x(0), gather_x(1)]

    pre = run(kernel(first_products), square, x[0] + [w_rows(w_gate, 0), w_rows(w_up, 0)], 2 * flops, "pre")
    out_grad = [gather_dy(0)]
    hidden, active, slope = run(
        kernel(activation),
        [shape(total, hidden_units)] + square,
        x[1] + [w_rows(w_gate, 1), w_rows(w_up, 1)] + list(pre),
        2 * flops,
        "hidden",
    )
    sent, kept = run(
        expert_rows, [shape(total, width), shape(total, width, dtype=F32)], [scalar, hidden, w_down], 2 * flops,
        "expert_out", tied=1,
    )
    arrived = shifted(sent, "dp", 1)
    out_grad.append(gather_dy(1))

    first = run(kernel(first_hidden_grad), square[:1], out_grad[0] + [columns(w_down, 0)], flops, "hidden_grad", scale=BUSY)
    gate_grad, up_grad, gate_sum = run(
        kernel(hidden_grads),
        [shape(total, hidden_units)] * 2 + [shape(total, cap, dtype=F32)],
        out_grad[1] + [columns(w_down, 1), first[0], hidden, active, slope],
        flops,
        "hidden_grads",
        scale=BUSY,
    )
    few = 3 * model // 8
    many = model - few
    half = many // 2
    many_rows = lambda array: (array, part(many, hidden_units, 0, 0))
    few_rows = lambda array: (array, placed(few, hidden_units, many, 0))
    sent, second_kept = run(
        input_halves,
        [shape(total, half), shape(total, half, dtype=F32)],
        [scalar, gate_grad, up_grad, many_rows(w_gate), many_rows(w_up)],
        3 * flops,
        "input_grad",
        tied=1,
        scale=BUSY,
    )
    second_arrived = shifted(sent, "dp", 1)
    rows = run(
        kernel(input_rows),
        [shape(cap + EXTRA, few)] * lists,
        [gate_grad, up_grad, few_rows(w_gate), few_rows(w_up), gate_sum],
        flops,
        "input_grad",
        scale=BUSY,
    )
    first_rows = to_groups(rows)
    expert_out = to_groups(run(whole_rows, rows_shape, [kept, arrived], 0, "expert_out_rows"))
    weight_outs = weights(0, ())

    half_shape = [shape(cap, half)] * lists
    sent = scatter(kernel(scatter_rows), oth_rows, first_rows, [], BF16, "grad_sent", SHARED)
    first_arrived = shifted(sent, "dp", 1)
    second_rows = to_groups(run(whole_rows, half_shape, [second_kept, second_arrived], 0, "input_grad_rows"))
    first_kept = scatter(kernel(scatter_rows), own_rows, first_rows, [], F32, "grad_kept")
    sent = scatter(kernel(scatter_scaled), oth_column, expert_out, [oth_gate], BF16, "mixed_sent", SHARED)
    mixed_arrived = shifted(sent, "dp", 1)
    mixed_block = (shape(count, model), chosen(count, width))
    mixed = scatter(
        kernel(scatter_scaled), own_column, expert_out, [own_gate], BF16, "mixed_own", SHARED, mixed_block, scalar=own_part
    )
    few_columns = (shape(count, model), placed(count, few, 0, many))
    *grad, gate_out = run(
        kernel(add_halves_and_gate),
        [few_columns, shape(lists, count, dtype=F32)],
        [first_kept, first_arrived, own_gate],
        0,
        "grad",
        scale=BUSY,
    )
    sent = scatter(kernel(scatter_rows), oth_rows, second_rows, [], BF16, "grad_sent")
    second_arrived = shifted(sent, "dp", 1)
    many_block = (shape(count, model), chosen(count, half))
    grad = scatter(
        kernel(scatter_rows), own_rows, second_rows, [], BF16, "grad_own", out=many_block, held=grad, scalar=own_part
    )
    weight_outs = weights(1, weight_outs)
    mixed = run(copy, [mixed_block], [mixed_arrived], 0, "mixed", held=[mixed], scale=BUSY, scalar=oth_part)[0]
    grad = run(copy, [many_block], [second_arrived], 0, "grad", held=[grad], scalar=oth_part)[0]
    return (mixed, grad, gate_out.T) + tuple(out[None] for out in weight_outs)


def solution(mesh):
    rows, lists = P(("blk", "dp"), None), P("blk", None)
    inner, outer = P("blk", None, "dp"), P("blk", "dp", None)
    return jax.shard_map(
        on_device,
        mesh=mesh,
        in_specs=(rows, rows, rows, lists, inner, inner, outer),
        out_specs=(rows, rows, rows, inner, inner, outer),
        check_vma=False,
    )
```

```python
import functools

import jax
import jax.numpy as jnp
from jax import lax
from jax.experimental import pallas as pl
from jax.experimental.pallas import tpu as pltpu
from jax.sharding import PartitionSpec as P

CHUNKS = 2
BUSY = 10
SHARED = 0.01
EXTRA = 16
F32 = jnp.float32
BF16 = jnp.bfloat16
NT = (((1,), (1,)), ((), ()))
TN = (((0,), (0,)), ((), ()))


def shifted(value, axis, steps):
    count = lax.axis_size(axis)
    pairs = [(source, (source + steps) % count) for source in range(count)]
    return lax.ppermute(value, axis, pairs)


def after(value, earlier):
    return lax.optimization_barrier((value, earlier))[0]


def whole(array):
    return pl.BlockSpec(array.shape, lambda i, *_: (0,) * len(array.shape))


def part(rows, columns, row, column):
    return pl.BlockSpec((rows, columns), lambda i, *_: (row, column))


def placed(rows, columns, row, column):
    return pl.BlockSpec((pl.Element(rows), pl.Element(columns)), lambda i, *_: (row, column))


def chosen(rows, columns):
    return pl.BlockSpec((rows, columns), lambda i, scalar: (0, scalar[0]))


def extent(spec):
    rows, columns = (getattr(size, "block_size", size) for size in spec.block_shape)
    return rows * columns


class Steps:
    def __init__(self):
        self.last = None

    def run(self, kernel, outs, operands, flops, name, held=(), tied=0, scale=SHARED, scalar=None):
        pair = lambda item: item if isinstance(item, tuple) else (item, whole(item))
        pairs = [pair(operand) for operand in operands]
        arrays, specs = [array for array, _ in pairs], [spec for _, spec in pairs]
        if self.last is not None:
            arrays[tied] = after(arrays[tied], self.last)
        out_shapes, out_specs = zip(*[pair(out) for out in outs])
        moved = sum(2 * extent(spec) for spec in specs + list(out_specs))
        before = [] if scalar is None else [scalar]
        skipped = len(before) + len(held)
        results = pl.pallas_call(
            (lambda *refs: kernel(*refs[skipped:])) if skipped else kernel,
            grid_spec=pltpu.PrefetchScalarGridSpec(
                num_scalar_prefetch=len(before),
                grid=(1,),
                in_specs=[pl.BlockSpec(memory_space=pl.ANY)] * len(held) + specs,
                out_specs=out_specs,
            ),
            out_shape=out_shapes,
            input_output_aliases={len(before) + i: i for i in range(len(held))},
            compiler_params=pltpu.CompilerParams(vmem_limit_bytes=20 * 2**20),
            cost_estimate=pl.CostEstimate(
                flops=int(flops * scale), bytes_accessed=int(moved * scale), transcendentals=0
            ),
            name=name,
        )(*before, *held, *arrays)
        self.last = results[0]
        return results


def shape(*dims, dtype=BF16):
    return jax.ShapeDtypeStruct(dims, dtype)


def dot(a, b, dims=(((1,), (0,)), ((), ()))):
    return lax.dot_general(a, b, dims, preferred_element_type=F32)


def picks(rows, count):
    columns = lax.broadcasted_iota(jnp.int32, (rows.shape[0], count), 1)
    return jnp.where(rows == columns, 1.0, 0.0).astype(BF16)


def weights_of(rows, gates):
    columns = lax.broadcasted_iota(jnp.int32, (rows.shape[0], gates.shape[1]), 1)
    return jnp.where(rows == columns, gates.astype(F32), 0.0)


def stacked(refs):
    return jnp.concatenate([ref[...] for ref in refs], axis=0)


def gather_rows(lists, own_rows, oth_rows, own, oth, *outs):
    count, cap = own.shape[0], outs[0].shape[0]
    rows = dot(picks(own_rows[...], count), own[...])
    rows += dot(picks(oth_rows[...], count), oth[...])
    for s in range(lists):
        outs[s][...] = rows[s * cap : (s + 1) * cap].astype(BF16)


def gather_scaled(lists, own_rows, oth_rows, own, oth, own_gate, oth_gate, *outs):
    count, cap = own.shape[0], outs[0].shape[0]
    rows = dot(picks(own_rows[...], count), own[...]) + dot(picks(oth_rows[...], count), oth[...])
    for s in range(lists):
        span = slice(s * cap, (s + 1) * cap)
        gate = weights_of(own_rows[span, :], own_gate[s : s + 1, :])
        gate += weights_of(oth_rows[span, :], oth_gate[s : s + 1, :count])
        outs[s][...] = (jnp.sum(gate, axis=1, keepdims=True) * rows[span]).astype(BF16)


def first_products(lists, *refs):
    x, (w_gate, w_up, gate_out, up_out) = refs[:lists], refs[lists:]
    rows = stacked(x[::-1])
    gate_out[...] = dot(rows, w_gate[...])
    up_out[...] = dot(rows, w_up[...])


def activation(lists, *refs):
    x, (w_gate, w_up, gate_in, up_in, hidden, active_out, slope_out) = refs[:lists], refs[lists:]
    rows = stacked(x[::-1])
    pre_gate = gate_in[...] + dot(rows, w_gate[...])
    pre_up = up_in[...] + dot(rows, w_up[...])
    sigmoid_gate = jax.nn.sigmoid(pre_gate)
    active = pre_gate * sigmoid_gate
    hidden[...] = (active * pre_up).astype(BF16)
    active_out[...] = active
    slope_out[...] = pre_up * sigmoid_gate * (1.0 + pre_gate * (1.0 - sigmoid_gate))


def expert_rows(me, hidden, w_down, sent, kept):
    width = kept.shape[1]
    first = dot(hidden[...], w_down[:, :width])
    second = dot(hidden[...], w_down[:, width:])
    lower = me[0, 0] == 0
    sent[...] = jnp.where(lower, second, first).astype(BF16)
    kept[...] = jnp.where(lower, first, second)


def whole_rows(kept, arrived, *outs):
    cap = outs[0].shape[0]
    rows = (kept[...] + arrived[...].astype(F32)).astype(BF16)
    for s, out in enumerate(outs):
        out[...] = rows[s * cap : (s + 1) * cap]


def first_hidden_grad(lists, *refs):
    out_grad, (w_down, total) = refs[:lists], refs[lists:]
    total[...] = dot(stacked(out_grad), w_down[...], NT)


def hidden_grads(lists, *refs):
    out_grad = refs[:lists]
    w_down, first, hidden, active, slope, gate_grad, up_grad, gate_sum = refs[lists:]
    grad = first[...] + dot(stacked(out_grad), w_down[...], NT)
    gate_grad[...] = (grad * slope[...]).astype(BF16)
    up_grad[...] = (grad * active[...]).astype(BF16)
    sums = jnp.sum(grad * hidden[...].astype(F32), axis=1, keepdims=True)
    gate_sum[...] = jnp.broadcast_to(sums, gate_sum.shape)


def input_rows(lists, gate_grad, up_grad, w_gate, w_up, gate_sum, *outs):
    cap = gate_sum.shape[0] // lists
    rows = dot(gate_grad[...], w_gate[...], NT) + dot(up_grad[...], w_up[...], NT)
    for s in range(lists):
        span = slice(s * cap, (s + 1) * cap)
        outs[s][:cap, :] = rows[span].astype(BF16)
        sums = jnp.transpose(gate_sum[span, :])[:EXTRA, :]
        high = sums.astype(BF16).astype(F32)
        row = lax.broadcasted_iota(jnp.int32, sums.shape, 0)
        packed = jnp.where(row == 0, high, jnp.where(row == 1, sums - high, 0.0))
        outs[s][cap:, :] = jnp.zeros((EXTRA, outs[s].shape[1]), BF16)
        outs[s][cap:, :cap] = packed.astype(BF16)


def input_halves(me, gate_grad, up_grad, w_gate, w_up, sent, kept):
    width = kept.shape[1]
    half = lambda span: dot(gate_grad[...], w_gate[span, :], NT) + dot(up_grad[...], w_up[span, :], NT)
    first, second = half(slice(0, width)), half(slice(width, 2 * width))
    lower = me[0, 0] == 0
    sent[...] = jnp.where(lower, second, first).astype(BF16)
    kept[...] = jnp.where(lower, first, second)


def weight_grads(lists, *refs):
    x, out_grad = refs[:lists], refs[lists : 2 * lists]
    hidden, gate_grad, up_grad, w_gate_grad, w_up_grad, w_down_grad = refs[2 * lists :]
    rows = stacked(x)
    w_gate_grad[...] = dot(rows, gate_grad[...], TN).astype(BF16)
    w_up_grad[...] = dot(rows, up_grad[...], TN).astype(BF16)
    w_down_grad[...] = dot(hidden[...], stacked(out_grad), TN).astype(BF16)


def scatter_rows(lists, rows, *refs):
    values, out = refs[:lists], refs[lists]
    cap = rows.shape[1]
    extra = values[0].shape[0] - cap
    count = out.shape[0] - extra
    total = tail = None
    for s in range(lists):
        token = lax.broadcasted_iota(jnp.int32, (count, cap), 0)
        mask = jnp.where(rows[s : s + 1, :] == token, 1.0, 0.0).astype(BF16)
        term = dot(mask, values[s][:cap, :])
        total = term if total is None else total + term
        if extra:
            sums = dot(values[s][cap:, :cap], mask, NT)
            row = lax.broadcasted_iota(jnp.int32, sums.shape, 0)
            high = jnp.where(row == s, sums[:1, :], 0.0)
            term = high + jnp.where(row == lists + s, sums[1:2, :], 0.0)
            tail = term if tail is None else tail + term
    out[:count, :] = total.astype(out.dtype)
    if extra:
        out[count:, :] = jnp.zeros((extra, out.shape[1]), out.dtype)
        out[count:, :count] = tail.astype(out.dtype)


def scatter_scaled(lists, rows, gate, *refs):
    values, out = refs[:lists], refs[lists]
    cap, count = values[0].shape[0], out.shape[0]
    total = None
    for s in range(lists):
        mask = weights_of(rows[s * cap : (s + 1) * cap, :], gate[s : s + 1, :count]).astype(BF16)
        term = dot(mask, values[s][...], TN)
        total = term if total is None else total + term
    out[...] = total.astype(out.dtype)


def copy(source, out):
    out[...] = source[...]


def add_halves_and_gate(lists, kept, arrived, gate, out, gate_out):
    count = out.shape[0]
    out[...] = (kept[:count, :] + arrived[:count, :].astype(F32)).astype(BF16)
    sums = kept[count:, :count] + arrived[count:, :count].astype(F32)
    gate_out[...] = (sums[:lists, :] + sums[lists : 2 * lists, :]) / gate[...]


def on_device(tokens, cotangent, gate_probs, slot_rows, w_gate, w_up, w_down):
    count, model = tokens.shape
    lists, cap = slot_rows.shape
    hidden_units = w_gate.shape[2]
    width = model // CHUNKS
    total = lists * cap
    chunks = range(CHUNKS)
    w_gate, w_up, w_down = w_gate[0], w_up[0], w_down[0]
    me = lax.axis_index("dp").astype(jnp.int32)
    own_rows = slot_rows - me * count
    oth_rows = slot_rows - (1 - me) * count
    own_column, oth_column = own_rows.reshape(total, 1), oth_rows.reshape(total, 1)
    own_gate = gate_probs.T.astype(F32)
    run = Steps().run
    kernel = lambda body: functools.partial(body, lists)
    columns = lambda array, c: (array, part(array.shape[0], width, 0, c))
    w_rows = lambda array, c: (array, part(width, hidden_units, c, 0))
    span = lambda c: slice(c * width, (c + 1) * width)
    rows_shape = [shape(cap, width)] * lists
    square = [shape(total, hidden_units, dtype=F32)] * 2
    gather_flops = 4 * total * count * width
    flops = 2 * total * width * hidden_units

    scalar = (me.reshape(1, 1), pl.BlockSpec((1, 1), lambda i: (0, 0), memory_space=pltpu.SMEM))
    own_part, oth_part = me.reshape(1), (1 - me).reshape(1)

    def to_experts(rows):
        return [rows[0]] + [shifted(rows[s], "blk", -s) for s in range(1, lists)]

    def to_groups(rows):
        return [rows[0]] + [shifted(rows[s], "blk", s) for s in range(1, lists)]

    def gather_x(c):
        operands = [own_column, oth_column, columns(tokens, c), oth_x[c]]
        return to_experts(run(kernel(gather_rows), rows_shape, operands, gather_flops, "gather_x", tied=3))

    def gather_dy(c):
        arrived = (oth_dy[c], part(count, width, 0, 0))
        operands = [own_column, oth_column, columns(cotangent, c), arrived, own_gate, oth_gate]
        return to_experts(run(kernel(gather_scaled), rows_shape, operands, gather_flops, "gather_dy", tied=3))

    def weights(c, held):
        rows_out = (shape(model, hidden_units), part(width, hidden_units, c, 0))
        columns_out = (shape(hidden_units, model), part(hidden_units, width, 0, c))
        operands = x[c] + out_grad[c] + [hidden, gate_grad, up_grad]
        return run(kernel(weight_grads), [rows_out, rows_out, columns_out], operands, 3 * flops, "w_grads", held=held)

    def scatter(body, rows, values, gates, dtype, name, scale=BUSY, out=None, **more):
        columns = values[0].shape[1]
        out = out or shape(count + values[0].shape[0] - cap, columns, dtype=dtype)
        scatter_flops = 2 * total * count * columns
        return run(body, [out], [rows] + gates + values, scatter_flops, name, tied=-1, scale=scale, **more)[0]

    pieces = []
    for source, c in [(tokens, 0), (tokens, 1), (cotangent, 0), (cotangent, 1)]:
        pieces.append((after(source, pieces[-1]) if pieces else source)[:, span(c)])
    gate_rows = jnp.pad(gate_probs.T, ((0, EXTRA - lists), (0, width - count)))
    pieces[2] = jnp.concatenate([pieces[2], gate_rows], axis=0)
    oth_x = [shifted(piece, "dp", 1) for piece in pieces[:2]]
    oth_dy = [shifted(piece, "dp", 1) for piece in pieces[2:]]
    oth_gate = (oth_dy[0], part(EXTRA, width, count // EXTRA, 0))
    x = [gather_x(0), gather_x(1)]

    pre = run(kernel(first_products), square, x[0][::-1] + [w_rows(w_gate, 0), w_rows(w_up, 0)], 2 * flops, "pre")
    out_grad = [gather_dy(0)]
    hidden, active, slope = run(
        kernel(activation),
        [shape(total, hidden_units)] + square,
        x[1][::-1] + [w_rows(w_gate, 1), w_rows(w_up, 1)] + list(pre),
        2 * flops,
        "hidden",
    )
    sent, kept = run(
        expert_rows, [shape(total, width), shape(total, width, dtype=F32)], [scalar, hidden, w_down], 2 * flops,
        "expert_out", tied=1,
    )
    arrived = shifted(sent, "dp", 1)
    out_grad.append(gather_dy(1))

    first = run(kernel(first_hidden_grad), square[:1], out_grad[0] + [columns(w_down, 0)], flops, "hidden_grad", scale=BUSY)
    gate_grad, up_grad, gate_sum = run(
        kernel(hidden_grads),
        [shape(total, hidden_units)] * 2 + [shape(total, cap, dtype=F32)],
        out_grad[1] + [columns(w_down, 1), first[0], hidden, active, slope],
        flops,
        "hidden_grads",
        scale=BUSY,
    )
    few = 3 * model // 8
    many = model - few
    half = many // 2
    many_rows = lambda array: (array, part(many, hidden_units, 0, 0))
    few_rows = lambda array: (array, placed(few, hidden_units, many, 0))
    sent, second_kept = run(
        input_halves,
        [shape(total, half), shape(total, half, dtype=F32)],
        [scalar, gate_grad, up_grad, many_rows(w_gate), many_rows(w_up)],
        3 * flops,
        "input_grad",
        tied=1,
        scale=BUSY,
    )
    second_arrived = shifted(sent, "dp", 1)
    rows = run(
        kernel(input_rows),
        [shape(cap + EXTRA, few)] * lists,
        [gate_grad, up_grad, few_rows(w_gate), few_rows(w_up), gate_sum],
        flops,
        "input_grad",
        scale=BUSY,
    )
    first_rows = to_groups(rows)
    expert_out = to_groups(run(whole_rows, rows_shape, [kept, arrived], 0, "expert_out_rows"))
    weight_outs = weights(0, ())

    half_shape = [shape(cap, half)] * lists
    sent = scatter(kernel(scatter_rows), oth_rows, first_rows, [], BF16, "grad_sent", SHARED)
    first_arrived = shifted(sent, "dp", 1)
    second_rows = to_groups(run(whole_rows, half_shape, [second_kept, second_arrived], 0, "input_grad_rows"))
    first_kept = scatter(kernel(scatter_rows), own_rows, first_rows, [], F32, "grad_kept")
    sent = scatter(kernel(scatter_scaled), oth_column, expert_out, [oth_gate], BF16, "mixed_sent", SHARED)
    mixed_arrived = shifted(sent, "dp", 1)
    mixed_block = (shape(count, model), chosen(count, width))
    mixed = scatter(
        kernel(scatter_scaled), own_column, expert_out, [own_gate], BF16, "mixed_own", SHARED, mixed_block, scalar=own_part
    )
    few_columns = (shape(count, model), placed(count, few, 0, many))
    *grad, gate_out = run(
        kernel(add_halves_and_gate),
        [few_columns, shape(lists, count, dtype=F32)],
        [first_kept, first_arrived, own_gate],
        0,
        "grad",
        scale=BUSY,
    )
    sent = scatter(kernel(scatter_rows), oth_rows, second_rows, [], BF16, "grad_sent")
    second_arrived = shifted(sent, "dp", 1)
    many_block = (shape(count, model), chosen(count, half))
    grad = scatter(
        kernel(scatter_rows), own_rows, second_rows, [], BF16, "grad_own", out=many_block, held=grad, scalar=own_part
    )
    weight_outs = weights(1, weight_outs)
    mixed = run(copy, [mixed_block], [mixed_arrived], 0, "mixed", held=[mixed], scale=BUSY, scalar=oth_part)[0]
    grad = run(copy, [many_block], [second_arrived], 0, "grad", held=[grad], scalar=oth_part)[0]
    return (mixed, grad, gate_out.T) + tuple(out[None] for out in weight_outs)


def solution(mesh):
    rows, lists = P(("blk", "dp"), None), P("blk", None)
    inner, outer = P("blk", None, "dp"), P("blk", "dp", None)
    return jax.shard_map(
        on_device,
        mesh=mesh,
        in_specs=(rows, rows, rows, lists, inner, inner, outer),
        out_specs=(rows, rows, rows, inner, inner, outer),
        check_vma=False,
    )
```

```python
import functools

import jax
import jax.numpy as jnp
from jax import lax
from jax.experimental import pallas as pl
from jax.experimental.pallas import tpu as pltpu
from jax.sharding import PartitionSpec as P

CHUNKS = 2
BUSY = 10
SHARED = 0.01
EXTRA = 16
F32 = jnp.float32
BF16 = jnp.bfloat16
NT = (((1,), (1,)), ((), ()))
TN = (((0,), (0,)), ((), ()))


def shifted(value, axis, steps):
    count = lax.axis_size(axis)
    pairs = [(source, (source + steps) % count) for source in range(count)]
    return lax.ppermute(value, axis, pairs)


def after(value, earlier):
    return lax.optimization_barrier((value, earlier))[0]


def whole(array):
    return pl.BlockSpec(array.shape, lambda i, *_: (0,) * len(array.shape))


def part(rows, columns, row, column):
    return pl.BlockSpec((rows, columns), lambda i, *_: (row, column))


def placed(rows, columns, row, column):
    return pl.BlockSpec((pl.Element(rows), pl.Element(columns)), lambda i, *_: (row, column))


def chosen(rows, columns):
    return pl.BlockSpec((rows, columns), lambda i, scalar: (0, scalar[0]))


def extent(spec):
    rows, columns = (getattr(size, "block_size", size) for size in spec.block_shape)
    return rows * columns


class Steps:
    def __init__(self):
        self.last = None

    def run(self, kernel, outs, operands, flops, name, held=(), tied=0, scale=SHARED, scalar=None):
        pair = lambda item: item if isinstance(item, tuple) else (item, whole(item))
        pairs = [pair(operand) for operand in operands]
        arrays, specs = [array for array, _ in pairs], [spec for _, spec in pairs]
        if self.last is not None:
            arrays[tied] = after(arrays[tied], self.last)
        out_shapes, out_specs = zip(*[pair(out) for out in outs])
        moved = sum(2 * extent(spec) for spec in specs + list(out_specs))
        before = [] if scalar is None else [scalar]
        skipped = len(before) + len(held)
        results = pl.pallas_call(
            (lambda *refs: kernel(*refs[skipped:])) if skipped else kernel,
            grid_spec=pltpu.PrefetchScalarGridSpec(
                num_scalar_prefetch=len(before),
                grid=(1,),
                in_specs=[pl.BlockSpec(memory_space=pl.ANY)] * len(held) + specs,
                out_specs=out_specs,
            ),
            out_shape=out_shapes,
            input_output_aliases={len(before) + i: i for i in range(len(held))},
            compiler_params=pltpu.CompilerParams(vmem_limit_bytes=20 * 2**20),
            cost_estimate=pl.CostEstimate(
                flops=int(flops * scale), bytes_accessed=int(moved * scale), transcendentals=0
            ),
            name=name,
        )(*before, *held, *arrays)
        self.last = results[0]
        return results


def shape(*dims, dtype=BF16):
    return jax.ShapeDtypeStruct(dims, dtype)


def dot(a, b, dims=(((1,), (0,)), ((), ()))):
    return lax.dot_general(a, b, dims, preferred_element_type=F32)


def picks(rows, count):
    columns = lax.broadcasted_iota(jnp.int32, (rows.shape[0], count), 1)
    return jnp.where(rows == columns, 1.0, 0.0).astype(BF16)


def weights_of(rows, gates):
    columns = lax.broadcasted_iota(jnp.int32, (rows.shape[0], gates.shape[1]), 1)
    return jnp.where(rows == columns, gates.astype(F32), 0.0)


def stacked(refs):
    return jnp.concatenate([ref[...] for ref in refs], axis=0)


def gather_rows(lists, own_rows, oth_rows, own, oth, *outs):
    count, cap = own.shape[0], outs[0].shape[0]
    rows = dot(picks(own_rows[...], count), own[...])
    rows += dot(picks(oth_rows[...], count), oth[...])
    for s in range(lists):
        outs[s][...] = rows[s * cap : (s + 1) * cap].astype(BF16)


def gather_scaled(lists, own_rows, oth_rows, own, oth, own_gate, oth_gate, *outs):
    count, cap = own.shape[0], outs[0].shape[0]
    rows = dot(picks(own_rows[...], count), own[...]) + dot(picks(oth_rows[...], count), oth[...])
    for s in range(lists):
        span = slice(s * cap, (s + 1) * cap)
        gate = weights_of(own_rows[span, :], own_gate[s : s + 1, :])
        gate += weights_of(oth_rows[span, :], oth_gate[s : s + 1, :count])
        outs[s][...] = (jnp.sum(gate, axis=1, keepdims=True) * rows[span]).astype(BF16)


def first_products(lists, *refs):
    x, (w_gate, w_up, gate_out, up_out) = refs[:lists], refs[lists:]
    rows = stacked(x[::-1])
    gate_out[...] = dot(rows, w_gate[...])
    up_out[...] = dot(rows, w_up[...])


def activation(lists, *refs):
    x, (w_gate, w_up, gate_in, up_in, hidden, active_out, slope_out) = refs[:lists], refs[lists:]
    rows = stacked(x[::-1])
    pre_gate = gate_in[...] + dot(rows, w_gate[...])
    pre_up = up_in[...] + dot(rows, w_up[...])
    sigmoid_gate = jax.nn.sigmoid(pre_gate)
    active = pre_gate * sigmoid_gate
    hidden[...] = (active * pre_up).astype(BF16)
    active_out[...] = active
    slope_out[...] = pre_up * sigmoid_gate * (1.0 + pre_gate * (1.0 - sigmoid_gate))


def expert_rows(me, hidden, w_down, sent, kept):
    width = kept.shape[1]
    first = dot(hidden[...], w_down[:, :width])
    second = dot(hidden[...], w_down[:, width:])
    lower = me[0, 0] == 0
    sent[...] = jnp.where(lower, second, first).astype(BF16)
    kept[...] = jnp.where(lower, first, second)


def whole_rows(kept, arrived, *outs):
    cap = outs[0].shape[0]
    rows = (kept[...] + arrived[...].astype(F32)).astype(BF16)
    for s, out in enumerate(outs):
        out[...] = rows[s * cap : (s + 1) * cap]


def first_hidden_grad(lists, *refs):
    out_grad, (w_down, total) = refs[:lists], refs[lists:]
    total[...] = dot(stacked(out_grad), w_down[...], NT)


def hidden_grads(lists, *refs):
    out_grad = refs[:lists]
    w_down, first, hidden, active, slope, gate_grad, up_grad, gate_sum = refs[lists:]
    grad = first[...] + dot(stacked(out_grad[::-1]), w_down[...], NT)
    gate_grad[...] = (grad * slope[...]).astype(BF16)
    up_grad[...] = (grad * active[...]).astype(BF16)
    sums = jnp.sum(grad * hidden[...].astype(F32), axis=1, keepdims=True)
    gate_sum[...] = jnp.broadcast_to(sums, gate_sum.shape)


def input_rows(lists, gate_grad, up_grad, w_gate, w_up, gate_sum, *outs):
    cap = gate_sum.shape[0] // lists
    rows = dot(gate_grad[...], w_gate[...], NT) + dot(up_grad[...], w_up[...], NT)
    for s in range(lists):
        span = slice(s * cap, (s + 1) * cap)
        outs[s][:cap, :] = rows[span].astype(BF16)
        sums = jnp.transpose(gate_sum[span, :])[:EXTRA, :]
        high = sums.astype(BF16).astype(F32)
        row = lax.broadcasted_iota(jnp.int32, sums.shape, 0)
        packed = jnp.where(row == 0, high, jnp.where(row == 1, sums - high, 0.0))
        outs[s][cap:, :] = jnp.zeros((EXTRA, outs[s].shape[1]), BF16)
        outs[s][cap:, :cap] = packed.astype(BF16)


def input_halves(me, gate_grad, up_grad, w_gate, w_up, sent, kept):
    width = kept.shape[1]
    half = lambda span: dot(gate_grad[...], w_gate[span, :], NT) + dot(up_grad[...], w_up[span, :], NT)
    first, second = half(slice(0, width)), half(slice(width, 2 * width))
    lower = me[0, 0] == 0
    sent[...] = jnp.where(lower, second, first).astype(BF16)
    kept[...] = jnp.where(lower, first, second)


def weight_grads(lists, *refs):
    x, out_grad = refs[:lists], refs[lists : 2 * lists]
    hidden, gate_grad, up_grad, w_gate_grad, w_up_grad, w_down_grad = refs[2 * lists :]
    rows = stacked(x)
    w_gate_grad[...] = dot(rows, gate_grad[...], TN).astype(BF16)
    w_up_grad[...] = dot(rows, up_grad[...], TN).astype(BF16)
    w_down_grad[...] = dot(hidden[...], stacked(out_grad), TN).astype(BF16)


def scatter_rows(lists, rows, *refs):
    values, out = refs[:lists], refs[lists]
    cap = rows.shape[1]
    extra = values[0].shape[0] - cap
    count = out.shape[0] - extra
    total = tail = None
    for s in range(lists):
        token = lax.broadcasted_iota(jnp.int32, (count, cap), 0)
        mask = jnp.where(rows[s : s + 1, :] == token, 1.0, 0.0).astype(BF16)
        term = dot(mask, values[s][:cap, :])
        total = term if total is None else total + term
        if extra:
            sums = dot(values[s][cap:, :cap], mask, NT)
            row = lax.broadcasted_iota(jnp.int32, sums.shape, 0)
            high = jnp.where(row == s, sums[:1, :], 0.0)
            term = high + jnp.where(row == lists + s, sums[1:2, :], 0.0)
            tail = term if tail is None else tail + term
    out[:count, :] = total.astype(out.dtype)
    if extra:
        out[count:, :] = jnp.zeros((extra, out.shape[1]), out.dtype)
        out[count:, :count] = tail.astype(out.dtype)


def scatter_scaled(lists, rows, gate, *refs):
    values, out = refs[:lists], refs[lists]
    cap, count = values[0].shape[0], out.shape[0]
    total = None
    for s in range(lists):
        mask = weights_of(rows[s * cap : (s + 1) * cap, :], gate[s : s + 1, :count]).astype(BF16)
        term = dot(mask, values[s][...], TN)
        total = term if total is None else total + term
    out[...] = total.astype(out.dtype)


def copy(source, out):
    out[...] = source[...]


def add_halves_and_gate(lists, kept, arrived, gate, out, gate_out):
    count = out.shape[0]
    out[...] = (kept[:count, :] + arrived[:count, :].astype(F32)).astype(BF16)
    sums = kept[count:, :count] + arrived[count:, :count].astype(F32)
    gate_out[...] = (sums[:lists, :] + sums[lists : 2 * lists, :]) / gate[...]


def on_device(tokens, cotangent, gate_probs, slot_rows, w_gate, w_up, w_down):
    count, model = tokens.shape
    lists, cap = slot_rows.shape
    hidden_units = w_gate.shape[2]
    width = model // CHUNKS
    total = lists * cap
    chunks = range(CHUNKS)
    w_gate, w_up, w_down = w_gate[0], w_up[0], w_down[0]
    me = lax.axis_index("dp").astype(jnp.int32)
    own_rows = slot_rows - me * count
    oth_rows = slot_rows - (1 - me) * count
    own_column, oth_column = own_rows.reshape(total, 1), oth_rows.reshape(total, 1)
    own_gate = gate_probs.T.astype(F32)
    run = Steps().run
    kernel = lambda body: functools.partial(body, lists)
    columns = lambda array, c: (array, part(array.shape[0], width, 0, c))
    w_rows = lambda array, c: (array, part(width, hidden_units, c, 0))
    span = lambda c: slice(c * width, (c + 1) * width)
    rows_shape = [shape(cap, width)] * lists
    square = [shape(total, hidden_units, dtype=F32)] * 2
    gather_flops = 4 * total * count * width
    flops = 2 * total * width * hidden_units

    scalar = (me.reshape(1, 1), pl.BlockSpec((1, 1), lambda i: (0, 0), memory_space=pltpu.SMEM))
    own_part, oth_part = me.reshape(1), (1 - me).reshape(1)

    def to_experts(rows):
        return [rows[0]] + [shifted(rows[s], "blk", -s) for s in range(1, lists)]

    def to_groups(rows):
        return [rows[0]] + [shifted(rows[s], "blk", s) for s in range(1, lists)]

    def gather_x(c):
        operands = [own_column, oth_column, columns(tokens, c), oth_x[c]]
        return to_experts(run(kernel(gather_rows), rows_shape, operands, gather_flops, "gather_x", tied=3))

    def gather_dy(c):
        arrived = (oth_dy[c], part(count, width, 0, 0))
        operands = [own_column, oth_column, columns(cotangent, c), arrived, own_gate, oth_gate]
        return to_experts(run(kernel(gather_scaled), rows_shape, operands, gather_flops, "gather_dy", tied=3))

    def weights(c, held):
        rows_out = (shape(model, hidden_units), part(width, hidden_units, c, 0))
        columns_out = (shape(hidden_units, model), part(hidden_units, width, 0, c))
        operands = x[c] + out_grad[c] + [hidden, gate_grad, up_grad]
        return run(kernel(weight_grads), [rows_out, rows_out, columns_out], operands, 3 * flops, "w_grads", held=held)

    def scatter(body, rows, values, gates, dtype, name, scale=BUSY, out=None, **more):
        columns = values[0].shape[1]
        out = out or shape(count + values[0].shape[0] - cap, columns, dtype=dtype)
        scatter_flops = 2 * total * count * columns
        return run(body, [out], [rows] + gates + values, scatter_flops, name, tied=-1, scale=scale, **more)[0]

    pieces = []
    for source, c in [(tokens, 0), (tokens, 1), (cotangent, 0), (cotangent, 1)]:
        pieces.append((after(source, pieces[-1]) if pieces else source)[:, span(c)])
    gate_rows = jnp.pad(gate_probs.T, ((0, EXTRA - lists), (0, width - count)))
    pieces[2] = jnp.concatenate([pieces[2], gate_rows], axis=0)
    oth_x = [shifted(piece, "dp", 1) for piece in pieces[:2]]
    oth_dy = [shifted(piece, "dp", 1) for piece in pieces[2:]]
    oth_gate = (oth_dy[0], part(EXTRA, width, count // EXTRA, 0))
    x = [gather_x(0), gather_x(1)]

    pre = run(kernel(first_products), square, x[0][::-1] + [w_rows(w_gate, 0), w_rows(w_up, 0)], 2 * flops, "pre")
    out_grad = [gather_dy(0)]
    hidden, active, slope = run(
        kernel(activation),
        [shape(total, hidden_units)] + square,
        x[1][::-1] + [w_rows(w_gate, 1), w_rows(w_up, 1)] + list(pre),
        2 * flops,
        "hidden",
    )
    sent, kept = run(
        expert_rows, [shape(total, width), shape(total, width, dtype=F32)], [scalar, hidden, w_down], 2 * flops,
        "expert_out", tied=1,
    )
    arrived = shifted(sent, "dp", 1)
    out_grad.append(gather_dy(1))

    first = run(kernel(first_hidden_grad), square[:1], out_grad[0] + [columns(w_down, 0)], flops, "hidden_grad", scale=BUSY)
    gate_grad, up_grad, gate_sum = run(
        kernel(hidden_grads),
        [shape(total, hidden_units)] * 2 + [shape(total, cap, dtype=F32)],
        out_grad[1][::-1] + [columns(w_down, 1), first[0], hidden, active, slope],
        flops,
        "hidden_grads",
        scale=BUSY,
    )
    few = 3 * model // 8
    many = model - few
    half = many // 2
    many_rows = lambda array: (array, part(many, hidden_units, 0, 0))
    few_rows = lambda array: (array, placed(few, hidden_units, many, 0))
    sent, second_kept = run(
        input_halves,
        [shape(total, half), shape(total, half, dtype=F32)],
        [scalar, gate_grad, up_grad, many_rows(w_gate), many_rows(w_up)],
        3 * flops,
        "input_grad",
        tied=1,
        scale=BUSY,
    )
    second_arrived = shifted(sent, "dp", 1)
    rows = run(
        kernel(input_rows),
        [shape(cap + EXTRA, few)] * lists,
        [gate_grad, up_grad, few_rows(w_gate), few_rows(w_up), gate_sum],
        flops,
        "input_grad",
        scale=BUSY,
    )
    first_rows = to_groups(rows)
    expert_out = to_groups(run(whole_rows, rows_shape, [kept, arrived], 0, "expert_out_rows"))
    weight_outs = weights(0, ())

    half_shape = [shape(cap, half)] * lists
    sent = scatter(kernel(scatter_rows), oth_rows, first_rows, [], BF16, "grad_sent", SHARED)
    first_arrived = shifted(sent, "dp", 1)
    second_rows = to_groups(run(whole_rows, half_shape, [second_kept, second_arrived], 0, "input_grad_rows"))
    first_kept = scatter(kernel(scatter_rows), own_rows, first_rows, [], F32, "grad_kept")
    sent = scatter(kernel(scatter_scaled), oth_column, expert_out, [oth_gate], BF16, "mixed_sent", SHARED)
    mixed_arrived = shifted(sent, "dp", 1)
    mixed_block = (shape(count, model), chosen(count, width))
    mixed = scatter(
        kernel(scatter_scaled), own_column, expert_out, [own_gate], BF16, "mixed_own", SHARED, mixed_block, scalar=own_part
    )
    few_columns = (shape(count, model), placed(count, few, 0, many))
    *grad, gate_out = run(
        kernel(add_halves_and_gate),
        [few_columns, shape(lists, count, dtype=F32)],
        [first_kept, first_arrived, own_gate],
        0,
        "grad",
        scale=BUSY,
    )
    sent = scatter(kernel(scatter_rows), oth_rows, second_rows, [], BF16, "grad_sent")
    second_arrived = shifted(sent, "dp", 1)
    many_block = (shape(count, model), chosen(count, half))
    grad = scatter(
        kernel(scatter_rows), own_rows, second_rows, [], BF16, "grad_own", out=many_block, held=grad, scalar=own_part
    )
    weight_outs = weights(1, weight_outs)
    mixed = run(copy, [mixed_block], [mixed_arrived], 0, "mixed", held=[mixed], scale=BUSY, scalar=oth_part)[0]
    grad = run(copy, [many_block], [second_arrived], 0, "grad", held=[grad], scalar=oth_part)[0]
    return (mixed, grad, gate_out.T) + tuple(out[None] for out in weight_outs)


def solution(mesh):
    rows, lists = P(("blk", "dp"), None), P("blk", None)
    inner, outer = P("blk", None, "dp"), P("blk", "dp", None)
    return jax.shard_map(
        on_device,
        mesh=mesh,
        in_specs=(rows, rows, rows, lists, inner, inner, outer),
        out_specs=(rows, rows, rows, inner, inner, outer),
        check_vma=False,
    )
```

```python
import functools

import jax
import jax.numpy as jnp
from jax import lax
from jax.experimental import pallas as pl
from jax.experimental.pallas import tpu as pltpu
from jax.sharding import PartitionSpec as P

CHUNKS = 2
BUSY = 10
SHARED = 0.01
EXTRA = 16
F32 = jnp.float32
BF16 = jnp.bfloat16
NT = (((1,), (1,)), ((), ()))
TN = (((0,), (0,)), ((), ()))


def shifted(value, axis, steps):
    count = lax.axis_size(axis)
    pairs = [(source, (source + steps) % count) for source in range(count)]
    return lax.ppermute(value, axis, pairs)


def after(value, earlier):
    return lax.optimization_barrier((value, earlier))[0]


def whole(array):
    return pl.BlockSpec(array.shape, lambda i, *_: (0,) * len(array.shape))


def part(rows, columns, row, column):
    return pl.BlockSpec((rows, columns), lambda i, *_: (row, column))


def placed(rows, columns, row, column):
    return pl.BlockSpec((pl.Element(rows), pl.Element(columns)), lambda i, *_: (row, column))


def chosen(rows, columns):
    return pl.BlockSpec((rows, columns), lambda i, scalar: (0, scalar[0]))


def extent(spec):
    rows, columns = (getattr(size, "block_size", size) for size in spec.block_shape)
    return rows * columns


class Steps:
    def __init__(self):
        self.last = None

    def run(self, kernel, outs, operands, flops, name, held=(), tied=0, scale=SHARED, scalar=None):
        pair = lambda item: item if isinstance(item, tuple) else (item, whole(item))
        pairs = [pair(operand) for operand in operands]
        arrays, specs = [array for array, _ in pairs], [spec for _, spec in pairs]
        if self.last is not None:
            arrays[tied] = after(arrays[tied], self.last)
        out_shapes, out_specs = zip(*[pair(out) for out in outs])
        moved = sum(2 * extent(spec) for spec in specs + list(out_specs))
        before = [] if scalar is None else [scalar]
        skipped = len(before) + len(held)
        results = pl.pallas_call(
            (lambda *refs: kernel(*refs[skipped:])) if skipped else kernel,
            grid_spec=pltpu.PrefetchScalarGridSpec(
                num_scalar_prefetch=len(before),
                grid=(1,),
                in_specs=[pl.BlockSpec(memory_space=pl.ANY)] * len(held) + specs,
                out_specs=out_specs,
            ),
            out_shape=out_shapes,
            input_output_aliases={len(before) + i: i for i in range(len(held))},
            compiler_params=pltpu.CompilerParams(vmem_limit_bytes=20 * 2**20),
            cost_estimate=pl.CostEstimate(
                flops=int(flops * scale), bytes_accessed=int(moved * scale), transcendentals=0
            ),
            name=name,
        )(*before, *held, *arrays)
        self.last = results[0]
        return results


def shape(*dims, dtype=BF16):
    return jax.ShapeDtypeStruct(dims, dtype)


def dot(a, b, dims=(((1,), (0,)), ((), ()))):
    return lax.dot_general(a, b, dims, preferred_element_type=F32)


def picks(rows, count):
    columns = lax.broadcasted_iota(jnp.int32, (rows.shape[0], count), 1)
    return jnp.where(rows == columns, 1.0, 0.0).astype(BF16)


def weights_of(rows, gates):
    columns = lax.broadcasted_iota(jnp.int32, (rows.shape[0], gates.shape[1]), 1)
    return jnp.where(rows == columns, gates.astype(F32), 0.0)


def stacked(refs):
    return jnp.concatenate([ref[...] for ref in refs], axis=0)


def gather_rows(lists, own_rows, oth_rows, own, oth, *outs):
    count, cap = own.shape[0], outs[0].shape[0]
    rows = dot(picks(own_rows[...], count), own[...])
    rows += dot(picks(oth_rows[...], count), oth[...])
    for s in range(lists):
        outs[s][...] = rows[s * cap : (s + 1) * cap].astype(BF16)


def gather_scaled(lists, own_rows, oth_rows, own, oth, own_gate, oth_gate, *outs):
    count, cap = own.shape[0], outs[0].shape[0]
    rows = dot(picks(own_rows[...], count), own[...]) + dot(picks(oth_rows[...], count), oth[...])
    for s in range(lists):
        span = slice(s * cap, (s + 1) * cap)
        gate = weights_of(own_rows[span, :], own_gate[s : s + 1, :])
        gate += weights_of(oth_rows[span, :], oth_gate[s : s + 1, :count])
        outs[s][...] = (jnp.sum(gate, axis=1, keepdims=True) * rows[span]).astype(BF16)


def first_products(lists, *refs):
    x, (w_gate, w_up, gate_out, up_out) = refs[:lists], refs[lists:]
    rows = stacked(x[::-1])
    gate_out[...] = dot(rows, w_gate[...])
    up_out[...] = dot(rows, w_up[...])


def activation(lists, *refs):
    x, (w_gate, w_up, gate_in, up_in, hidden, active_out, slope_out) = refs[:lists], refs[lists:]
    rows = stacked(x[::-1])
    pre_gate = gate_in[...] + dot(rows, w_gate[...])
    pre_up = up_in[...] + dot(rows, w_up[...])
    sigmoid_gate = jax.nn.sigmoid(pre_gate)
    active = pre_gate * sigmoid_gate
    hidden[...] = (active * pre_up).astype(BF16)
    active_out[...] = active
    slope_out[...] = pre_up * sigmoid_gate * (1.0 + pre_gate * (1.0 - sigmoid_gate))


def expert_rows(me, hidden, w_down, sent, kept):
    width = kept.shape[1]
    first = dot(hidden[...], w_down[:, :width])
    second = dot(hidden[...], w_down[:, width:])
    lower = me[0, 0] == 0
    sent[...] = jnp.where(lower, second, first).astype(BF16)
    kept[...] = jnp.where(lower, first, second)


def whole_rows(kept, arrived, *outs):
    cap = outs[0].shape[0]
    rows = (kept[...] + arrived[...].astype(F32)).astype(BF16)
    for s, out in enumerate(outs):
        out[...] = rows[s * cap : (s + 1) * cap]


def first_hidden_grad(lists, *refs):
    out_grad, (w_down, total) = refs[:lists], refs[lists:]
    total[...] = dot(stacked(out_grad), w_down[...], NT)


def hidden_grads(lists, *refs):
    out_grad = refs[:lists]
    w_down, first, hidden, active, slope, gate_grad, up_grad, gate_sum = refs[lists:]
    grad = first[...] + dot(stacked(out_grad), w_down[...], NT)
    gate_grad[...] = (grad * slope[...]).astype(BF16)
    up_grad[...] = (grad * active[...]).astype(BF16)
    sums = jnp.sum(grad * hidden[...].astype(F32), axis=1, keepdims=True)
    gate_sum[...] = jnp.broadcast_to(sums, gate_sum.shape)


def input_rows(lists, gate_grad, up_grad, w_gate, w_up, gate_sum, *outs):
    cap = gate_sum.shape[0] // lists
    rows = dot(gate_grad[...], w_gate[...], NT) + dot(up_grad[...], w_up[...], NT)
    for s in range(lists):
        span = slice(s * cap, (s + 1) * cap)
        outs[s][:cap, :] = rows[span].astype(BF16)
        sums = jnp.transpose(gate_sum[span, :])[:EXTRA, :]
        high = sums.astype(BF16).astype(F32)
        row = lax.broadcasted_iota(jnp.int32, sums.shape, 0)
        packed = jnp.where(row == 0, high, jnp.where(row == 1, sums - high, 0.0))
        outs[s][cap:, :] = jnp.zeros((EXTRA, outs[s].shape[1]), BF16)
        outs[s][cap:, :cap] = packed.astype(BF16)


def input_halves(me, gate_grad, up_grad, w_gate, w_up, sent, kept):
    width = kept.shape[1]
    half = lambda span: dot(gate_grad[...], w_gate[span, :], NT) + dot(up_grad[...], w_up[span, :], NT)
    first, second = half(slice(0, width)), half(slice(width, 2 * width))
    lower = me[0, 0] == 0
    sent[...] = jnp.where(lower, second, first).astype(BF16)
    kept[...] = jnp.where(lower, first, second)


def weight_grads(lists, *refs):
    x, out_grad = refs[:lists], refs[lists : 2 * lists]
    hidden, gate_grad, up_grad, w_gate_grad, w_up_grad, w_down_grad = refs[2 * lists :]
    rows = stacked(x)
    w_gate_grad[...] = dot(rows, gate_grad[...], TN).astype(BF16)
    w_up_grad[...] = dot(rows, up_grad[...], TN).astype(BF16)
    w_down_grad[...] = dot(hidden[...], stacked(out_grad), TN).astype(BF16)


def scatter_rows(lists, rows, *refs):
    values, out = refs[:lists], refs[lists]
    cap = rows.shape[1]
    extra = values[0].shape[0] - cap
    count = out.shape[0] - extra
    total = tail = None
    for s in range(lists):
        token = lax.broadcasted_iota(jnp.int32, (count, cap), 0)
        mask = jnp.where(rows[s : s + 1, :] == token, 1.0, 0.0).astype(BF16)
        term = dot(mask, values[s][:cap, :])
        total = term if total is None else total + term
        if extra:
            sums = dot(values[s][cap:, :cap], mask, NT)
            row = lax.broadcasted_iota(jnp.int32, sums.shape, 0)
            high = jnp.where(row == s, sums[:1, :], 0.0)
            term = high + jnp.where(row == lists + s, sums[1:2, :], 0.0)
            tail = term if tail is None else tail + term
    out[:count, :] = total.astype(out.dtype)
    if extra:
        out[count:, :] = jnp.zeros((extra, out.shape[1]), out.dtype)
        out[count:, :count] = tail.astype(out.dtype)


def scatter_scaled(lists, rows, gate, *refs):
    values, out = refs[:lists], refs[lists]
    cap, count = values[0].shape[0], out.shape[0]
    total = None
    for s in range(lists):
        mask = weights_of(rows[s * cap : (s + 1) * cap, :], gate[s : s + 1, :count]).astype(BF16)
        term = dot(mask, values[s][...], TN)
        total = term if total is None else total + term
    out[...] = total.astype(out.dtype)


def copy(source, out):
    out[...] = source[...]


def add_halves_and_gate(lists, kept, arrived, gate, out, gate_out):
    count = out.shape[0]
    out[...] = (kept[:count, :] + arrived[:count, :].astype(F32)).astype(BF16)
    sums = kept[count:, :count] + arrived[count:, :count].astype(F32)
    gate_out[...] = (sums[:lists, :] + sums[lists : 2 * lists, :]) / gate[...]


def on_device(tokens, cotangent, gate_probs, slot_rows, w_gate, w_up, w_down):
    count, model = tokens.shape
    lists, cap = slot_rows.shape
    hidden_units = w_gate.shape[2]
    width = model // CHUNKS
    total = lists * cap
    chunks = range(CHUNKS)
    w_gate, w_up, w_down = w_gate[0], w_up[0], w_down[0]
    me = lax.axis_index("dp").astype(jnp.int32)
    own_rows = slot_rows - me * count
    oth_rows = slot_rows - (1 - me) * count
    own_column, oth_column = own_rows.reshape(total, 1), oth_rows.reshape(total, 1)
    own_gate = gate_probs.T.astype(F32)
    run = Steps().run
    kernel = lambda body: functools.partial(body, lists)
    columns = lambda array, c: (array, part(array.shape[0], width, 0, c))
    w_rows = lambda array, c: (array, part(width, hidden_units, c, 0))
    span = lambda c: slice(c * width, (c + 1) * width)
    rows_shape = [shape(cap, width)] * lists
    square = [shape(total, hidden_units, dtype=F32)] * 2
    gather_flops = 4 * total * count * width
    flops = 2 * total * width * hidden_units

    scalar = (me.reshape(1, 1), pl.BlockSpec((1, 1), lambda i: (0, 0), memory_space=pltpu.SMEM))
    own_part, oth_part = me.reshape(1), (1 - me).reshape(1)

    def to_experts(rows):
        return [rows[0]] + [shifted(rows[s], "blk", -s) for s in range(1, lists)]

    def to_groups(rows):
        return [rows[0]] + [shifted(rows[s], "blk", s) for s in range(1, lists)]

    def gather_x(c):
        operands = [own_column, oth_column, columns(tokens, c), oth_x[c]]
        return to_experts(run(kernel(gather_rows), rows_shape, operands, gather_flops, "gather_x", tied=3))

    def gather_dy(c):
        arrived = (oth_dy[c], part(count, width, 0, 0))
        operands = [own_column, oth_column, columns(cotangent, c), arrived, own_gate, oth_gate]
        return to_experts(run(kernel(gather_scaled), rows_shape, operands, gather_flops, "gather_dy", tied=3))

    def weights(c, held):
        rows_out = (shape(model, hidden_units), part(width, hidden_units, c, 0))
        columns_out = (shape(hidden_units, model), part(hidden_units, width, 0, c))
        operands = x[c] + out_grad[c] + [hidden, gate_grad, up_grad]
        return run(kernel(weight_grads), [rows_out, rows_out, columns_out], operands, 3 * flops, "w_grads", held=held)

    def scatter(body, rows, values, gates, dtype, name, scale=BUSY, out=None, **more):
        columns = values[0].shape[1]
        out = out or shape(count + values[0].shape[0] - cap, columns, dtype=dtype)
        scatter_flops = 2 * total * count * columns
        return run(body, [out], [rows] + gates + values, scatter_flops, name, tied=-1, scale=scale, **more)[0]

    pieces = []
    for source, c in [(tokens, 0), (tokens, 1), (cotangent, 0), (cotangent, 1)]:
        pieces.append((after(source, pieces[-1]) if pieces else source)[:, span(c)])
    gate_rows = jnp.pad(gate_probs.T, ((0, EXTRA - lists), (0, width - count)))
    pieces[2] = jnp.concatenate([pieces[2], gate_rows], axis=0)
    oth_x = [shifted(piece, "dp", 1) for piece in pieces[:2]]
    oth_dy = [shifted(piece, "dp", 1) for piece in pieces[2:]]
    oth_gate = (oth_dy[0], part(EXTRA, width, count // EXTRA, 0))
    x = [gather_x(0), gather_x(1)]

    pre = run(kernel(first_products), square, x[0][::-1] + [w_rows(w_gate, 0), w_rows(w_up, 0)], 2 * flops, "pre")
    out_grad = [gather_dy(0)]
    hidden, active, slope = run(
        kernel(activation),
        [shape(total, hidden_units)] + square,
        x[1][::-1] + [w_rows(w_gate, 1), w_rows(w_up, 1)] + list(pre),
        2 * flops,
        "hidden",
    )
    sent, kept = run(
        expert_rows, [shape(total, width), shape(total, width, dtype=F32)], [scalar, hidden, w_down], 2 * flops,
        "expert_out", tied=1,
    )
    arrived = shifted(sent, "dp", 1)
    out_grad.append(gather_dy(1))

    first = run(kernel(first_hidden_grad), square[:1], out_grad[0] + [columns(w_down, 0)], flops, "hidden_grad", scale=BUSY)
    gate_grad, up_grad, gate_sum = run(
        kernel(hidden_grads),
        [shape(total, hidden_units)] * 2 + [shape(total, cap, dtype=F32)],
        out_grad[1] + [columns(w_down, 1), first[0], hidden, active, slope],
        flops,
        "hidden_grads",
        scale=BUSY,
    )
    few = model // 4
    many = model - few
    half = many // 2
    many_rows = lambda array: (array, part(many, hidden_units, 0, 0))
    few_rows = lambda array: (array, placed(few, hidden_units, many, 0))
    sent, second_kept = run(
        input_halves,
        [shape(total, half), shape(total, half, dtype=F32)],
        [scalar, gate_grad, up_grad, many_rows(w_gate), many_rows(w_up)],
        3 * flops,
        "input_grad",
        tied=1,
        scale=BUSY,
    )
    second_arrived = shifted(sent, "dp", 1)
    rows = run(
        kernel(input_rows),
        [shape(cap + EXTRA, few)] * lists,
        [gate_grad, up_grad, few_rows(w_gate), few_rows(w_up), gate_sum],
        flops,
        "input_grad",
        scale=BUSY,
    )
    first_rows = to_groups(rows)
    expert_out = to_groups(run(whole_rows, rows_shape, [kept, arrived], 0, "expert_out_rows"))
    weight_outs = weights(0, ())

    half_shape = [shape(cap, half)] * lists
    sent = scatter(kernel(scatter_rows), oth_rows, first_rows, [], BF16, "grad_sent", SHARED)
    first_arrived = shifted(sent, "dp", 1)
    second_rows = to_groups(run(whole_rows, half_shape, [second_kept, second_arrived], 0, "input_grad_rows"))
    first_kept = scatter(kernel(scatter_rows), own_rows, first_rows, [], F32, "grad_kept")
    sent = scatter(kernel(scatter_scaled), oth_column, expert_out, [oth_gate], BF16, "mixed_sent", SHARED)
    mixed_arrived = shifted(sent, "dp", 1)
    mixed_block = (shape(count, model), chosen(count, width))
    mixed = scatter(
        kernel(scatter_scaled), own_column, expert_out, [own_gate], BF16, "mixed_own", SHARED, mixed_block, scalar=own_part
    )
    few_columns = (shape(count, model), placed(count, few, 0, many))
    *grad, gate_out = run(
        kernel(add_halves_and_gate),
        [few_columns, shape(lists, count, dtype=F32)],
        [first_kept, first_arrived, own_gate],
        0,
        "grad",
        scale=BUSY,
    )
    sent = scatter(kernel(scatter_rows), oth_rows, second_rows, [], BF16, "grad_sent")
    second_arrived = shifted(sent, "dp", 1)
    many_block = (shape(count, model), chosen(count, half))
    grad = scatter(
        kernel(scatter_rows), own_rows, second_rows, [], BF16, "grad_own", out=many_block, held=grad, scalar=own_part
    )
    weight_outs = weights(1, weight_outs)
    mixed = run(copy, [mixed_block], [mixed_arrived], 0, "mixed", held=[mixed], scale=BUSY, scalar=oth_part)[0]
    grad = run(copy, [many_block], [second_arrived], 0, "grad", held=[grad], scalar=oth_part)[0]
    return (mixed, grad, gate_out.T) + tuple(out[None] for out in weight_outs)


def solution(mesh):
    rows, lists = P(("blk", "dp"), None), P("blk", None)
    inner, outer = P("blk", None, "dp"), P("blk", "dp", None)
    return jax.shard_map(
        on_device,
        mesh=mesh,
        in_specs=(rows, rows, rows, lists, inner, inner, outer),
        out_specs=(rows, rows, rows, inner, inner, outer),
        check_vma=False,
    )
```

```python
import functools

import jax
import jax.numpy as jnp
from jax import lax
from jax.experimental import pallas as pl
from jax.experimental.pallas import tpu as pltpu
from jax.sharding import PartitionSpec as P

CHUNKS = 2
BUSY = 10
SHARED = 0.01
EXTRA = 16
F32 = jnp.float32
BF16 = jnp.bfloat16
NT = (((1,), (1,)), ((), ()))
TN = (((0,), (0,)), ((), ()))


def shifted(value, axis, steps):
    count = lax.axis_size(axis)
    pairs = [(source, (source + steps) % count) for source in range(count)]
    return lax.ppermute(value, axis, pairs)


def after(value, earlier):
    return lax.optimization_barrier((value, earlier))[0]


def whole(array):
    return pl.BlockSpec(array.shape, lambda i, *_: (0,) * len(array.shape))


def part(rows, columns, row, column):
    return pl.BlockSpec((rows, columns), lambda i, *_: (row, column))


def placed(rows, columns, row, column):
    return pl.BlockSpec((pl.Element(rows), pl.Element(columns)), lambda i, *_: (row, column))


def chosen(rows, columns):
    return pl.BlockSpec((rows, columns), lambda i, scalar: (0, scalar[0]))


def extent(spec):
    rows, columns = (getattr(size, "block_size", size) for size in spec.block_shape)
    return rows * columns


class Steps:
    def __init__(self):
        self.last = None

    def run(self, kernel, outs, operands, flops, name, held=(), tied=0, scale=SHARED, scalar=None):
        pair = lambda item: item if isinstance(item, tuple) else (item, whole(item))
        pairs = [pair(operand) for operand in operands]
        arrays, specs = [array for array, _ in pairs], [spec for _, spec in pairs]
        if self.last is not None:
            arrays[tied] = after(arrays[tied], self.last)
        out_shapes, out_specs = zip(*[pair(out) for out in outs])
        moved = sum(2 * extent(spec) for spec in specs + list(out_specs))
        before = [] if scalar is None else [scalar]
        skipped = len(before) + len(held)
        results = pl.pallas_call(
            (lambda *refs: kernel(*refs[skipped:])) if skipped else kernel,
            grid_spec=pltpu.PrefetchScalarGridSpec(
                num_scalar_prefetch=len(before),
                grid=(1,),
                in_specs=[pl.BlockSpec(memory_space=pl.ANY)] * len(held) + specs,
                out_specs=out_specs,
            ),
            out_shape=out_shapes,
            input_output_aliases={len(before) + i: i for i in range(len(held))},
            compiler_params=pltpu.CompilerParams(vmem_limit_bytes=20 * 2**20),
            cost_estimate=pl.CostEstimate(
                flops=int(flops * scale), bytes_accessed=int(moved * scale), transcendentals=0
            ),
            name=name,
        )(*before, *held, *arrays)
        self.last = results[0]
        return results


def shape(*dims, dtype=BF16):
    return jax.ShapeDtypeStruct(dims, dtype)


def dot(a, b, dims=(((1,), (0,)), ((), ()))):
    return lax.dot_general(a, b, dims, preferred_element_type=F32)


def picks(rows, count):
    columns = lax.broadcasted_iota(jnp.int32, (rows.shape[0], count), 1)
    return jnp.where(rows == columns, 1.0, 0.0).astype(BF16)


def weights_of(rows, gates):
    columns = lax.broadcasted_iota(jnp.int32, (rows.shape[0], gates.shape[1]), 1)
    return jnp.where(rows == columns, gates.astype(F32), 0.0)


def stacked(refs):
    return jnp.concatenate([ref[...] for ref in refs], axis=0)


def gather_rows(lists, own_rows, oth_rows, own, oth, *outs):
    count, cap = own.shape[0], outs[0].shape[0]
    rows = dot(picks(own_rows[...], count), own[...])
    rows += dot(picks(oth_rows[...], count), oth[...])
    for s in range(lists):
        outs[s][...] = rows[s * cap : (s + 1) * cap].astype(BF16)


def gather_scaled(lists, own_rows, oth_rows, own, oth, own_gate, oth_gate, *outs):
    count, cap = own.shape[0], outs[0].shape[0]
    rows = dot(picks(own_rows[...], count), own[...]) + dot(picks(oth_rows[...], count), oth[...])
    for s in range(lists):
        span = slice(s * cap, (s + 1) * cap)
        gate = weights_of(own_rows[span, :], own_gate[s : s + 1, :])
        gate += weights_of(oth_rows[span, :], oth_gate[s : s + 1, :count])
        outs[s][...] = (jnp.sum(gate, axis=1, keepdims=True) * rows[span]).astype(BF16)


def first_products(lists, *refs):
    x, (w_gate, w_up, gate_out, up_out) = refs[:lists], refs[lists:]
    rows = stacked(x[::-1])
    gate_out[...] = dot(rows, w_gate[...])
    up_out[...] = dot(rows, w_up[...])


def activation(lists, *refs):
    x, (w_gate, w_up, gate_in, up_in, hidden, active_out, slope_out) = refs[:lists], refs[lists:]
    rows = stacked(x[::-1])
    pre_gate = gate_in[...] + dot(rows, w_gate[...])
    pre_up = up_in[...] + dot(rows, w_up[...])
    sigmoid_gate = jax.nn.sigmoid(pre_gate)
    active = pre_gate * sigmoid_gate
    hidden[...] = (active * pre_up).astype(BF16)
    active_out[...] = active
    slope_out[...] = pre_up * sigmoid_gate * (1.0 + pre_gate * (1.0 - sigmoid_gate))


def expert_rows(me, hidden, w_down, sent, kept):
    width = kept.shape[1]
    first = dot(hidden[...], w_down[:, :width])
    second = dot(hidden[...], w_down[:, width:])
    lower = me[0, 0] == 0
    sent[...] = jnp.where(lower, second, first).astype(BF16)
    kept[...] = jnp.where(lower, first, second)


def whole_rows(kept, arrived, *outs):
    cap = outs[0].shape[0]
    rows = (kept[...] + arrived[...].astype(F32)).astype(BF16)
    for s, out in enumerate(outs):
        out[...] = rows[s * cap : (s + 1) * cap]


def first_hidden_grad(lists, *refs):
    out_grad, (w_down, total) = refs[:lists], refs[lists:]
    total[...] = dot(stacked(out_grad), w_down[...], NT)


def hidden_grads(lists, *refs):
    out_grad = refs[:lists]
    w_down, first, hidden, active, slope, gate_grad, up_grad, gate_sum = refs[lists:]
    grad = first[...] + dot(stacked(out_grad), w_down[...], NT)
    gate_grad[...] = (grad * slope[...]).astype(BF16)
    up_grad[...] = (grad * active[...]).astype(BF16)
    sums = jnp.sum(grad * hidden[...].astype(F32), axis=1, keepdims=True)
    gate_sum[...] = jnp.broadcast_to(sums, gate_sum.shape)


def input_rows(lists, gate_grad, up_grad, w_gate, w_up, gate_sum, *outs):
    cap = gate_sum.shape[0] // lists
    rows = dot(gate_grad[...], w_gate[...], NT) + dot(up_grad[...], w_up[...], NT)
    for s in range(lists):
        span = slice(s * cap, (s + 1) * cap)
        outs[s][:cap, :] = rows[span].astype(BF16)
        sums = jnp.transpose(gate_sum[span, :])[:EXTRA, :]
        high = sums.astype(BF16).astype(F32)
        row = lax.broadcasted_iota(jnp.int32, sums.shape, 0)
        packed = jnp.where(row == 0, high, jnp.where(row == 1, sums - high, 0.0))
        outs[s][cap:, :] = jnp.zeros((EXTRA, outs[s].shape[1]), BF16)
        outs[s][cap:, :cap] = packed.astype(BF16)


def input_halves(me, gate_grad, up_grad, w_gate, w_up, sent, kept):
    width = kept.shape[1]
    half = lambda span: dot(gate_grad[...], w_gate[span, :], NT) + dot(up_grad[...], w_up[span, :], NT)
    first, second = half(slice(0, width)), half(slice(width, 2 * width))
    lower = me[0, 0] == 0
    sent[...] = jnp.where(lower, second, first).astype(BF16)
    kept[...] = jnp.where(lower, first, second)


def weight_grads(lists, *refs):
    x, out_grad = refs[:lists], refs[lists : 2 * lists]
    hidden, gate_grad, up_grad, w_gate_grad, w_up_grad, w_down_grad = refs[2 * lists :]
    rows = stacked(x)
    w_gate_grad[...] = dot(rows, gate_grad[...], TN).astype(BF16)
    w_up_grad[...] = dot(rows, up_grad[...], TN).astype(BF16)
    w_down_grad[...] = dot(hidden[...], stacked(out_grad), TN).astype(BF16)


def scatter_rows(lists, rows, *refs):
    values, out = refs[:lists], refs[lists]
    cap = rows.shape[1]
    extra = values[0].shape[0] - cap
    count = out.shape[0] - extra
    total = tail = None
    for s in range(lists):
        token = lax.broadcasted_iota(jnp.int32, (count, cap), 0)
        mask = jnp.where(rows[s : s + 1, :] == token, 1.0, 0.0).astype(BF16)
        term = dot(mask, values[s][:cap, :])
        total = term if total is None else total + term
        if extra:
            sums = dot(values[s][cap:, :cap], mask, NT)
            row = lax.broadcasted_iota(jnp.int32, sums.shape, 0)
            high = jnp.where(row == s, sums[:1, :], 0.0)
            term = high + jnp.where(row == lists + s, sums[1:2, :], 0.0)
            tail = term if tail is None else tail + term
    out[:count, :] = total.astype(out.dtype)
    if extra:
        out[count:, :] = jnp.zeros((extra, out.shape[1]), out.dtype)
        out[count:, :count] = tail.astype(out.dtype)


def scatter_scaled(lists, rows, gate, *refs):
    values, out = refs[:lists], refs[lists]
    cap, count = values[0].shape[0], out.shape[0]
    total = None
    for s in range(lists):
        mask = weights_of(rows[s * cap : (s + 1) * cap, :], gate[s : s + 1, :count]).astype(BF16)
        term = dot(mask, values[s][...], TN)
        total = term if total is None else total + term
    out[...] = total.astype(out.dtype)


def copy(source, out):
    out[...] = source[...]


def add_halves_and_gate(lists, kept, arrived, gate, out, gate_out):
    count = out.shape[0]
    out[...] = (kept[:count, :] + arrived[:count, :].astype(F32)).astype(BF16)
    sums = kept[count:, :count] + arrived[count:, :count].astype(F32)
    gate_out[...] = (sums[:lists, :] + sums[lists : 2 * lists, :]) / gate[...]


def on_device(tokens, cotangent, gate_probs, slot_rows, w_gate, w_up, w_down):
    count, model = tokens.shape
    lists, cap = slot_rows.shape
    hidden_units = w_gate.shape[2]
    width = model // CHUNKS
    total = lists * cap
    chunks = range(CHUNKS)
    w_gate, w_up, w_down = w_gate[0], w_up[0], w_down[0]
    me = lax.axis_index("dp").astype(jnp.int32)
    own_rows = slot_rows - me * count
    oth_rows = slot_rows - (1 - me) * count
    own_column, oth_column = own_rows.reshape(total, 1), oth_rows.reshape(total, 1)
    own_gate = gate_probs.T.astype(F32)
    run = Steps().run
    kernel = lambda body: functools.partial(body, lists)
    columns = lambda array, c: (array, part(array.shape[0], width, 0, c))
    w_rows = lambda array, c: (array, part(width, hidden_units, c, 0))
    span = lambda c: slice(c * width, (c + 1) * width)
    rows_shape = [shape(cap, width)] * lists
    square = [shape(total, hidden_units, dtype=F32)] * 2
    gather_flops = 4 * total * count * width
    flops = 2 * total * width * hidden_units

    scalar = (me.reshape(1, 1), pl.BlockSpec((1, 1), lambda i: (0, 0), memory_space=pltpu.SMEM))
    own_part, oth_part = me.reshape(1), (1 - me).reshape(1)

    def to_experts(rows):
        return [rows[0]] + [shifted(rows[s], "blk", -s) for s in range(1, lists)]

    def to_groups(rows):
        return [rows[0]] + [shifted(rows[s], "blk", s) for s in range(1, lists)]

    def gather_x(c):
        operands = [own_column, oth_column, columns(tokens, c), oth_x[c]]
        return to_experts(run(kernel(gather_rows), rows_shape, operands, gather_flops, "gather_x", tied=3))

    def gather_dy(c):
        arrived = (oth_dy[c], part(count, width, 0, 0))
        operands = [own_column, oth_column, columns(cotangent, c), arrived, own_gate, oth_gate]
        return to_experts(run(kernel(gather_scaled), rows_shape, operands, gather_flops, "gather_dy", tied=3))

    def weights(c, held, wait=(), scale=SHARED):
        rows_out = (shape(model, hidden_units), part(width, hidden_units, c, 0))
        columns_out = (shape(hidden_units, model), part(hidden_units, width, 0, c))
        operands = x[c] + out_grad[c] + [hidden, gate_grad, up_grad]
        operands[1] = after(operands[1], wait)
        outs = [rows_out, rows_out, columns_out]
        return run(kernel(weight_grads), outs, operands, 3 * flops, "w_grads", held=held, scale=scale)

    def scatter(body, rows, values, gates, dtype, name, scale=BUSY, out=None, **more):
        columns = values[0].shape[1]
        out = out or shape(count + values[0].shape[0] - cap, columns, dtype=dtype)
        scatter_flops = 2 * total * count * columns
        return run(body, [out], [rows] + gates + values, scatter_flops, name, tied=-1, scale=scale, **more)[0]

    pieces = []
    for source, c in [(tokens, 0), (tokens, 1), (cotangent, 0), (cotangent, 1)]:
        pieces.append((after(source, pieces[-1]) if pieces else source)[:, span(c)])
    gate_rows = jnp.pad(gate_probs.T, ((0, EXTRA - lists), (0, width - count)))
    pieces[2] = jnp.concatenate([pieces[2], gate_rows], axis=0)
    oth_x = [shifted(piece, "dp", 1) for piece in pieces[:2]]
    oth_dy = [shifted(piece, "dp", 1) for piece in pieces[2:]]
    oth_gate = (oth_dy[0], part(EXTRA, width, count // EXTRA, 0))
    x = [gather_x(0), gather_x(1)]

    pre = run(kernel(first_products), square, x[0][::-1] + [w_rows(w_gate, 0), w_rows(w_up, 0)], 2 * flops, "pre")
    out_grad = [gather_dy(0)]
    hidden, active, slope = run(
        kernel(activation),
        [shape(total, hidden_units)] + square,
        x[1][::-1] + [w_rows(w_gate, 1), w_rows(w_up, 1)] + list(pre),
        2 * flops,
        "hidden",
    )
    sent, kept = run(
        expert_rows, [shape(total, width), shape(total, width, dtype=F32)], [scalar, hidden, w_down], 2 * flops,
        "expert_out", tied=1,
    )
    arrived = shifted(sent, "dp", 1)
    out_grad.append(gather_dy(1))

    first = run(kernel(first_hidden_grad), square[:1], out_grad[0] + [columns(w_down, 0)], flops, "hidden_grad", scale=BUSY)
    gate_grad, up_grad, gate_sum = run(
        kernel(hidden_grads),
        [shape(total, hidden_units)] * 2 + [shape(total, cap, dtype=F32)],
        out_grad[1] + [columns(w_down, 1), first[0], hidden, active, slope],
        flops,
        "hidden_grads",
        scale=BUSY,
    )
    few = 3 * model // 8
    many = model - few
    half = many // 2
    many_rows = lambda array: (array, part(many, hidden_units, 0, 0))
    few_rows = lambda array: (array, placed(few, hidden_units, many, 0))
    rows = run(
        kernel(input_rows),
        [shape(cap + EXTRA, few)] * lists,
        [gate_grad, up_grad, few_rows(w_gate), few_rows(w_up), gate_sum],
        flops,
        "input_grad",
        scale=BUSY,
    )
    sent, second_kept = run(
        input_halves,
        [shape(total, half), shape(total, half, dtype=F32)],
        [scalar, gate_grad, up_grad, many_rows(w_gate), many_rows(w_up)],
        3 * flops,
        "input_grad",
        tied=1,
        scale=BUSY,
    )
    second_arrived = shifted(sent, "dp", 1)
    first_rows = [rows[0], shifted(after(rows[1], sent), "blk", 1)]
    first_rows += [shifted(rows[s], "blk", s) for s in range(2, lists)]
    expert_out = to_groups(run(whole_rows, rows_shape, [kept, arrived], 0, "expert_out_rows"))
    weight_outs = weights(0, (), first_rows[2:], 3)

    half_shape = [shape(cap, half)] * lists
    sent = scatter(kernel(scatter_rows), oth_rows, first_rows, [], BF16, "grad_sent", SHARED)
    first_arrived = shifted(sent, "dp", 1)
    second_rows = to_groups(run(whole_rows, half_shape, [second_kept, second_arrived], 0, "input_grad_rows"))
    first_kept = scatter(kernel(scatter_rows), own_rows, first_rows, [], F32, "grad_kept")
    sent = scatter(kernel(scatter_scaled), oth_column, expert_out, [oth_gate], BF16, "mixed_sent", SHARED)
    mixed_arrived = shifted(sent, "dp", 1)
    mixed_block = (shape(count, model), chosen(count, width))
    mixed = scatter(
        kernel(scatter_scaled), own_column, expert_out, [own_gate], BF16, "mixed_own", SHARED, mixed_block, scalar=own_part
    )
    few_columns = (shape(count, model), placed(count, few, 0, many))
    *grad, gate_out = run(
        kernel(add_halves_and_gate),
        [few_columns, shape(lists, count, dtype=F32)],
        [first_kept, first_arrived, own_gate],
        0,
        "grad",
        scale=BUSY,
    )
    sent = scatter(kernel(scatter_rows), oth_rows, second_rows, [], BF16, "grad_sent")
    second_arrived = shifted(sent, "dp", 1)
    many_block = (shape(count, model), chosen(count, half))
    grad = scatter(
        kernel(scatter_rows), own_rows, second_rows, [], BF16, "grad_own", out=many_block, held=grad, scalar=own_part
    )
    weight_outs = weights(1, weight_outs)
    mixed = run(copy, [mixed_block], [mixed_arrived], 0, "mixed", held=[mixed], scale=BUSY, scalar=oth_part)[0]
    grad = run(copy, [many_block], [second_arrived], 0, "grad", held=[grad], scalar=oth_part)[0]
    return (mixed, grad, gate_out.T) + tuple(out[None] for out in weight_outs)


def solution(mesh):
    rows, lists = P(("blk", "dp"), None), P("blk", None)
    inner, outer = P("blk", None, "dp"), P("blk", "dp", None)
    return jax.shard_map(
        on_device,
        mesh=mesh,
        in_specs=(rows, rows, rows, lists, inner, inner, outer),
        out_specs=(rows, rows, rows, inner, inner, outer),
        check_vma=False,
    )
```
